128 devices in a mesh: section: 2 (over core), dp: 16 (over y, x), tensor: 4 (over z).
Axes of the slice: x: 4, y: 4, z: 4, core: 2. Of those that a mesh axis runs over, the one named last changes fastest.
Arguments:
- section_ends: bfloat16 [2, 2, 8192, 1536], P('section', None, ('dp', 'tensor')), may hold values from -6 to 6
- norm_gain: bfloat16 [2, 1536], P('section', ('dp', 'tensor')), may hold values from 0.5 to 1.5
- proj_inner: bfloat16 [2, 1536, 2, 3072], P('section', 'dp', None, 'tensor'), may hold values from -0.15625 to 0.15625
- proj_step: bfloat16 [2, 1536, 48], P('section', 'dp', 'tensor'), may hold values from -0.15625 to 0.15625
- proj_state: bfloat16 [2, 1536, 256], P('section', ('dp', 'tensor')), may hold values from -0.15625 to 0.15625
- conv_inner: bfloat16 [2, 5, 3072], P('section', None, ('dp', 'tensor')), may hold values from -0.5 to 0.5
- conv_state: bfloat16 [2, 5, 256], P('section', None, ('dp', 'tensor')), may hold values from -0.5 to 0.5
- gate_gain: bfloat16 [2, 3072], P('section', ('dp', 'tensor')), may hold values from 0.5 to 1.5
- head_params: bfloat16 [2, 3, 48], P('section', None, 'tensor'), may hold values from -5 to 1.5, as said below
- proj_output: bfloat16 [2, 3072, 1536], P('section', 'tensor', 'dp'), may hold values from -0.109375 to 0.109375
Outputs:
- section_results: float32 [2, 2, 8192, 1536], P('section', None, ('dp', 'tensor'))
- grad_norm_gain: float32 [2, 1536], P('section', ('dp', 'tensor'))
- grad_proj_inner: float32 [2, 1536, 2, 3072], P('section', 'dp', None, 'tensor')
- grad_proj_step: float32 [2, 1536, 48], P('section', 'dp', 'tensor')
- grad_proj_state: float32 [2, 1536, 256], P('section', ('dp', 'tensor'))
- grad_conv_inner: float32 [2, 5, 3072], P('section', None, ('dp', 'tensor'))
- grad_conv_state: float32 [2, 5, 256], P('section', None, ('dp', 'tensor'))
- grad_gate_gain: float32 [2, 3072], P('section', ('dp', 'tensor'))
- grad_head_params: float32 [2, 3, 48], P('section', None, 'tensor')
- grad_proj_output: float32 [2, 3072, 1536], P('section', 'tensor', 'dp')
The draws below stay inside these ranges and needn't reach their ends.
Inputs may be any that keep to these rules, and one draw needn't show every extreme that they name: `head_params`: row 0 lies in -5 to -1, row 1 in -1 to 1.5, row 2 in 0.5 to 1.5.
All inputs are finite; a program needn't handle non-finite values.
Results may differ from the reference program's by a relative error of at most 0.018.
Values may be sent and summed in bfloat16 or wider, within the bound.
No kernel may reach another device: no remote copies, remote signals or barrier semaphores. Data moves between devices by JAX's collectives and lax.ppermute only.
A program may use at most 192 MiB of HBM per device.

```python
import jax
import jax.numpy as jnp
from jax import lax

D = 1536
H = 48
N = 128
KERNEL = 4
GROUP = 256
MICRO = 2
DI = 3072
SEQ_LEN = 512
TOK_MB = 8192


def draw_head_params(key, part):
    key = jax.random.fold_in(key, 7)
    unit_draw = jax.random.uniform(key, (2, 3, H), jnp.float32)
    low_end = jnp.array([-5.0, -1.0, 0.5], jnp.float32)[None, :, None]
    span_width = jnp.array([4.0, 2.5, 1.0], jnp.float32)[None, :, None]
    return (low_end + span_width * unit_draw).astype(jnp.bfloat16)


def block_levels(stream_key, dims, cuts, low, high):
    loudness, own = 1.0, jax.random.fold_in(stream_key, 6)
    for position, shards_of in cuts:
        draws = jnp.exp(jax.random.uniform(jax.random.fold_in(own, position), (shards_of,), jnp.float32, low / len(cuts), high / len(cuts)))
        loudness = loudness * jnp.repeat(draws, dims[position] // shards_of).reshape([-1 if axis == position else 1 for axis in range(len(dims))])
    return loudness


def scatter_about(rng, shape, spread, most, cuts=(), held_as=jnp.bfloat16):
    values = spread * jax.random.normal(rng, shape, jnp.float32)
    if cuts:
        values = values * block_levels(rng, shape, cuts, -0.22, 0.18)
    return jnp.clip(values, -most, most).astype(held_as)


def setup_inputs(seed: int = 0) -> dict:
    streams_of = jax.random.split(jax.random.key(seed), 11)
    return {
        "section_ends": scatter_about(streams_of[0], (2, MICRO, TOK_MB, D), 1.0, 6.0, ((0, 2), (2, 64))),
        "norm_gain": jnp.clip(1.0 + 0.1 * jax.random.normal(streams_of[1], (2, D), jnp.float32), 0.5, 1.5).astype(jnp.bfloat16),
        "proj_inner": scatter_about(streams_of[2], (2, D, 2, DI), D ** -0.5, 0.15625, ((0, 2), (1, 16), (3, 4))),
        "proj_step": scatter_about(streams_of[3], (2, D, H), D ** -0.5, 0.15625, ((0, 2), (1, 16), (2, 4))),
        "proj_state": scatter_about(streams_of[4], (2, D, 2 * N), D ** -0.5, 0.15625, ((0, 2), (1, 64))),
        "conv_inner": jnp.clip(jax.random.uniform(streams_of[5], (2, KERNEL + 1, DI), jnp.float32, -0.5, 0.5) * block_levels(streams_of[5], (2, KERNEL + 1, DI), ((0, 2), (2, 64)), -0.4, 0.0), -0.5, 0.5).astype(jnp.bfloat16),
        "conv_state": jnp.clip(jax.random.uniform(streams_of[6], (2, KERNEL + 1, 2 * N), jnp.float32, -0.5, 0.5) * block_levels(streams_of[6], (2, KERNEL + 1, 2 * N), ((0, 2), (2, 64)), -0.4, 0.0), -0.5, 0.5).astype(jnp.bfloat16),
        "gate_gain": jnp.clip(1.0 + 0.1 * jax.random.normal(streams_of[7], (2, DI), jnp.float32), 0.5, 1.5).astype(jnp.bfloat16),
        "head_params": draw_head_params(jax.random.fold_in(streams_of[10], 71), 0),
        "proj_output": scatter_about(streams_of[9], (2, DI, D), DI ** -0.5, 0.109375, ((0, 2), (1, 4), (2, 16))),
    }


EPS = 1e-05
HIGH = lax.Precision.HIGHEST

@jax.custom_vjp
def low(v):
    return lax.optimization_barrier(v.astype(jnp.bfloat16)).astype(jnp.float32)

@jax.custom_vjp
def low_back(v):
    return v

def low_keep(v):
    return (low(v), None)

def low_pass(kept, grad):
    return (grad,)

def back_keep(v):
    return (v, None)

def back_low(kept, grad):
    return (low(grad),)
low.defvjp(low_keep, low_pass)
low_back.defvjp(back_keep, back_low)

def matmul_high(left, right):
    return jnp.dot(left, right, precision=HIGH, preferred_element_type=jnp.float32)

def norm_rows(values, gain):
    return values * lax.rsqrt(lax.optimization_barrier(jnp.mean(values * values, axis=-1, keepdims=True)) + EPS) * gain

def causal_conv(values, taps):
    width = taps.shape[0] - 1
    length = values.shape[0]
    padded = jnp.pad(values, ((width - 1, 0), (0, 0)))
    total = jnp.zeros_like(values) + taps[width]
    for k in range(width):
        total = total + taps[k] * padded[k:k + length]
    return total

def mixer_core(gate_in, inner_in, state_in, step_in, taps_inner, taps_state, step_bias, decay_log, skip_gain):
    length, channels = inner_in.shape
    head_count = step_in.shape[1]
    headdim = channels // head_count
    states = state_in.shape[1] // 2
    inner_act = jax.nn.silu(causal_conv(inner_in, taps_inner))
    state_act = jax.nn.silu(causal_conv(state_in, taps_state))
    step_size = jax.nn.softplus(step_in + step_bias)
    log_decay = -step_size * jnp.exp(decay_log)
    block_count = length // GROUP
    weighted = (inner_act.reshape(length, head_count, headdim) * step_size[:, :, None]).reshape(block_count, GROUP, head_count, headdim)
    keys_input = state_act[:, :states].reshape(block_count, GROUP, states)
    queries_read = state_act[:, states:].reshape(block_count, GROUP, states)
    summed = jnp.cumsum(log_decay.reshape(block_count, GROUP, head_count), axis=1)
    summed_heads = jnp.transpose(summed, (0, 2, 1))
    causal = jnp.arange(GROUP)[:, None] >= jnp.arange(GROUP)[None, :]
    gaps_inside = summed_heads[:, :, :, None] - summed_heads[:, :, None, :]
    decays = jnp.where(causal, jnp.exp(jnp.where(causal, gaps_inside, 0.0)), 0.0)
    intersection = jnp.einsum('cin,cjn->cij', queries_read, keys_input, precision=HIGH)
    mixing = decays * intersection[:, None]
    within = jnp.einsum('chij,cjhp->cihp', mixing, weighted, precision=HIGH)
    to_end = jnp.exp(summed[:, -1:, :] - summed)
    block_states = jnp.einsum('cjh,cjn,cjhp->chpn', to_end, keys_input, weighted, precision=HIGH)
    carried = jnp.zeros((head_count, headdim, states), jnp.float32)
    start_list = []
    for block_index in range(block_count):
        start_list.append(carried)
        carried = jnp.exp(summed[block_index, -1])[:, None, None] * carried + block_states[block_index]
    start_states = jnp.stack(start_list)
    across = jnp.einsum('cin,chpn,cih->cihp', queries_read, start_states, jnp.exp(summed), precision=HIGH)
    output = (within + across).reshape(length, channels) + inner_act * jnp.repeat(skip_gain, headdim)
    return output * jax.nn.silu(gate_in)

def apply_layer(resid, params):
    gain_in, inner_w, step_w, state_w, taps_inner, taps_state, gain_gate, head_rows, output_w = params
    model_width = inner_w.shape[0]
    normed = low(norm_rows(resid, gain_in))
    inner_cols = low_back(matmul_high(normed, inner_w.reshape(model_width, -1)))
    half_width = inner_cols.shape[1] // 2
    step_raw = low_back(matmul_high(normed, step_w))
    state_raw = low_back(matmul_high(normed, state_w))
    gated = mixer_core(inner_cols[:, :half_width], inner_cols[:, half_width:], state_raw, step_raw, taps_inner, taps_state, head_rows[0], head_rows[1], head_rows[2])
    scaled = low(norm_rows(gated, gain_gate))
    return resid + low_back(matmul_high(scaled, output_w))

def reference(section_ends, norm_gain, proj_inner, proj_step, proj_state, conv_inner, conv_state, gate_gain, head_params, proj_output):
    weights = (norm_gain.astype(jnp.float32), proj_inner.astype(jnp.float32), proj_step.astype(jnp.float32), proj_state.astype(jnp.float32), conv_inner.astype(jnp.float32), conv_state.astype(jnp.float32), gate_gain.astype(jnp.float32), head_params.astype(jnp.float32), proj_output.astype(jnp.float32))
    inputs = section_ends[0].astype(jnp.float32).reshape(-1, SEQ_LEN, D)
    cotangent = section_ends[1].astype(jnp.float32).reshape(-1, SEQ_LEN, D)

    def network(sequences, params):

        def one_sequence(sequence):
            first_layer = tuple((w[0] for w in params))
            second_layer = tuple((w[1] for w in params))
            hidden = low_back(low(apply_layer(sequence, first_layer)))
            return apply_layer(hidden, second_layer)
        return lax.map(jax.checkpoint(one_sequence), sequences)
    result, pullback = jax.vjp(network, inputs, weights)
    grad_inputs, grad_weights = pullback(cotangent)
    section_results = jnp.stack([grad_inputs.reshape(MICRO, -1, D), result.reshape(MICRO, -1, D)])
    return (section_results, grad_weights[0], grad_weights[1], grad_weights[2], grad_weights[3], grad_weights[4], grad_weights[5], grad_weights[6], grad_weights[7], grad_weights[8])
```

```python
import jax
import jax.numpy as jnp
import numpy as np
from jax import lax
from jax.experimental import pallas as pl
from jax.experimental.pallas import tpu as pltpu
from jax.sharding import Mesh
from jax.sharding import PartitionSpec as P

D = 1536
SEQ = 512
BLOCK = 128
BLOCKS = SEQ // BLOCK
STATES = 128
CHANNELS = 768
HALF = CHANNELS // 2
HEADS = 12
HEAD_DIM = 64
PAIRS = HEADS // 2
DI = 3072
PAD = 8
EPS = 1e-05
NEG = -1e30
DP = ("dp_0", "dp_1")
DP_TENSOR = ("dp_0", "dp_1", "tensor")
SENT = D + 128
BF = jnp.bfloat16
F32 = jnp.float32
HIGH = lax.Precision.HIGHEST
VMEM = pl.BlockSpec(memory_space=pltpu.VMEM)
SMEM = pl.BlockSpec(memory_space=pltpu.SMEM)
LIMIT = pltpu.CompilerParams(vmem_limit_bytes=56 * 1024 * 1024)


def dot_nn(left, right):
    return lax.dot_general(left, right, (((1,), (0,)), ((), ())), preferred_element_type=F32)


def dot_nt(left, right):
    return lax.dot_general(left, right, (((1,), (1,)), ((), ())), preferred_element_type=F32)


def dot_tn(left, right):
    return lax.dot_general(left, right, (((0,), (0,)), ((), ())), preferred_element_type=F32)


def dot_high(left, right):
    return lax.dot_general(
        left, right, (((1,), (0,)), ((), ())), precision=HIGH, preferred_element_type=F32
    )


def sigmoid(v):
    return 1.0 / (1.0 + jnp.exp(-v))


def softplus(v):
    return jnp.maximum(v, 0.0) + jnp.log1p(jnp.exp(-jnp.abs(v)))


def rows_at(index):
    return pl.ds(pl.multiple_of(index * BLOCK, BLOCK), BLOCK)


def iota(shape, dim):
    return lax.broadcasted_iota(jnp.int32, shape, dim)


def two_parts(v):
    upper = v.astype(BF)
    lower = (v - upper.astype(F32)).astype(BF)
    return upper, lower


def lane_tiles(width):
    return [slice(at, at + 128) for at in range(0, width, 128)]


def conv_rows(padded, taps, out):
    for cols in lane_tiles(out.shape[1]):
        for start in range(0, SEQ, BLOCK):
            total = taps[4:5, cols] + taps[0:1, cols] * padded[start + 5 : start + 5 + BLOCK, cols]
            for k in range(1, 4):
                at = start + 5 + k
                total = total + taps[k : k + 1, cols] * padded[at : at + BLOCK, cols]
            out[start : start + BLOCK, cols] = total


def conv_back(padded_grad, padded, taps, grad_taps, store):
    for cols in lane_tiles(padded.shape[1]):
        sums = [jnp.zeros((1, 128), F32)] * 5
        for start in range(0, SEQ, BLOCK):
            own = padded_grad[start : start + BLOCK, cols]
            total = taps[3:4, cols] * own
            sums[4] = sums[4] + jnp.sum(own, axis=0, keepdims=True)
            for k in range(4):
                at = start + 5 + k
                sums[k] = sums[k] + jnp.sum(own * padded[at : at + BLOCK, cols], axis=0, keepdims=True)
                if k < 3:
                    at = start + 3 - k
                    total = total + taps[k : k + 1, cols] * padded_grad[at : at + BLOCK, cols]
            store(start, cols, total.astype(BF))
        for k in range(5):
            grad_taps[k : k + 1, cols] = sums[k]


def step_terms(raw, heads):
    valid = iota((BLOCK, 128), 1) < HEADS
    raised = jnp.where(valid, raw + heads[0:1, :], -30.0)
    step = softplus(raised)
    log_decay = -step * jnp.exp(heads[1:2, :])
    lower = (iota((BLOCK, BLOCK), 0) >= iota((BLOCK, BLOCK), 1)).astype(F32)
    summed = dot_high(lower, log_decay)
    return raised, step, log_decay, summed, jnp.transpose(summed)


def spread(values, head):
    first = iota((BLOCK, 128), 1) < HEAD_DIM
    return jnp.where(first, values[:, head : head + 1], values[:, head + 1 : head + 2])


def side_by_side(v):
    first = iota(v.shape, 1) < HEAD_DIM
    zero = jnp.zeros_like(v)
    return jnp.concatenate([jnp.where(first, v, zero), jnp.where(first, zero, v)], axis=0)


def place_chunks(place, chunks, held):
    for offset, chunk in zip((0, 3, 1, 2), chunks):
        held[rows_at(lax.rem(place + offset, 4)), :] = chunk[...]


def forward_kernel(with_cotangent, *refs):
    where_ref = refs[0]
    chunks = refs[1:5]
    own_w, other_w, taps_ref, taps_state_ref, heads_ref = refs[5:10]
    refs = refs[10:]
    if with_cotangent:
        cot_chunks, refs = refs[:4], refs[4:]
    normed, zx, ss, y_out, starts = refs[:5]
    outs, refs = refs[5:9], refs[9:]
    if with_cotangent:
        cot, dscaled, stats, refs = refs[0], refs[1], refs[2], refs[3:]
    x_pad, state_pad, x_conv, state_conv, hidden, gated_gain = refs
    place, core = where_ref[0], where_ref[1]
    place_chunks(place, chunks, normed)
    zx[core] = dot_nn(normed[...], own_w[:, :CHANNELS])
    zx[1 - core] = dot_nn(normed[...], other_w[:, :CHANNELS])
    ss[...] = dot_nn(normed[...], own_w[:, CHANNELS + HALF :])
    if with_cotangent:
        place_chunks(place, cot_chunks, cot)
        dscaled[core] = dot_nn(cot[...], own_w[:, CHANNELS : CHANNELS + HALF])
        dscaled[1 - core] = dot_nn(cot[...], other_w[:, CHANNELS : CHANNELS + HALF])
    x_pad[:PAD, :] = jnp.zeros((PAD, CHANNELS), F32)
    x_pad[PAD:, :] = zx[1]
    state_pad[:PAD, :] = jnp.zeros((PAD, 2 * STATES), F32)
    state_pad[PAD:, :] = ss[:, : 2 * STATES]
    hidden[...] = jnp.zeros_like(hidden)
    conv_rows(x_pad, taps_ref, x_conv)
    conv_rows(state_pad, taps_state_ref, state_conv)

    def block(b, carry):
        rows = rows_at(b)
        state_u = state_conv[rows, :]
        state = state_u * sigmoid(state_u)
        keys, reads = state[:, :STATES].astype(BF), state[:, STATES:].astype(BF)
        keys_t = jnp.transpose(state[:, :STATES]).astype(BF)
        _, step, _, summed, summed_t = step_terms(ss[rows, 2 * STATES :], heads_ref)
        meets = dot_nt(reads, keys)
        causal = iota((BLOCK, BLOCK), 0) >= iota((BLOCK, BLOCK), 1)
        squares = jnp.zeros((BLOCK, 128), F32)
        crosses = jnp.zeros((BLOCK, 128), F32)
        for p in range(PAIRS):
            cols = slice(p * 128, (p + 1) * 128)
            half, part = p // 3, slice((p % 3) * 128, (p % 3 + 1) * 128)
            u = x_conv[rows, cols]
            x = u * sigmoid(u)
            weighted = x * spread(step, 2 * p)
            summed_wide = spread(summed, 2 * p)
            grown = jnp.exp(summed_wide)
            to_end = jnp.exp(summed_wide[BLOCK - 1 : BLOCK, :] - summed_wide)
            mixes = []
            for h in (2 * p, 2 * p + 1):
                gaps = summed[:, h : h + 1] - summed_t[h : h + 1, :]
                mixes.append((jnp.exp(jnp.where(causal, gaps, NEG)) * meets).astype(BF))
            within = dot_nn(
                jnp.concatenate(mixes, axis=1), side_by_side(weighted).astype(BF)
            )
            held = hidden[:, cols]
            held_low = held.astype(BF)
            starts[b, :, cols] = held_low
            y = within + grown * dot_nn(reads, held_low) + x * taps_ref[6:7, cols]
            hidden[:, cols] = grown[BLOCK - 1 : BLOCK, :] * held + dot_nn(
                keys_t, (to_end * weighted).astype(BF)
            )
            y_out[rows, cols] = y
            z = zx[0, rows, cols]
            gated = y * z * sigmoid(z)
            squares = squares + gated * gated
            gained = gated * taps_ref[5:6, cols]
            gated_gain[half, rows, part] = gained.astype(BF)
            if with_cotangent:
                crosses = crosses + gained * dscaled[half, rows, part]
        square = jnp.sum(squares, axis=1, keepdims=True)
        upper, lower = two_parts(square)
        lane = iota((BLOCK, 128), 1)
        zero = jnp.zeros((BLOCK, 128), F32)
        tail = jnp.where(
            lane == 0, upper.astype(F32), jnp.where(lane == 1, lower.astype(F32), zero)
        ).astype(BF)
        for o, out in enumerate(outs):
            @pl.when(b == lax.rem(place + o, 4))
            def _(out=out):
                out[:, D:] = tail
        if with_cotangent:
            cross = jnp.sum(crosses, axis=1, keepdims=True)
            both = jnp.where(lane == 0, square, jnp.where(lane == 1, cross, zero))
            stats[:, rows] = jnp.transpose(both)[:8, :]
        return carry

    lax.fori_loop(0, BLOCKS, block, 0)
    for o, out in enumerate(outs):
        rows = rows_at(lax.rem(place + o, 4))
        out[:, :D] = (
            dot_nt(gated_gain[core, rows, :], own_w[:, CHANNELS : CHANNELS + HALF])
            + dot_nt(gated_gain[1 - core, rows, :], other_w[:, CHANNELS : CHANNELS + HALF])
        ).astype(BF)


def shape(*dims, dtype=F32):
    return jax.ShapeDtypeStruct(dims, dtype)


def forward_call(where, chunks, own_w, other_w, taps, taps_state, heads, cot_chunks=None):
    out_shape = [
        shape(SEQ, D, dtype=BF),
        shape(2, SEQ, CHANNELS),
        shape(SEQ, 384),
        shape(SEQ, CHANNELS),
        shape(BLOCKS, STATES, CHANNELS, dtype=BF),
    ]
    out_shape += [shape(BLOCK, SENT, dtype=BF)] * 4
    args = [where, *chunks, own_w, other_w, taps, taps_state, heads]
    if cot_chunks is not None:
        args += list(cot_chunks)
        out_shape += [shape(SEQ, D, dtype=BF), shape(2, SEQ, HALF), shape(8, SEQ)]

    def kernel(*refs):
        forward_kernel(cot_chunks is not None, *refs)

    return pl.pallas_call(
        kernel,
        out_shape=out_shape,
        in_specs=[SMEM] + [VMEM] * (len(args) - 1),
        out_specs=[VMEM] * len(out_shape),
        scratch_shapes=[
            pltpu.VMEM((PAD + SEQ, CHANNELS), F32),
            pltpu.VMEM((PAD + SEQ, 2 * STATES), F32),
            pltpu.VMEM((SEQ, CHANNELS), F32),
            pltpu.VMEM((SEQ, 2 * STATES), F32),
            pltpu.VMEM((STATES, CHANNELS), F32),
            pltpu.VMEM((2, SEQ, HALF), BF),
        ],
        compiler_params=LIMIT,
        name="layer_forward",
    )(*args)


def backward_kernel(last, *refs):
    where_ref = refs[0]
    normed, zx, ss, y_in, starts = refs[1:6]
    own_w, other_w, taps_ref, taps_state_ref, heads_ref, gain_ref = refs[6:12]
    refs = refs[12:]
    if last:
        dscaled, refs = refs[0], refs[1:]
        stat_parts, refs = refs[:4], refs[4:]
    else:
        chunks, refs = refs[:4], refs[4:]
    d_own, d_other, dss, scaled_own, scaled_other = refs[:5]
    outs, refs = refs[5:9], refs[9:]
    grad_taps, grad_taps_state, grad_heads, grad_gain = refs[:4]
    refs = refs[4:]
    if not last:
        rows_grad, refs = refs[0], refs[1:]
    x_pad, state_pad, x_conv, state_conv, du_pad, dstate_pad = refs[:6]
    d_hidden, d_inner, scaled, factors = refs[6:10]
    refs = refs[10:]
    if not last:
        dscaled = refs[0]
    place, core = where_ref[0], where_ref[1]
    x_pad[:PAD, :] = jnp.zeros((PAD, CHANNELS), F32)
    x_pad[PAD:, :] = zx[1]
    state_pad[:PAD, :] = jnp.zeros((PAD, 2 * STATES), F32)
    state_pad[PAD:, :] = ss[:, : 2 * STATES]
    du_pad[SEQ:, :] = jnp.zeros((PAD, CHANNELS), F32)
    dstate_pad[SEQ:, :] = jnp.zeros((PAD, 2 * STATES), F32)
    for ref in (d_hidden, grad_taps, grad_taps_state, grad_heads, grad_gain):
        ref[...] = jnp.zeros_like(ref)
    if last:
        total = stat_parts[0][...] + stat_parts[1][...] + stat_parts[2][...] + stat_parts[3][...]
        factor = lax.rsqrt(total[0:1, :] / DI + EPS)
        cubed = factor * factor * factor / DI * total[1:2, :]
        row = iota((128, SEQ), 0)
        both = jnp.where(row == 0, factor, jnp.where(row == 1, cubed, 0.0))
        for b in range(BLOCKS):
            part = slice(b * BLOCK, (b + 1) * BLOCK)
            factors[part, :] = jnp.transpose(both[:, part])
    else:
        for offset, chunk in zip((0, 3, 1, 2), chunks):
            rows = rows_at(lax.rem(place + offset, 4))
            rows_grad[rows, :] = chunk[:, :D]
            tail = chunk[:, D:].astype(F32)
            factor = tail[:, 0:1] + tail[:, 1:2]
            cross = tail[:, 2:3] + tail[:, 3:4]
            lane = iota((BLOCK, 128), 1)
            cubed = factor * factor * factor / DI * cross
            factors[rows, :] = jnp.where(lane == 0, factor, jnp.where(lane == 1, cubed, 0.0))
        dscaled[core] = dot_nn(rows_grad[...], own_w[:, CHANNELS : CHANNELS + HALF])
        dscaled[1 - core] = dot_nn(rows_grad[...], other_w[:, CHANNELS : CHANNELS + HALF])

    conv_rows(x_pad, taps_ref, x_conv)
    conv_rows(state_pad, taps_state_ref, state_conv)

    def block(turn, carry):
        b = BLOCKS - 1 - turn
        rows = rows_at(b)
        state_u = state_conv[rows, :]
        state_s = sigmoid(state_u)
        state = state_u * state_s
        keys, reads = state[:, :STATES].astype(BF), state[:, STATES:].astype(BF)
        reads_t = jnp.transpose(state[:, STATES:]).astype(BF)
        raised, step, log_decay, summed, summed_t = step_terms(ss[rows, 2 * STATES :], heads_ref)
        meets_t = dot_nt(keys, reads)
        causal_t = iota((BLOCK, BLOCK), 1) >= iota((BLOCK, BLOCK), 0)
        fac = factors[rows, :][:, 0:1]
        cub = factors[rows, :][:, 1:2]
        d_meets_t = jnp.zeros((BLOCK, BLOCK), F32)
        d_keys = jnp.zeros((BLOCK, STATES), F32)
        d_reads = jnp.zeros((BLOCK, STATES), F32)
        head_sums = jnp.zeros((2 * BLOCK, 128), F32)
        last_row = iota((BLOCK, 128), 0) == BLOCK - 1
        for p in range(PAIRS):
            cols = slice(p * 128, (p + 1) * 128)
            half, part = p // 3, slice((p % 3) * 128, (p % 3 + 1) * 128)
            u = x_conv[rows, cols]
            us = sigmoid(u)
            x = u * us
            step_wide = spread(step, 2 * p)
            summed_wide = spread(summed, 2 * p)
            grown = jnp.exp(summed_wide)
            end = grown[BLOCK - 1 : BLOCK, :]
            to_end = jnp.exp(summed_wide[BLOCK - 1 : BLOCK, :] - summed_wide)
            skip = taps_ref[6:7, cols]
            gain = taps_ref[5:6, cols]
            z = zx[0, rows, cols]
            zs = sigmoid(z)
            z_act = z * zs
            y = y_in[rows, cols]
            gated = y * z_act
            incoming = dscaled[half, rows, part]
            lifted = gated * fac
            scaled[half, rows, part] = (lifted * gain).astype(BF)
            grad_taps[5:6, cols] += jnp.sum(incoming * lifted, axis=0, keepdims=True)
            d_gated = fac * (gain * incoming) - gated * cub
            dy = d_gated * z_act
            d_inner[0, rows, cols] = (d_gated * y * (zs + z_act * (1.0 - zs))).astype(BF)
            dy_low = dy.astype(BF)
            weighted = x * step_wide
            weighted_low = weighted.astype(BF)
            dy_grown = (dy * grown).astype(BF)
            held_low = starts[b, :, cols]
            dh = d_hidden[:, cols]
            dh_low = dh.astype(BF)
            d_reads = d_reads + dot_nt(dy_grown, held_low)
            kept = dot_nn(keys, dh_low) * to_end
            d_keys = d_keys + dot_nt((to_end * weighted).astype(BF), dh_low)
            decays = []
            for h in (2 * p, 2 * p + 1):
                gaps = summed_t[h : h + 1, :] - summed[:, h : h + 1]
                decays.append(jnp.exp(jnp.where(causal_t, gaps, NEG)))
            mixes = jnp.concatenate([(d * meets_t).astype(BF) for d in decays], axis=1)
            d_weighted = dot_nn(mixes, side_by_side(dy).astype(BF)) + kept
            d_mixes = dot_nt(side_by_side(weighted).astype(BF), dy_low)
            d_meets_t = d_meets_t + d_mixes[:BLOCK] * decays[0] + d_mixes[BLOCK:] * decays[1]
            dx = skip * dy + d_weighted * step_wide
            weighted_f = weighted_low.astype(F32)
            moved = dy_low.astype(F32) * (y - skip * x) - weighted_f * d_weighted
            extra = jnp.sum(weighted_f * kept, axis=0, keepdims=True) + end * jnp.sum(
                dh * held_low.astype(F32), axis=0, keepdims=True
            )
            moved = jnp.where(last_row, moved + extra, moved)
            upper, lower = two_parts(jnp.concatenate([moved, x * d_weighted], axis=0))
            picks = (
                iota((256, 128), 1) == 2 * p + (iota((256, 128), 0) % 128) // HEAD_DIM
            ).astype(BF)
            head_sums = head_sums + dot_nn(jnp.concatenate([upper, lower], axis=1), picks)
            grad_taps[6:7, cols] += jnp.sum(dy * x, axis=0, keepdims=True)
            du_pad[rows, cols] = dx * (us + x * (1.0 - us))
            d_hidden[:, cols] = end * dh + dot_nn(reads_t, dy_grown)
        d_reads = d_reads + dot_nn(jnp.transpose(d_meets_t).astype(BF), keys)
        d_keys = d_keys + dot_nn(d_meets_t.astype(BF), reads)
        d_state = jnp.concatenate([d_keys, d_reads], axis=1)
        d_state = d_state * (state_s + state * (1.0 - state_s))
        dstate_pad[rows, :] = d_state
        upper_tri = (iota((BLOCK, BLOCK), 1) >= iota((BLOCK, BLOCK), 0)).astype(F32)
        d_decay = dot_high(upper_tri, head_sums[:BLOCK])
        d_step = head_sums[BLOCK:] - d_decay * jnp.exp(heads_ref[1:2, :])
        d_raw = d_step * sigmoid(raised)
        dss[rows, 2 * STATES :] = d_raw.astype(BF)
        grad_heads[0:1, :] += jnp.sum(d_raw, axis=0, keepdims=True)
        grad_heads[1:2, :] += jnp.sum(d_decay * log_decay, axis=0, keepdims=True)
        return carry

    lax.fori_loop(0, BLOCKS, block, 0)

    def store_inner(start, cols, value):
        d_inner[1, start : start + BLOCK, cols] = value

    def store_state(start, cols, value):
        dss[start : start + BLOCK, cols] = value

    conv_back(du_pad, x_pad, taps_ref, grad_taps, store_inner)
    conv_back(dstate_pad, state_pad, taps_state_ref, grad_taps_state, store_state)
    picks = (iota((CHANNELS, 128), 1) == iota((CHANNELS, 128), 0) // HEAD_DIM).astype(F32)
    grad_heads[2:3, :] = dot_high(grad_taps[...], picks)[6:7, :]
    for o, out in enumerate(outs):
        rows = rows_at(lax.rem(place + o, 4))
        part = (
            dot_nt(d_inner[core, rows, :], own_w[:, :CHANNELS])
            + dot_nt(d_inner[1 - core, rows, :], other_w[:, :CHANNELS])
            + dot_nt(dss[rows, :], own_w[:, CHANNELS + HALF :])
        )
        grad_gain[...] += jnp.sum(part * normed[rows, :].astype(F32), axis=0, keepdims=True)
        out[...] = part.astype(BF)
    grad_gain[...] = grad_gain[...] / gain_ref[...]
    d_own[...] = d_inner[core]
    d_other[...] = d_inner[1 - core]
    scaled_own[...] = scaled[core]
    scaled_other[...] = scaled[1 - core]


def backward_call(where, kept, own_w, other_w, taps, taps_state, heads, gain, last, extra):
    args = [where, *kept, own_w, other_w, taps, taps_state, heads, gain, *extra]
    out_shape = [
        shape(SEQ, CHANNELS, dtype=BF),
        shape(SEQ, CHANNELS, dtype=BF),
        shape(SEQ, 384, dtype=BF),
        shape(SEQ, HALF, dtype=BF),
        shape(SEQ, HALF, dtype=BF),
    ]
    out_shape += [shape(BLOCK, D, dtype=BF)] * 4
    out_shape += [shape(8, CHANNELS), shape(8, 2 * STATES), shape(8, 128), shape(1, D)]
    scratch = [
        pltpu.VMEM((PAD + SEQ, CHANNELS), F32),
        pltpu.VMEM((PAD + SEQ, 2 * STATES), F32),
        pltpu.VMEM((SEQ, CHANNELS), F32),
        pltpu.VMEM((SEQ, 2 * STATES), F32),
        pltpu.VMEM((PAD + SEQ, CHANNELS), F32),
        pltpu.VMEM((PAD + SEQ, 2 * STATES), F32),
        pltpu.VMEM((STATES, CHANNELS), F32),
        pltpu.VMEM((2, SEQ, CHANNELS), BF),
        pltpu.VMEM((2, SEQ, HALF), BF),
        pltpu.VMEM((SEQ, 128), F32),
    ]
    if not last:
        out_shape += [shape(SEQ, D, dtype=BF)]
        scratch += [pltpu.VMEM((2, SEQ, HALF), F32)]

    def kernel(*refs):
        backward_kernel(last, *refs)

    return pl.pallas_call(
        kernel,
        out_shape=out_shape,
        in_specs=[SMEM] + [VMEM] * (len(args) - 1),
        out_specs=[VMEM] * len(out_shape),
        scratch_shapes=scratch,
        compiler_params=LIMIT,
        name="layer_backward",
    )(*args)


def norm_kernel(rows_ref, gain_ref, out):
    v = rows_ref[...].astype(F32)
    q = lax.rsqrt(jnp.mean(v * v, axis=1, keepdims=True) + EPS)
    out[...] = (v * q * gain_ref[...]).astype(BF)


def norm_call(rows, gain):
    return pl.pallas_call(
        norm_kernel,
        out_shape=shape(BLOCK, D, dtype=BF),
        in_specs=[VMEM] * 2,
        out_specs=VMEM,
        name="norm_rows",
    )(rows, gain)


def arrived(parts):
    return sum((part[...].astype(F32) for part in parts[1:]), parts[0][...].astype(F32))


def after_first_kernel(rows_ref, a, b, c, d, gain_ref, hidden, normed, mixed, factor_out):
    total = arrived((a, b, c, d))
    mixed[...] = total[:, :D]
    square = total[:, D : D + 1] + total[:, D + 1 : D + 2]
    factor = lax.rsqrt(square / DI + EPS)
    factor_out[...] = jnp.broadcast_to(factor, (BLOCK, 128))
    low = (rows_ref[...].astype(F32) + factor * total[:, :D]).astype(BF)
    hidden[...] = low
    v = low.astype(F32)
    q = lax.rsqrt(jnp.mean(v * v, axis=1, keepdims=True) + EPS)
    normed[...] = (v * q * gain_ref[...]).astype(BF)


def after_first_call(rows, parts, gain):
    return pl.pallas_call(
        after_first_kernel,
        out_shape=[
            shape(BLOCK, D, dtype=BF),
            shape(BLOCK, D, dtype=BF),
            shape(BLOCK, D),
            shape(BLOCK, 128),
        ],
        in_specs=[VMEM] * 6,
        out_specs=[VMEM] * 4,
        name="between_layers",
    )(rows, *parts, gain)


def after_last_kernel(rows_ref, a, b, c, d, result):
    total = arrived((a, b, c, d))
    square = total[:, D : D + 1] + total[:, D + 1 : D + 2]
    factor = lax.rsqrt(square / DI + EPS)
    result[...] = rows_ref[...].astype(F32) + factor * total[:, :D]


def after_last_call(rows, parts):
    return pl.pallas_call(
        after_last_kernel,
        out_shape=shape(BLOCK, D),
        in_specs=[VMEM] * 5,
        out_specs=VMEM,
        name="last_rows",
    )(rows, *parts)


def rows_back(rows_ref, parts, gain_ref, grad_ref):
    incoming = arrived(parts)
    v = rows_ref[...].astype(F32)
    q = lax.rsqrt(jnp.mean(v * v, axis=1, keepdims=True) + EPS)
    weighted = incoming * gain_ref[...]
    inner = jnp.sum(weighted * v, axis=1, keepdims=True)
    return grad_ref[...].astype(F32) + q * weighted - v * (q * q * q / D * inner)


def back_last_kernel(rows_ref, a, b, c, d, gain_ref, grad_ref, mixed_ref, factor_ref, out):
    low = rows_back(rows_ref, (a, b, c, d), gain_ref, grad_ref).astype(BF)
    out[:, :D] = low
    cross = jnp.sum(low.astype(F32) * mixed_ref[...], axis=1, keepdims=True)
    factor = factor_ref[:, 0:1]
    pieces = [*two_parts(factor), *two_parts(cross)]
    lane = iota((BLOCK, 128), 1)
    tail = jnp.zeros((BLOCK, 128), F32)
    for k, piece in enumerate(pieces):
        tail = jnp.where(lane == k, piece.astype(F32), tail)
    out[:, D:] = tail.astype(BF)


def back_last_call(rows, parts, gain, grad, mixed, factor):
    return pl.pallas_call(
        back_last_kernel,
        out_shape=shape(BLOCK, SENT, dtype=BF),
        in_specs=[VMEM] * 9,
        out_specs=VMEM,
        name="between_layers_back",
    )(rows, *parts, gain, grad, mixed, factor)


def back_first_kernel(rows_ref, a, b, c, d, gain_ref, grad_ref, out):
    out[...] = rows_back(rows_ref, (a, b, c, d), gain_ref, grad_ref[:, :D])


def back_first_call(rows, parts, gain, grad):
    return pl.pallas_call(
        back_first_kernel,
        out_shape=shape(BLOCK, D),
        in_specs=[VMEM] * 7,
        out_specs=VMEM,
        name="first_rows_back",
    )(rows, *parts, gain, grad)


def swap(v):
    return lax.ppermute(v, "section", [(0, 1), (1, 0)])


def turn(v, by):
    return lax.ppermute(v, "tensor", [(i, (i + by) % 4) for i in range(4)])


def spread_rows(v):
    return (v, turn(v, 1), turn(v, -1), turn(v, 2))


def meet(parts):
    own, ahead, across, behind = parts
    return (own, turn(ahead, 1), turn(behind, -1), turn(across, 2))


def pick(v, index, axis):
    return lax.dynamic_index_in_dim(v, index, axis, keepdims=False)


def shards(
    section_ends,
    norm_gain,
    proj_inner,
    proj_step,
    proj_state,
    conv_inner,
    conv_state,
    gate_gain,
    head_params,
    proj_output,
):
    core = lax.axis_index("section")
    place = lax.axis_index("tensor")
    is_first = core == 0
    where = jnp.stack([place, core]).astype(jnp.int32)

    ends = section_ends[0]
    got_rows = swap(pick(ends, 1 - core, 0))
    rows_in = jnp.where(is_first, ends[0], got_rows)
    cot = jnp.where(is_first, got_rows, ends[1])

    inner = proj_inner[0]
    out_t = proj_output[0].T.reshape(96, 2, HALF)
    packed = jnp.concatenate(
        [
            proj_state[0].reshape(-1),
            norm_gain[0],
            conv_inner[0].reshape(-1),
            gate_gain[0],
            conv_state[0].reshape(-1),
            jnp.zeros((32 * 256 - 6144 - 332,), BF),
        ]
    ).reshape(32, 256)
    filled = lax.all_gather(packed, "tensor", axis=0).reshape(4, 32 * 256)
    state_rows = filled[:, :6144].reshape(96, 256)
    norm_col = filled[:, 6144:6168].reshape(96, 1)
    inner_cols = filled[:, 6168:6408].reshape(4, 5, 48).transpose(0, 2, 1).reshape(192, 5)
    gate_col = filled[:, 6408:6456].reshape(192, 1)
    both = jnp.concatenate([inner_cols, gate_col], axis=1)
    both = both.reshape(2, 96, 6).transpose(1, 0, 2).reshape(96, 12)
    state_cols = filled[:, 6456:6476].reshape(4, 5, 4).transpose(0, 2, 1).reshape(16, 5)
    state_cols = jnp.pad(state_cols, ((0, 80), (0, 0)))
    misc = jnp.concatenate(
        [proj_step[0], both, norm_col, state_cols, jnp.zeros((96, 128 - 30), BF)], axis=1
    )
    rest = jnp.concatenate([state_rows, misc], axis=1)
    keep = jnp.concatenate([pick(inner, core, 1), pick(out_t, core, 1), rest], axis=1)
    give = jnp.concatenate([pick(inner, 1 - core, 1), pick(out_t, 1 - core, 1), rest], axis=1)
    got = swap(give)
    own_w, other_w, taps, taps_state, gains = [], [], [], [], []
    for layer in range(2):
        shard = jnp.where(core == layer, keep, got)
        full = lax.all_gather(shard, DP, axis=0, tiled=True)
        own_w.append(full)
        other_w.append(swap(full[:, : CHANNELS + HALF]))
        small = full[:, CHANNELS + HALF + 256 :].astype(F32)
        gains.append(small[:, 24].reshape(1, D))
        mine = lax.dynamic_slice_in_dim(small, place * 384, 384, 0)[:, 12:24]
        taps.append(mine.reshape(4, 96, 2, 6).transpose(3, 0, 2, 1).reshape(6, CHANNELS))
        taps_state.append(
            jnp.pad(
                small.reshape(16, 96, 128)[:, :16, 25:30].reshape(256, 5).T, ((0, 3), (0, 0))
            )
        )
    heads_own = head_params[0].astype(F32)
    heads_got = swap(head_params[0]).astype(F32)
    heads = []
    for layer in range(2):
        h = jnp.where(core == layer, heads_own, heads_got)
        taps[layer] = jnp.concatenate(
            [taps[layer], jnp.repeat(h[2], HEAD_DIM)[None], jnp.zeros((1, CHANNELS), F32)], axis=0
        )
        heads.append(jnp.pad(h, ((0, 5), (0, 128 - HEADS))))

    normed_0 = norm_call(rows_in, gains[0])
    kept_0 = forward_call(
        where, spread_rows(normed_0), own_w[0], other_w[0], taps[0], taps_state[0], heads[0]
    )
    hidden, normed_1, mixed_0, factor_0 = after_first_call(rows_in, meet(kept_0[5:9]), gains[1])
    kept_1 = forward_call(
        where,
        spread_rows(normed_1),
        own_w[1],
        other_w[1],
        taps[1],
        taps_state[1],
        heads[1],
        spread_rows(cot),
    )
    cot_rows, dscaled_1, stats = kept_1[9:]
    back_1 = backward_call(
        where,
        kept_1[:5],
        own_w[1],
        other_w[1],
        taps[1],
        taps_state[1],
        heads[1],
        gains[1],
        True,
        (dscaled_1, *spread_rows(stats)),
    )
    result = after_last_call(hidden, meet(kept_1[5:9]))
    grad_1 = back_last_call(hidden, meet(back_1[5:9]), gains[1], cot, mixed_0, factor_0)
    back_0 = backward_call(
        where,
        kept_0[:5],
        own_w[0],
        other_w[0],
        taps[0],
        taps_state[0],
        heads[0],
        gains[0],
        False,
        spread_rows(grad_1),
    )
    grad_0 = back_first_call(rows_in, meet(back_0[5:9]), gains[0], grad_1)

    def weight_grads(normed, rows_grad, back):
        d_own, d_other, dss, scaled_own, scaled_other = back[:5]
        grad_taps, grad_taps_state, grad_heads, grad_gain = back[9:13]
        theirs = jnp.concatenate(
            [dot_tn(normed, d_other).astype(BF), dot_tn(rows_grad, scaled_other).astype(BF)],
            axis=1,
        )
        given = swap(theirs).astype(F32)
        mine_in = dot_tn(normed, d_own) + given[:, :CHANNELS]
        mine_out = dot_tn(rows_grad, scaled_own) + given[:, CHANNELS:]
        shared = dot_tn(normed, dss)
        lines = jnp.concatenate([grad_taps[:6]], axis=0)
        lines = lines.reshape(6, 4, 2, 96).transpose(1, 3, 2, 0).reshape(384, 12)
        lines = lax.dynamic_update_slice_in_dim(
            jnp.zeros((D, 12), F32), lines, place * 384, 0
        )
        state_lines = jnp.pad(
            grad_taps_state[:5].T.reshape(16, 16, 5), ((0, 0), (0, 80), (0, 0))
        ).reshape(D, 5)
        head_lines = jnp.pad(grad_heads[:3, :HEADS].T, ((0, 84), (0, 0)))
        head_lines = jnp.tile(head_lines, (16, 1))
        payload = jnp.concatenate(
            [
                mine_in,
                mine_out,
                shared[:, : 256 + HEADS],
                lines,
                grad_gain.reshape(D, 1),
                state_lines,
                head_lines,
                jnp.zeros((D, 128 - 33), F32),
            ],
            axis=1,
        ).astype(BF)
        return lax.psum_scatter(payload, DP, scatter_dimension=0, tiled=True).astype(F32)

    share_1 = weight_grads(kept_1[0], cot_rows, back_1)
    share_0 = weight_grads(kept_0[0], back_0[13], back_0)
    share_own = jnp.where(is_first, share_0, share_1)
    share_got = swap(jnp.where(is_first, share_1, share_0).astype(BF)).astype(F32)
    halves_in = jnp.stack([share_own[:, :CHANNELS], share_got[:, :CHANNELS]], axis=1)
    grad_inner = jnp.where(is_first, halves_in, halves_in[:, ::-1])
    out_own = share_own[:, CHANNELS : CHANNELS + HALF]
    out_got = share_got[:, CHANNELS : CHANNELS + HALF]
    grad_output = jnp.where(
        is_first,
        jnp.concatenate([out_own, out_got], axis=1),
        jnp.concatenate([out_got, out_own], axis=1),
    ).T
    summed = (share_own + share_got)[:, CHANNELS + HALF :]
    misc = summed[:, 256:]
    grad_step = misc[:, :HEADS]
    grad_heads = misc[:HEADS, 30:33].T
    to_send = jnp.concatenate(
        [
            summed[:, :256].reshape(4, 6144),
            misc[:, 24].reshape(4, 24),
            misc[:, 12:24].reshape(96, 2, 6).transpose(1, 0, 2).reshape(4, 48 * 6),
            misc[:16, 25:30].reshape(4, 20),
            jnp.zeros((4, 32 * 256 - 6144 - 332), F32),
        ],
        axis=1,
    ).reshape(4, 32, 256)
    pieces = [pick(to_send, lax.rem(place + o, 4), 0) for o in range(4)]
    met = meet(pieces)
    total = (met[0] + met[1] + met[2] + met[3]).reshape(-1)
    grad_state = total[:6144].reshape(24, 256)
    grad_norm = total[6144:6168]
    inner_lines = total[6168:6456].reshape(48, 6).T
    grad_conv_inner = inner_lines[:5]
    grad_gate = inner_lines[5]
    grad_conv_state = total[6456:6476].reshape(4, 5).T
    rows_got = swap(jnp.where(is_first, result, grad_0))
    section_rows = jnp.where(
        is_first, jnp.stack([grad_0, rows_got]), jnp.stack([rows_got, result])
    )
    return (
        section_rows[None],
        grad_norm[None],
        grad_inner[None],
        grad_step[None],
        grad_state[None],
        grad_conv_inner[None],
        grad_conv_state[None],
        grad_gate[None],
        grad_heads[None],
        grad_output[None],
    )


def solution(mesh):
    split = Mesh(
        mesh.devices.reshape(mesh.shape["section"], 4, 4, mesh.shape["tensor"]),
        ("section", "dp_0", "dp_1", "tensor"),
    )
    return jax.shard_map(
        shards,
        mesh=split,
        in_specs=(
            P("section", None, DP_TENSOR, None),
            P("section", DP_TENSOR),
            P("section", DP, None, "tensor"),
            P("section", DP, "tensor"),
            P("section", DP_TENSOR, None),
            P("section", None, DP_TENSOR),
            P("section", None, DP_TENSOR),
            P("section", DP_TENSOR),
            P("section", None, "tensor"),
            P("section", "tensor", DP),
        ),
        out_specs=(
            P("section", None, DP_TENSOR, None),
            P("section", DP_TENSOR),
            P("section", DP, None, "tensor"),
            P("section", DP, "tensor"),
            P("section", DP_TENSOR, None),
            P("section", None, DP_TENSOR),
            P("section", None, DP_TENSOR),
            P("section", DP_TENSOR),
            P("section", None, "tensor"),
            P("section", "tensor", DP),
        ),
        check_vma=False,
    )
```

```python
import jax
import jax.numpy as jnp
import numpy as np
from jax import lax
from jax.experimental import pallas as pl
from jax.experimental.pallas import tpu as pltpu
from jax.sharding import Mesh
from jax.sharding import PartitionSpec as P

D = 1536
SEQ = 512
BLOCK = 128
BLOCKS = SEQ // BLOCK
STATES = 128
CHANNELS = 768
HALF = CHANNELS // 2
HEADS = 12
HEAD_DIM = 64
PAIRS = HEADS // 2
DI = 3072
PAD = 8
EPS = 1e-05
NEG = -1e30
DP = ("dp_0", "dp_1")
DP_TENSOR = ("dp_0", "dp_1", "tensor")
SENT = D + 128
BF = jnp.bfloat16
F32 = jnp.float32
HIGH = lax.Precision.HIGHEST
VMEM = pl.BlockSpec(memory_space=pltpu.VMEM)
SMEM = pl.BlockSpec(memory_space=pltpu.SMEM)
HBM = pl.BlockSpec(memory_space=pltpu.HBM)
ANY = pl.BlockSpec(memory_space=pl.ANY)
WIDE = CHANNELS + HALF + 256
IN = slice(0, CHANNELS)
OUT = slice(CHANNELS, CHANNELS + HALF)
STATE = slice(CHANNELS + HALF, CHANNELS + HALF + 128)
MISC = slice(CHANNELS + HALF + 128, WIDE)
REST = slice(CHANNELS + HALF, WIDE)
SPLIT = 768
VMEM_LIMIT = 54


def shape(*dims, dtype=F32):
    return jax.ShapeDtypeStruct(dims, dtype)


def limit(megabytes):
    return pltpu.CompilerParams(vmem_limit_bytes=megabytes * 1024 * 1024)


def cost(flops, read):
    return pl.CostEstimate(flops=flops, bytes_accessed=read, transcendentals=0)


def dot_nn(left, right):
    return lax.dot_general(left, right, (((1,), (0,)), ((), ())), preferred_element_type=F32)


def dot_nt(left, right):
    return lax.dot_general(left, right, (((1,), (1,)), ((), ())), preferred_element_type=F32)


def dot_tn(left, right):
    return lax.dot_general(left, right, (((0,), (0,)), ((), ())), preferred_element_type=F32)


def dot_high(left, right):
    return lax.dot_general(
        left, right, (((1,), (0,)), ((), ())), precision=HIGH, preferred_element_type=F32
    )


def sigmoid(v):
    return 1.0 / (1.0 + jnp.exp(-v))


def softplus(v):
    return jnp.maximum(v, 0.0) + jnp.log1p(jnp.exp(-jnp.abs(v)))


def rows_at(index):
    return pl.ds(pl.multiple_of(index * BLOCK, BLOCK), BLOCK)


def lanes_at(index):
    return pl.ds(pl.multiple_of(index * 128, 128), 128)


def iota(shape, dim):
    return lax.broadcasted_iota(jnp.int32, shape, dim)


def two_parts(v):
    upper = v.astype(BF)
    lower = (v - upper.astype(F32)).astype(BF)
    return upper, lower


def lane_tiles(width):
    return [slice(at, at + 128) for at in range(0, width, 128)]


def conv_rows(padded, taps, out):
    for cols in lane_tiles(out.shape[1]):
        for start in range(0, SEQ, BLOCK):
            total = taps[4:5, cols] + taps[0:1, cols] * padded[start + 5 : start + 5 + BLOCK, cols]
            for k in range(1, 4):
                at = start + 5 + k
                total = total + taps[k : k + 1, cols] * padded[at : at + BLOCK, cols]
            out[start : start + BLOCK, cols] = total


def conv_back(padded_grad, padded, taps, grad_taps, store):
    for cols in lane_tiles(padded.shape[1]):
        sums = [jnp.zeros((1, 128), F32)] * 5
        for start in range(0, SEQ, BLOCK):
            own = padded_grad[start : start + BLOCK, cols]
            total = taps[3:4, cols] * own
            sums[4] = sums[4] + jnp.sum(own, axis=0, keepdims=True)
            for k in range(4):
                at = start + 5 + k
                sums[k] = sums[k] + jnp.sum(own * padded[at : at + BLOCK, cols], axis=0, keepdims=True)
                if k < 3:
                    at = start + 3 - k
                    total = total + taps[k : k + 1, cols] * padded_grad[at : at + BLOCK, cols]
            store(start, cols, total.astype(BF))
        for k in range(5):
            grad_taps[k : k + 1, cols] = sums[k]


def step_terms(raw, heads):
    valid = iota((BLOCK, 128), 1) < HEADS
    raised = jnp.where(valid, raw + heads[0:1, :], -30.0)
    step = softplus(raised)
    log_decay = -step * jnp.exp(heads[1:2, :])
    lower = (iota((BLOCK, BLOCK), 0) >= iota((BLOCK, BLOCK), 1)).astype(F32)
    summed = dot_high(lower, log_decay)
    return raised, step, log_decay, summed, jnp.transpose(summed)


def spread(values, head):
    first = iota((BLOCK, 128), 1) < HEAD_DIM
    return jnp.where(first, values[:, head : head + 1], values[:, head + 1 : head + 2])


def side_by_side(v):
    first = iota(v.shape, 1) < HEAD_DIM
    zero = jnp.zeros_like(v)
    return jnp.concatenate([jnp.where(first, v, zero), jnp.where(first, zero, v)], axis=0)


class Copies:
    def __init__(self, sems):
        self.sems = sems
        self.count = 0
        self.pending = []

    def start(self, source, target):
        copy = pltpu.make_async_copy(source, target, self.sems.at[self.count])
        self.count += 1
        copy.start()
        return copy

    def store(self, source, target):
        self.pending.append(self.start(source, target))

    def finish(self):
        for copy in self.pending:
            copy.wait()


def forward_kernel(last, *refs):
    refs = list(refs)

    def take(n):
        taken, refs[:n] = refs[:n], []
        return taken

    (where_ref,), chunks, (own_in, other_in) = take(1), take(4 if last else 1), take(2)
    taps_ref, taps_state_ref, heads_ref, gain_ref = take(4)
    cot = take(1)[0] if last else None
    normed_out, zx_out, ss_out, y_out, starts_out, gg_out = take(6)
    if last:
        dscaled_out, stats, mixed_out = take(3)
    else:
        outs = take(4)
    own_w, other_w, normed, zx, ss, y_all, starts, gated_gain = take(8)
    x_pad, state_pad, x_conv, state_conv, hidden, sems = take(6)
    if last:
        dscaled, mixed = take(2)
    copies = Copies(sems)
    place, core = where_ref[0], where_ref[1]
    loads = []
    for cols in (IN, REST, OUT):
        loads.append(copies.start(own_in.at[:, cols], own_w.at[:, cols]))
        loads.append(copies.start(other_in.at[:, cols], other_w.at[:, cols]))
    for k, offset in enumerate((0, 3, 1, 2)):
        rows = rows_at(lax.rem(place + offset, 4))
        v = (chunks[k][...] if last else chunks[0][lax.rem(place + offset, 4), 0]).astype(F32)
        q = lax.rsqrt(jnp.mean(v * v, axis=1, keepdims=True) + EPS)
        normed[rows, :] = (v * q * gain_ref[...]).astype(BF)
    copies.store(normed, normed_out)
    loads[0].wait()
    zx[core] = dot_nn(normed[...], own_w[:, IN])
    loads[1].wait()
    zx[1 - core] = dot_nn(normed[...], other_w[:, IN])
    copies.store(zx, zx_out)
    loads[2].wait()
    ss[:, lanes_at(core)] = dot_nn(normed[...], own_w[:, STATE])
    ss[:, 2 * STATES :] = dot_nn(normed[...], own_w[:, MISC])
    loads[3].wait()
    ss[:, lanes_at(1 - core)] = dot_nn(normed[...], other_w[:, STATE])
    copies.store(ss, ss_out)
    loads[4].wait()
    loads[5].wait()
    if last:
        for k in range(BLOCKS):
            rows = slice(k * BLOCK, (k + 1) * BLOCK)
            dscaled[core, rows, :] = dot_nn(cot[k, 1], own_w[:, OUT])
            dscaled[1 - core, rows, :] = dot_nn(cot[k, 1], other_w[:, OUT])
        copies.store(dscaled, dscaled_out)
    x_pad[:PAD, :] = jnp.zeros((PAD, CHANNELS), F32)
    x_pad[PAD:, :] = zx[1]
    state_pad[:PAD, :] = jnp.zeros((PAD, 2 * STATES), F32)
    state_pad[PAD:, :] = ss[:, : 2 * STATES]
    hidden[...] = jnp.zeros_like(hidden)
    conv_rows(x_pad, taps_ref, x_conv)
    conv_rows(state_pad, taps_state_ref, state_conv)

    def block(b, carry):
        rows = rows_at(b)
        state_u = state_conv[rows, :]
        state = state_u * sigmoid(state_u)
        keys, reads = state[:, :STATES].astype(BF), state[:, STATES:].astype(BF)
        keys_t = jnp.transpose(state[:, :STATES]).astype(BF)
        _, step, _, summed, summed_t = step_terms(ss[rows, 2 * STATES :], heads_ref)
        meets = dot_nt(reads, keys)
        causal = iota((BLOCK, BLOCK), 0) >= iota((BLOCK, BLOCK), 1)
        squares = jnp.zeros((BLOCK, 128), F32)
        crosses = jnp.zeros((BLOCK, 128), F32)
        for p in range(PAIRS):
            cols = slice(p * 128, (p + 1) * 128)
            half, part = p // 3, slice((p % 3) * 128, (p % 3 + 1) * 128)
            u = x_conv[rows, cols]
            x = u * sigmoid(u)
            weighted = x * spread(step, 2 * p)
            summed_wide = spread(summed, 2 * p)
            grown = jnp.exp(summed_wide)
            to_end = jnp.exp(summed_wide[BLOCK - 1 : BLOCK, :] - summed_wide)
            mixes = []
            for h in (2 * p, 2 * p + 1):
                gaps = summed[:, h : h + 1] - summed_t[h : h + 1, :]
                mixes.append((jnp.exp(jnp.where(causal, gaps, NEG)) * meets).astype(BF))
            within = dot_nn(
                jnp.concatenate(mixes, axis=1), side_by_side(weighted).astype(BF)
            )
            held = hidden[:, cols]
            held_low = held.astype(BF)
            starts[b, :, cols] = held_low
            y = within + grown * dot_nn(reads, held_low) + x * taps_ref[6:7, cols]
            hidden[:, cols] = grown[BLOCK - 1 : BLOCK, :] * held + dot_nn(
                keys_t, (to_end * weighted).astype(BF)
            )
            y_all[rows, cols] = y
            z = zx[0, rows, cols]
            gated = y * z * sigmoid(z)
            squares = squares + gated * gated
            gained = gated * taps_ref[5:6, cols]
            gated_gain[half, rows, part] = gained.astype(BF)
            if last:
                crosses = crosses + gained * dscaled[half, rows, part]
        square = jnp.sum(squares, axis=1, keepdims=True)
        upper, lower = two_parts(square)
        lane = iota((BLOCK, 128), 1)
        zero = jnp.zeros((BLOCK, 128), F32)
        tail = jnp.where(
            lane == 0, upper.astype(F32), jnp.where(lane == 1, lower.astype(F32), zero)
        ).astype(BF)
        for o, out in enumerate(() if last else outs):

            @pl.when(b == lax.rem(place + o, 4))
            def _(out=out):
                out[:, D:] = tail

        if last:
            cross = jnp.sum(crosses, axis=1, keepdims=True)
            both = jnp.where(lane == 0, square, jnp.where(lane == 1, cross, zero))
            stats[:, rows] = jnp.transpose(both)[:8, :]
        return carry

    lax.fori_loop(0, BLOCKS, block, 0)
    copies.store(y_all, y_out)
    copies.store(starts, starts_out)
    copies.store(gated_gain, gg_out)
    for o in range(4):
        rows = rows_at(o if last else lax.rem(place + o, 4))
        part = dot_nt(gated_gain[core, rows, :], own_w[:, OUT])
        part = part + dot_nt(gated_gain[1 - core, rows, :], other_w[:, OUT])
        if last:
            mixed[rows, :] = part.astype(BF)
        else:
            outs[o][:, :D] = part.astype(BF)
    if last:
        copies.store(mixed, mixed_out)
    copies.finish()


def in_hbm(shapes):
    return [pltpu.HBM(k.shape, k.dtype) for k in shapes]


def forward_call(where, chunks, own_w, other_w, taps, taps_state, heads, gain, cot=None):
    last = cot is not None
    kept = [
        shape(SEQ, D, dtype=BF),
        shape(2, SEQ, CHANNELS),
        shape(SEQ, 384),
        shape(SEQ, CHANNELS),
        shape(BLOCKS, STATES, CHANNELS, dtype=BF),
        shape(2, SEQ, HALF, dtype=BF),
    ]
    out_shape, out_specs = in_hbm(kept), [HBM] * 6
    if not last:
        out_shape += [shape(BLOCK, SENT, dtype=BF)] * 4
        out_specs += [VMEM] * 4
    scratch = [pltpu.VMEM((D, WIDE), BF)] * 2 + [pltpu.VMEM(k.shape, k.dtype) for k in kept]
    scratch += [
        pltpu.VMEM((PAD + SEQ, CHANNELS), F32),
        pltpu.VMEM((PAD + SEQ, 2 * STATES), F32),
        pltpu.VMEM((SEQ, CHANNELS), F32),
        pltpu.VMEM((SEQ, 2 * STATES), F32),
        pltpu.VMEM((STATES, CHANNELS), F32),
        pltpu.SemaphoreType.DMA((16,)),
    ]
    if last:
        more = [shape(2, SEQ, HALF), shape(SEQ, D, dtype=BF)]
        out_shape += in_hbm(more[:1]) + [shape(8, SEQ)] + in_hbm(more[1:])
        out_specs += [HBM, VMEM, HBM]
        scratch += [pltpu.VMEM(k.shape, k.dtype) for k in more]

    def kernel(*refs):
        forward_kernel(last, *refs)

    return pl.pallas_call(
        kernel,
        out_shape=out_shape,
        in_specs=[SMEM] + [VMEM] * len(chunks) + [ANY] * 2 + [VMEM] * (5 if last else 4),
        out_specs=out_specs,
        scratch_shapes=scratch,
        compiler_params=limit(VMEM_LIMIT),
        cost_estimate=cost(20 * 10**9, 24 * 10**6),
        name="layer_forward",
    )(where, *chunks, own_w, other_w, taps, taps_state, heads, gain, *([cot] if last else []))


def theirs_tiles(core, normed, rows_held, d_other, gated_gain, dss, out):
    def tile(i, carry):
        rows = pl.ds(pl.multiple_of(i * 256, 256), 256)
        out[rows, IN] = dot_tn(normed[:, rows], d_other[...]).astype(BF)
        out[rows, OUT] = dot_tn(rows_held[:, rows], gated_gain[1 - core]).astype(BF)
        out[rows, STATE] = dot_tn(normed[:, rows], dss[:, lanes_at(1 - core)]).astype(BF)
        return carry

    lax.fori_loop(0, D // 256, tile, 0)


def scaled_rows(rows_grad, factor):
    return (rows_grad.astype(F32) * factor).astype(BF)


def backward_kernel(last, *refs):
    refs = list(refs)

    def take(n):
        taken, refs[:n] = refs[:n], []
        return taken

    (where_ref,) = take(1)
    normed_in, zx_in, ss_in, y_in, starts_in, own_in, other_in = take(7)
    taps_ref, taps_state_ref, heads_ref, gain_ref = take(4)
    if last:
        dscaled_in, cot = take(2)
        stat_parts = take(4)
    else:
        chunks = take(4)
    (gated_gain_in,) = take(1)
    d_own, dss = take(2)
    outs = take(4)
    grad_taps, grad_taps_state, grad_heads, grad_gain = take(4)
    theirs, rows_grad = take(2)
    own_w, other_w, normed, zx, ss, y_all, starts, dscaled = take(8)
    x_pad, state_pad, x_conv, state_conv, du_pad, dstate_pad = take(6)
    d_hidden, d_inner, factors, sems, gated_gain = take(5)
    copies = Copies(sems)
    place, core = where_ref[0], where_ref[1]
    if not last:
        load_out = [
            copies.start(own_in.at[:, OUT], own_w.at[:, OUT]),
            copies.start(other_in.at[:, OUT], other_w.at[:, OUT]),
        ]
    load_x = copies.start(zx_in.at[1], zx.at[1])
    load_rows = [
        copies.start(ss_in, ss),
        copies.start(zx_in.at[0], zx.at[0]),
        copies.start(y_in, y_all),
        copies.start(starts_in, starts),
    ]
    if last:
        load_rows.append(copies.start(dscaled_in, dscaled))
    load_late = [
        copies.start(own_in.at[:, IN], own_w.at[:, IN]),
        copies.start(other_in.at[:, IN], other_w.at[:, IN]),
        copies.start(own_in.at[:, REST], own_w.at[:, REST]),
        copies.start(other_in.at[:, REST], other_w.at[:, REST]),
        copies.start(normed_in, normed),
    ]
    load_late.append(copies.start(gated_gain_in, gated_gain))
    du_pad[SEQ:, :] = jnp.zeros((PAD, CHANNELS), F32)
    dstate_pad[SEQ:, :] = jnp.zeros((PAD, 2 * STATES), F32)
    for ref in (d_hidden, grad_taps, grad_taps_state, grad_heads, grad_gain):
        ref[...] = jnp.zeros_like(ref)
    if last:
        total = stat_parts[0][...] + stat_parts[1][...] + stat_parts[2][...] + stat_parts[3][...]
        factor = lax.rsqrt(total[0:1, :] / DI + EPS)
        cubed = factor * factor * factor / DI * total[1:2, :]
        row = iota((128, SEQ), 0)
        both = jnp.where(row == 0, factor, jnp.where(row == 1, cubed, 0.0))
        for b in range(BLOCKS):
            part = slice(b * BLOCK, (b + 1) * BLOCK)
            factors[part, :] = jnp.transpose(both[:, part])
        for k in range(BLOCKS):
            rows = slice(k * BLOCK, (k + 1) * BLOCK)
            rows_grad[rows, :] = scaled_rows(cot[k, 1], factors[rows, 0:1])
    else:
        for offset, chunk in zip((0, 3, 1, 2), chunks):
            rows = rows_at(lax.rem(place + offset, 4))
            rows_grad[rows, :] = chunk[:, :D]
            tail = chunk[:, D:].astype(F32)
            factor = tail[:, 0:1] + tail[:, 1:2]
            cross = tail[:, 2:3] + tail[:, 3:4]
            lane = iota((BLOCK, 128), 1)
            cubed = factor * factor * factor / DI * cross
            factors[rows, :] = jnp.where(lane == 0, factor, jnp.where(lane == 1, cubed, 0.0))
        for load in load_out:
            load.wait()
        dscaled[core] = dot_nn(rows_grad[...], own_w[:, OUT])
        dscaled[1 - core] = dot_nn(rows_grad[...], other_w[:, OUT])
    load_x.wait()
    x_pad[:PAD, :] = jnp.zeros((PAD, CHANNELS), F32)
    x_pad[PAD:, :] = zx[1]
    load_rows[0].wait()
    state_pad[:PAD, :] = jnp.zeros((PAD, 2 * STATES), F32)
    state_pad[PAD:, :] = ss[:, : 2 * STATES]
    conv_rows(x_pad, taps_ref, x_conv)
    conv_rows(state_pad, taps_state_ref, state_conv)
    for load in load_rows[1:]:
        load.wait()

    def block(turn, carry):
        b = BLOCKS - 1 - turn
        rows = rows_at(b)
        state_u = state_conv[rows, :]
        state_s = sigmoid(state_u)
        state = state_u * state_s
        keys, reads = state[:, :STATES].astype(BF), state[:, STATES:].astype(BF)
        reads_t = jnp.transpose(state[:, STATES:]).astype(BF)
        raised, step, log_decay, summed, summed_t = step_terms(ss[rows, 2 * STATES :], heads_ref)
        meets_t = dot_nt(keys, reads)
        causal_t = iota((BLOCK, BLOCK), 1) >= iota((BLOCK, BLOCK), 0)
        fac = factors[rows, :][:, 0:1]
        cub = factors[rows, :][:, 1:2]
        d_meets_t = jnp.zeros((BLOCK, BLOCK), F32)
        d_keys = jnp.zeros((BLOCK, STATES), F32)
        d_reads = jnp.zeros((BLOCK, STATES), F32)
        head_sums = jnp.zeros((2 * BLOCK, 128), F32)
        last_row = iota((BLOCK, 128), 0) == BLOCK - 1
        for p in range(PAIRS):
            cols = slice(p * 128, (p + 1) * 128)
            half, part = p // 3, slice((p % 3) * 128, (p % 3 + 1) * 128)
            u = x_conv[rows, cols]
            us = sigmoid(u)
            x = u * us
            step_wide = spread(step, 2 * p)
            summed_wide = spread(summed, 2 * p)
            grown = jnp.exp(summed_wide)
            end = grown[BLOCK - 1 : BLOCK, :]
            to_end = jnp.exp(summed_wide[BLOCK - 1 : BLOCK, :] - summed_wide)
            skip = taps_ref[6:7, cols]
            gain = taps_ref[5:6, cols]
            z = zx[0, rows, cols]
            zs = sigmoid(z)
            z_act = z * zs
            y = y_all[rows, cols]
            gated = y * z_act
            incoming = dscaled[half, rows, part]
            lifted = gated * fac
            grad_taps[5:6, cols] += jnp.sum(incoming * lifted, axis=0, keepdims=True)
            d_gated = fac * (gain * incoming) - gated * cub
            dy = d_gated * z_act
            d_inner[0, rows, cols] = (d_gated * y * (zs + z_act * (1.0 - zs))).astype(BF)
            dy_low = dy.astype(BF)
            weighted = x * step_wide
            weighted_low = weighted.astype(BF)
            dy_grown = (dy * grown).astype(BF)
            held_low = starts[b, :, cols]
            dh = d_hidden[:, cols]
            dh_low = dh.astype(BF)
            d_reads = d_reads + dot_nt(dy_grown, held_low)
            kept = dot_nn(keys, dh_low) * to_end
            d_keys = d_keys + dot_nt((to_end * weighted).astype(BF), dh_low)
            decays = []
            for h in (2 * p, 2 * p + 1):
                gaps = summed_t[h : h + 1, :] - summed[:, h : h + 1]
                decays.append(jnp.exp(jnp.where(causal_t, gaps, NEG)))
            mixes = jnp.concatenate([(d * meets_t).astype(BF) for d in decays], axis=1)
            d_weighted = dot_nn(mixes, side_by_side(dy).astype(BF)) + kept
            d_mixes = dot_nt(side_by_side(weighted).astype(BF), dy_low)
            d_meets_t = d_meets_t + d_mixes[:BLOCK] * decays[0] + d_mixes[BLOCK:] * decays[1]
            dx = skip * dy + d_weighted * step_wide
            weighted_f = weighted_low.astype(F32)
            moved = dy_low.astype(F32) * (y - skip * x) - weighted_f * d_weighted
            extra = jnp.sum(weighted_f * kept, axis=0, keepdims=True) + end * jnp.sum(
                dh * held_low.astype(F32), axis=0, keepdims=True
            )
            moved = jnp.where(last_row, moved + extra, moved)
            upper, lower = two_parts(jnp.concatenate([moved, x * d_weighted], axis=0))
            picks = (
                iota((256, 128), 1) == 2 * p + (iota((256, 128), 0) % 128) // HEAD_DIM
            ).astype(BF)
            head_sums = head_sums + dot_nn(jnp.concatenate([upper, lower], axis=1), picks)
            grad_taps[6:7, cols] += jnp.sum(dy * x, axis=0, keepdims=True)
            du_pad[rows, cols] = dx * (us + x * (1.0 - us))
            d_hidden[:, cols] = end * dh + dot_nn(reads_t, dy_grown)
        d_reads = d_reads + dot_nn(jnp.transpose(d_meets_t).astype(BF), keys)
        d_keys = d_keys + dot_nn(d_meets_t.astype(BF), reads)
        d_state = jnp.concatenate([d_keys, d_reads], axis=1)
        d_state = d_state * (state_s + state * (1.0 - state_s))
        dstate_pad[rows, :] = d_state
        upper_tri = (iota((BLOCK, BLOCK), 1) >= iota((BLOCK, BLOCK), 0)).astype(F32)
        d_decay = dot_high(upper_tri, head_sums[:BLOCK])
        d_step = head_sums[BLOCK:] - d_decay * jnp.exp(heads_ref[1:2, :])
        d_raw = d_step * sigmoid(raised)
        dss[rows, 2 * STATES :] = d_raw.astype(BF)
        grad_heads[0:1, :] += jnp.sum(d_raw, axis=0, keepdims=True)
        grad_heads[1:2, :] += jnp.sum(d_decay * log_decay, axis=0, keepdims=True)
        return carry

    lax.fori_loop(0, BLOCKS, block, 0)

    def store_inner(start, cols, value):
        d_inner[1, start : start + BLOCK, cols] = value

    def store_state(start, cols, value):
        dss[start : start + BLOCK, cols] = value

    conv_back(du_pad, x_pad, taps_ref, grad_taps, store_inner)
    conv_back(dstate_pad, state_pad, taps_state_ref, grad_taps_state, store_state)
    for load in load_late:
        load.wait()
    picks = (iota((CHANNELS, 128), 1) == iota((CHANNELS, 128), 0) // HEAD_DIM).astype(F32)
    grad_heads[2:3, :] = dot_high(grad_taps[...], picks)[6:7, :]
    for o, out in enumerate(outs):
        rows = rows_at(lax.rem(place + o, 4))
        part = (
            dot_nt(d_inner[core, rows, :], own_w[:, IN])
            + dot_nt(d_inner[1 - core, rows, :], other_w[:, IN])
            + dot_nt(dss[rows, lanes_at(core)], own_w[:, STATE])
            + dot_nt(dss[rows, lanes_at(1 - core)], other_w[:, STATE])
            + dot_nt(dss[rows, 2 * STATES :], own_w[:, MISC])
        )
        grad_gain[...] += jnp.sum(part * normed[rows, :].astype(F32), axis=0, keepdims=True)
        out[...] = part.astype(BF)
    grad_gain[...] = grad_gain[...] / gain_ref[...]
    d_own[...] = d_inner[core]
    if not last:
        rows_grad[...] = scaled_rows(rows_grad[...], factors[:, 0:1])
    theirs_tiles(core, normed, rows_grad, d_inner.at[1 - core], gated_gain, dss, theirs)


def backward_call(where, kept, own_w, other_w, taps, taps_state, heads, gain, last, extra):
    args = [where, *kept, own_w, other_w, taps, taps_state, heads, gain, *extra]
    in_specs = [SMEM] + [HBM] * 5 + [ANY] * 2 + [VMEM] * 4
    in_specs += [HBM] + [VMEM] * 5 + [HBM] if last else [VMEM] * 4 + [HBM]
    out_shape = [shape(SEQ, CHANNELS, dtype=BF), shape(SEQ, 384, dtype=BF)]
    out_shape += [shape(BLOCK, D, dtype=BF)] * 4
    out_shape += [shape(8, CHANNELS), shape(8, 2 * STATES), shape(8, 128), shape(1, D)]
    out_shape += [shape(D, MISC.start, dtype=BF), shape(SEQ, D, dtype=BF)]
    scratch = [pltpu.VMEM((D, WIDE), BF)] * 2 + [pltpu.VMEM(k.shape, k.dtype) for k in kept]
    scratch += [
        pltpu.VMEM((2, SEQ, HALF), F32),
        pltpu.VMEM((PAD + SEQ, CHANNELS), F32),
        pltpu.VMEM((PAD + SEQ, 2 * STATES), F32),
        pltpu.VMEM((SEQ, CHANNELS), F32),
        pltpu.VMEM((SEQ, 2 * STATES), F32),
        pltpu.VMEM((PAD + SEQ, CHANNELS), F32),
        pltpu.VMEM((PAD + SEQ, 2 * STATES), F32),
        pltpu.VMEM((STATES, CHANNELS), F32),
        pltpu.VMEM((2, SEQ, CHANNELS), BF),
        pltpu.VMEM((SEQ, 128), F32),
        pltpu.SemaphoreType.DMA((20,)),
        pltpu.VMEM((2, SEQ, HALF), BF),
    ]

    def kernel(*refs):
        backward_kernel(last, *refs)

    return pl.pallas_call(
        kernel,
        out_shape=out_shape,
        in_specs=in_specs,
        out_specs=[VMEM] * len(out_shape),
        scratch_shapes=scratch,
        compiler_params=limit(VMEM_LIMIT),
        cost_estimate=cost(32 * 10**9, 30 * 10**6),
        name="layer_backward",
    )(*args)


def arrived(parts):
    return sum((part[...].astype(F32) for part in parts[1:]), parts[0][...].astype(F32))


def after_first_kernel(rows_ref, a, b, c, d, hidden, mixed, factor_out):
    total = arrived((a, b, c, d))
    mixed[...] = total[:, :D]
    square = total[:, D : D + 1] + total[:, D + 1 : D + 2]
    factor = lax.rsqrt(square / DI + EPS)
    factor_out[...] = jnp.broadcast_to(factor, (BLOCK, 128))
    hidden[...] = (rows_ref[...].astype(F32) + factor * total[:, :D]).astype(BF)


def after_first_call(rows, parts):
    return pl.pallas_call(
        after_first_kernel,
        out_shape=[shape(BLOCK, D, dtype=BF), shape(BLOCK, D), shape(BLOCK, 128)],
        in_specs=[VMEM] * 5,
        out_specs=[VMEM] * 3,
        name="between_layers",
    )(rows, *parts)


def after_last_kernel(where_ref, rows_ref, mixed, a, b, c, d, result):
    total = a[...] + b[...] + c[...] + d[...]
    factor = lax.rsqrt(total[0:1, :] / DI + EPS)
    row = iota((128, SEQ), 0)
    column = jnp.zeros((BLOCK, 128), F32)
    for k in range(4):
        part = slice(k * BLOCK, (k + 1) * BLOCK)
        turned = jnp.transpose(jnp.where(row[:, part] == 0, factor[:, part], 0.0))
        column = jnp.where(where_ref[0] == k, turned, column)
    result[...] = rows_ref[...].astype(F32) + column[:, 0:1] * mixed[...].astype(F32)


def after_last_call(where, rows, mixed, stat_parts):
    return pl.pallas_call(
        after_last_kernel,
        out_shape=shape(BLOCK, D),
        in_specs=[SMEM] + [VMEM] * 6,
        out_specs=VMEM,
        name="last_rows",
    )(where, rows, mixed, *stat_parts)


def rows_back(rows_ref, parts, gain_ref, grad_ref):
    incoming = arrived(parts)
    v = rows_ref[...].astype(F32)
    q = lax.rsqrt(jnp.mean(v * v, axis=1, keepdims=True) + EPS)
    weighted = incoming * gain_ref[...]
    inner = jnp.sum(weighted * v, axis=1, keepdims=True)
    return grad_ref[...].astype(F32) + q * weighted - v * (q * q * q / D * inner)


def back_last_kernel(rows_ref, a, b, c, d, gain_ref, grad_ref, mixed_ref, factor_ref, out):
    low = rows_back(rows_ref, (a, b, c, d), gain_ref, grad_ref).astype(BF)
    out[:, :D] = low
    cross = jnp.sum(low.astype(F32) * mixed_ref[...], axis=1, keepdims=True)
    factor = factor_ref[:, 0:1]
    pieces = [*two_parts(factor), *two_parts(cross)]
    lane = iota((BLOCK, 128), 1)
    tail = jnp.zeros((BLOCK, 128), F32)
    for k, piece in enumerate(pieces):
        tail = jnp.where(lane == k, piece.astype(F32), tail)
    out[:, D:] = tail.astype(BF)


def back_last_call(rows, parts, gain, grad, mixed, factor):
    return pl.pallas_call(
        back_last_kernel,
        out_shape=shape(BLOCK, SENT, dtype=BF),
        in_specs=[VMEM] * 9,
        out_specs=VMEM,
        name="between_layers_back",
    )(rows, *parts, gain, grad, mixed, factor)


def back_first_kernel(rows_ref, a, b, c, d, gain_ref, grad_ref, out):
    out[...] = rows_back(rows_ref, (a, b, c, d), gain_ref, grad_ref[:, :D])


def back_first_call(rows, parts, gain, grad):
    return pl.pallas_call(
        back_first_kernel,
        out_shape=shape(BLOCK, D),
        in_specs=[VMEM] * 7,
        out_specs=VMEM,
        name="first_rows_back",
    )(rows, *parts, gain, grad)


def over_96(v):
    return lax.shift_right_logical(v * 683, 16)


def select_lines(half):
    row, channel = iota((384, CHANNELS), 0), iota((384, CHANNELS), 1)
    group = over_96(row)
    return (channel == group * 96 + row + 96 * half).astype(BF)


def select_state(rows, first):
    row, channel = iota((rows, 256), 0) + first, iota((rows, 256), 1)
    group = over_96(row)
    inside = row - 96 * group
    return ((inside < 16) & (channel == 16 * group + inside)).astype(BF)


def small_params(place, misc, heads_ref, taps, taps_state, gain):
    lines = misc[pl.ds(pl.multiple_of(place * 384, 128), 384), :]
    first = dot_tn(lines, select_lines(0))
    second = dot_tn(lines, select_lines(1))
    picks = (iota((128, CHANNELS), 0) == iota((128, CHANNELS), 1) // HEAD_DIM).astype(BF)
    skip = dot_nn(heads_ref[...].astype(BF), picks)
    taps[0:6, :] = first[12:18, :] + second[18:24, :]
    taps[6:7, :] = skip[2:3, :]
    taps[7:8, :] = jnp.zeros((1, CHANNELS), F32)
    taps_state[...] = jnp.zeros((8, 256), F32)
    taps_state[0:5, :] = dot_tn(misc[...], select_state(D, 0))[25:30, :]
    gain[...] = jnp.transpose(misc[...].astype(F32))[24:25, :]


SMALL = (shape(8, CHANNELS), shape(8, 256), shape(1, D))


def params_kernel(where_ref, misc, heads_ref, taps, taps_state, gain):
    small_params(where_ref[0], misc, heads_ref, taps, taps_state, gain)


def params_call(where, misc, heads):
    return pl.pallas_call(
        params_kernel,
        out_shape=SMALL,
        in_specs=[SMEM, VMEM, VMEM],
        out_specs=[VMEM] * 3,
        compiler_params=limit(16),
        name="small_parameters",
    )(where, misc, heads)


def ordered_kernel(where_ref, *refs):
    row, col = where_ref[2], where_ref[3]
    heads_ref, full, taps, taps_state, gain, misc = refs[10:]
    left, right = slice(0, SPLIT), slice(SPLIT, WIDE)
    for side in range(2):
        own, after_own, far_left, far_right, before_own = refs[5 * side : 5 * side + 5]
        for q, o in [(q, o) for q in range(4) for o in range(4)]:
            piece = slice(o * 48, (o + 1) * 48)
            if side == 0:
                at = lax.rem(row + o, 4) * 4 + lax.rem(col + q, 4)
            else:
                at = lax.rem(row + q, 4) * 4 + lax.rem(col + o, 4)
            spot = pl.ds(pl.multiple_of(at * 96 + 48 * side, 16), 48)
            if q == 2:
                full[spot, left] = far_left[piece, :]
                full[spot, right] = far_right[piece, :]
            else:
                full[spot, :] = {0: own, 1: after_own, 3: before_own}[q][piece, :]
    misc[...] = full[:, MISC]
    small_params(where_ref[0], misc, heads_ref, taps, taps_state, gain)


def ordered_call(where, first, second, heads):
    return pl.pallas_call(
        ordered_kernel,
        out_shape=[pltpu.HBM((D, WIDE), BF), *SMALL],
        in_specs=[SMEM] + [VMEM] * 11,
        out_specs=[VMEM] * 4,
        scratch_shapes=[pltpu.VMEM((D, 128), BF)],
        compiler_params=limit(20),
        name="weights_in_order",
    )(where, *first, *second, heads)


def misc_parts(grad_taps, grad_taps_state, grad_heads):
    taps_low = grad_taps[...].astype(BF)
    lane, rank = iota((128, 8), 0), iota((128, 8), 1)
    lines = jnp.zeros((384, 128), F32)
    for half in range(2):
        put = ((lane == 12 + 6 * half + rank) & (rank < 6)).astype(BF)
        lines = lines + dot_nt(select_lines(half), dot_nn(put, taps_low).astype(BF))
    put = ((lane == 25 + rank) & (rank < 5)).astype(BF)
    state_lines = dot_nn(put, grad_taps_state[...].astype(BF)).astype(BF)
    put = ((lane == 30 + rank) & (rank < 3)).astype(BF)
    head_lines = dot_nn(put, grad_heads[...].astype(BF)).astype(BF)
    r, h = iota((384, 128), 0), iota((384, 128), 1)
    head_rows = ((r - 96 * over_96(r) == h) & (h < HEADS)).astype(BF)
    return lines, state_lines, dot_nt(head_rows, head_lines)


def misc_tile(i, rows, place, normed, dss, parts, grad_gain):
    lines, state_lines, head_part = parts
    misc = dot_tn(normed[:, rows], dss[:, 2 * STATES :]) + head_part
    misc = misc + dot_nt(select_state(384, i * 384), state_lines)
    misc = misc + jnp.where(i == place, lines, 0.0)
    gain = jnp.where(iota((128, 384), 0) == 24, grad_gain[:, rows], 0.0)
    return misc + jnp.transpose(gain)


def mine_kernel(relative, where_ref, *refs):
    normed, rows_held, d_own, gated_gain, dss, given = refs[:6]
    grad_taps, grad_taps_state, grad_heads, grad_gain = refs[6:10]
    outs = refs[10:]
    place, core, row, col = where_ref[0], where_ref[1], where_ref[2], where_ref[3]
    parts = misc_parts(grad_taps, grad_taps_state, grad_heads)
    if relative:
        outs, first, second = outs[:8], outs[8], outs[9]
    for i in range(4):
        rows = slice(i * 384, (i + 1) * 384)
        values = (
            (IN, dot_tn(normed[:, rows], d_own[...]) + given[rows, IN].astype(F32)),
            (OUT, dot_tn(rows_held[:, rows], gated_gain[core]) + given[rows, OUT].astype(F32)),
            (
                STATE,
                dot_tn(normed[:, rows], dss[:, lanes_at(core)]) + given[rows, STATE].astype(F32),
            ),
            (MISC, misc_tile(i, rows, place, normed, dss, parts, grad_gain)),
        )
        for cols, value in values:
            low = value.astype(BF)
            if not relative:
                outs[0][rows, cols] = low
                continue
            o = lax.rem(i - row + 4, 4)
            for j in range(4):
                q = lax.rem(j - col + 4, 4)
                spot = pl.ds(pl.multiple_of(q * 48, 16), 48)
                first[o, spot, cols] = low[j * 96 : j * 96 + 48]
                spot = pl.ds(pl.multiple_of(o * 48, 16), 48)
                second[q, spot, cols] = low[j * 96 + 48 : j * 96 + 96]
    if relative:
        for o in range(4):
            outs[o][...] = first[o]
            outs[4 + o][...] = second[o]


def mine_call(where, normed, gated_gain, back, relative):
    d_own, dss, small, theirs, rows_held = back[0], back[1], back[6:10], back[10], back[11]
    out_shape, scratch = [shape(D, WIDE, dtype=BF)], []
    if relative:
        out_shape = [shape(192, WIDE, dtype=BF)] * 8
        scratch = [pltpu.VMEM((4, 192, WIDE), BF)] * 2

    def kernel(*refs):
        mine_kernel(relative, *refs)

    return pl.pallas_call(
        kernel,
        out_shape=out_shape,
        in_specs=[SMEM] + [VMEM] * 10,
        out_specs=[VMEM] * len(out_shape),
        scratch_shapes=scratch,
        compiler_params=limit(28),
        cost_estimate=cost(10**6, 10**4),
        name="weight_grads_kept",
    )(where, normed, rows_held, d_own, gated_gain, dss, swap(theirs), *small)


LEFT, RIGHT = slice(0, SPLIT), slice(SPLIT, WIDE)


def passed_kernel(*refs):
    for side in range(2):
        ahead, behind, left, right = refs[4 * side : 4 * side + 4]
        out_ahead, out_behind = refs[8 + 2 * side : 10 + 2 * side]
        out_ahead[:, LEFT] = (ahead[:, LEFT].astype(F32) + left[...].astype(F32)).astype(BF)
        out_ahead[:, RIGHT] = ahead[:, RIGHT]
        out_behind[:, LEFT] = behind[:, LEFT]
        out_behind[:, RIGHT] = (behind[:, RIGHT].astype(F32) + right[...].astype(F32)).astype(BF)


def passed_call(rows, parts):
    return pl.pallas_call(
        passed_kernel,
        out_shape=[shape(rows, WIDE, dtype=BF)] * 4,
        in_specs=[VMEM] * 8,
        out_specs=[VMEM] * 4,
        compiler_params=limit(16),
        name="grads_passed_on",
    )(*parts)


def halfway_kernel(*refs):
    for side in range(2):
        total = arrived(refs[3 * side : 3 * side + 3]).astype(BF)
        for q in range(4):
            refs[6 + 4 * side + q][...] = total[q * 48 : (q + 1) * 48]


def halfway_call(first, second):
    return pl.pallas_call(
        halfway_kernel,
        out_shape=[shape(48, WIDE, dtype=BF)] * 8,
        in_specs=[VMEM] * 6,
        out_specs=[VMEM] * 8,
        compiler_params=limit(20),
        name="grads_halfway",
    )(*first, *second)


def shard_kernel(where_ref, *refs):
    share_1, own, given = refs[6:]
    share_0 = jnp.concatenate([arrived(refs[:3]), arrived(refs[3:6])], axis=0)
    is_first = where_ref[1] == 0
    other = share_1[...].astype(F32)
    own[...] = jnp.where(is_first, share_0, other)
    given[...] = jnp.where(is_first, other, share_0).astype(BF)


def shard_call(where, first, second, share_1):
    return pl.pallas_call(
        shard_kernel,
        out_shape=[shape(96, WIDE), shape(96, WIDE, dtype=BF)],
        in_specs=[SMEM] + [VMEM] * 7,
        out_specs=[VMEM] * 2,
        name="grads_shard",
    )(where, *first, *second, share_1)


def swap(v):
    return lax.ppermute(v, "section", [(0, 1), (1, 0)])


def turn(v, by, axis="tensor"):
    return lax.ppermute(v, axis, [(i, (i + by) % 4) for i in range(4)])


def spread_rows(v):
    return (v, turn(v, 1), turn(v, -1), turn(v, 2))


def meet(parts, axis="tensor"):
    own, ahead, across, behind = parts
    return (own, turn(ahead, 1, axis), turn(behind, -1, axis), turn(across, 2, axis))


def from_ring(v, axis):
    return (v, turn(v, -1, axis), turn(v, 2, axis), turn(v, 1, axis))


def from_rings(pairs):
    near = [(turn(v, -1, axis), turn(v, 1, axis)) for v, axis in pairs]
    near = lax.optimization_barrier(tuple(near))
    return [
        (
            v,
            ahead,
            turn(ahead[:, :SPLIT], -1, axis),
            turn(behind[:, SPLIT:], 1, axis),
            behind,
        )
        for (v, axis), (ahead, behind) in zip(pairs, near)
    ]


def stacked(pieces):
    own, ahead, far_left, far_right, behind = pieces
    far = jnp.concatenate([far_left, far_right], axis=1)
    return jnp.concatenate([own, ahead, far, behind], axis=0)


def pick(v, index, axis):
    return lax.dynamic_index_in_dim(v, index, axis, keepdims=False)


def after(values, earlier):
    return lax.optimization_barrier((values, earlier))[0]


def toward_rings(rows, pairs):
    far = [(turn(p[2][:, LEFT], 1, a), turn(p[2][:, RIGHT], -1, a)) for p, a in pairs]
    given = [v for (p, _), (left, right) in zip(pairs, far) for v in (p[1], p[3], left, right)]
    sent = passed_call(rows, given)
    return [
        (p[0], turn(sent[2 * k], 1, a), turn(sent[2 * k + 1], -1, a))
        for k, (p, a) in enumerate(pairs)
    ]


def gather_by_turns(where, shard, heads):
    first, second = from_rings([(shard[:48], "dp_0"), (shard[48:], "dp_1")])
    first, second = lax.optimization_barrier((stacked(first), stacked(second)))
    first, second = from_rings([(first, "dp_1"), (second, "dp_0")])
    return ordered_call(where, first, second, heads)


def shards(
    section_ends,
    norm_gain,
    proj_inner,
    proj_step,
    proj_state,
    conv_inner,
    conv_state,
    gate_gain,
    head_params,
    proj_output,
):
    core = lax.axis_index("section")
    place = lax.axis_index("tensor")
    is_first = core == 0
    where = jnp.stack(
        [place, core, lax.axis_index("dp_0"), lax.axis_index("dp_1")]
    ).astype(jnp.int32)

    inner = proj_inner[0]
    out_t = proj_output[0].T.reshape(96, 2, HALF)
    packed = jnp.concatenate(
        [
            proj_state[0].reshape(-1),
            norm_gain[0],
            conv_inner[0].reshape(-1),
            gate_gain[0],
            conv_state[0].reshape(-1),
            jnp.zeros((32 * 256 - 6144 - 332,), BF),
        ]
    ).reshape(32, 256)
    around = jnp.stack(from_ring(packed, "tensor") * 2)
    filled = lax.dynamic_slice_in_dim(around, lax.rem(4 - place, 4), 4, 0).reshape(4, 32 * 256)
    state_rows = filled[:, :6144].reshape(96, 2, 128)
    norm_col = filled[:, 6144:6168].reshape(96, 1)
    inner_cols = filled[:, 6168:6408].reshape(4, 5, 48).transpose(0, 2, 1).reshape(192, 5)
    gate_col = filled[:, 6408:6456].reshape(192, 1)
    both = jnp.concatenate([inner_cols, gate_col], axis=1)
    both = both.reshape(2, 96, 6).transpose(1, 0, 2).reshape(96, 12)
    state_cols = filled[:, 6456:6476].reshape(4, 5, 4).transpose(0, 2, 1).reshape(16, 5)
    state_cols = jnp.pad(state_cols, ((0, 80), (0, 0)))
    misc = jnp.concatenate(
        [proj_step[0], both, norm_col, state_cols, jnp.zeros((96, 128 - 30), BF)], axis=1
    )

    def half_of(index):
        return jnp.concatenate(
            [pick(inner, index, 1), pick(out_t, index, 1), pick(state_rows, index, 1), misc],
            axis=1,
        )

    keep = half_of(core)
    got = swap(half_of(1 - core))
    shard_0, shard_1 = jnp.where(is_first, keep, got), jnp.where(is_first, got, keep)

    ends = section_ends[0]
    got_rows = swap(pick(ends, 1 - core, 0))
    rows_in = jnp.where(is_first, ends[0], got_rows)
    cot = jnp.where(is_first, got_rows, ends[1])
    heads_own = head_params[0].astype(F32)
    heads_got = swap(head_params[0]).astype(F32)
    heads = [
        jnp.pad(jnp.where(core == layer, heads_own, heads_got), ((0, 5), (0, 128 - HEADS)))
        for layer in range(2)
    ]
    ends_all = lax.all_gather(jnp.stack([rows_in, cot]), "tensor", axis=0)
    own_0, taps_0, taps_state_0, gain_0 = gather_by_turns(where, shard_0, heads[0])
    full_1 = lax.all_gather(after(shard_1, own_0), DP, axis=0, tiled=True)
    other_0 = swap(own_0)
    weights_0 = (own_0, other_0, taps_0, taps_state_0, heads[0], gain_0)
    kept_0 = forward_call(where, (ends_all,), *weights_0)
    met_0 = meet(kept_0[6:10])
    own_1 = after(full_1, met_0)
    other_1 = swap(own_1)
    taps_1, taps_state_1, gain_1 = params_call(where, own_1[:, MISC], heads[1])
    weights_1 = (own_1, other_1, taps_1, taps_state_1, heads[1], gain_1)
    hidden, mixed_0, factor_0 = after_first_call(rows_in, met_0)
    kept_1 = forward_call(where, spread_rows(hidden), *weights_1, ends_all)
    dscaled_1, stats, mixed_1 = kept_1[6:]
    stat_parts = spread_rows(stats)
    met_1 = lax.psum_scatter(mixed_1, "tensor", scatter_dimension=0, tiled=True)
    back_1 = backward_call(
        where, kept_1[:5], *weights_1, True, (dscaled_1, ends_all, *stat_parts, kept_1[5])
    )
    payload_1 = mine_call(where, kept_1[0], kept_1[5], back_1, False)[0]
    d_met_1 = after(meet(back_1[2:6]), payload_1)
    grad_1 = back_last_call(hidden, d_met_1, gain_1, cot, mixed_0, factor_0)
    chunks_0 = spread_rows(grad_1)
    share_1 = lax.psum_scatter(after(payload_1, grad_1), DP, scatter_dimension=0, tiled=True)
    result = after_last_call(where, hidden, after(met_1, grad_1), stat_parts)
    chunks_0 = after(chunks_0, result)
    back_0 = backward_call(where, kept_0[:5], *weights_0, False, (*chunks_0, kept_0[5]))
    parts_0 = mine_call(where, kept_0[0], kept_0[5], back_0, True)
    first_met, second_met = toward_rings(
        192, [(parts_0[:4], "dp_0"), (parts_0[4:], "dp_1")]
    )
    pieces = halfway_call(first_met, second_met)
    first_met, second_met = toward_rings(48, [(pieces[:4], "dp_1"), (pieces[4:], "dp_0")])
    share_own, share_given = shard_call(where, first_met, second_met, share_1)
    d_met_0 = after(meet(back_0[2:6]), parts_0[0])
    grad_0 = back_first_call(rows_in, d_met_0, gain_0, grad_1)

    share_got = swap(share_given).astype(F32)
    halves_in = jnp.stack([share_own[:, IN], share_got[:, IN]], axis=1)
    grad_inner = jnp.where(is_first, halves_in, halves_in[:, ::-1])

    def joined(cols):
        own, other = share_own[:, cols], share_got[:, cols]
        return jnp.concatenate(
            [jnp.where(is_first, own, other), jnp.where(is_first, other, own)], axis=1
        )

    grad_output = joined(OUT).T
    misc = (share_own + share_got)[:, MISC]
    grad_step = misc[:, :HEADS]
    grad_heads = misc[:HEADS, 30:33].T
    to_send = jnp.concatenate(
        [
            joined(STATE).reshape(4, 6144),
            misc[:, 24].reshape(4, 24),
            misc[:, 12:24].reshape(96, 2, 6).transpose(1, 0, 2).reshape(4, 48 * 6),
            misc[:16, 25:30].reshape(4, 20),
            jnp.zeros((4, 32 * 256 - 6144 - 332), F32),
        ],
        axis=1,
    ).reshape(4, 32, 256)
    pieces = [pick(to_send, lax.rem(place + o, 4), 0) for o in range(4)]
    met = meet(pieces)
    total = (met[0] + met[1] + met[2] + met[3]).reshape(-1)
    grad_state = total[:6144].reshape(24, 256)
    grad_norm = total[6144:6168]
    inner_lines = total[6168:6456].reshape(48, 6).T
    grad_conv_inner = inner_lines[:5]
    grad_gate = inner_lines[5]
    grad_conv_state = total[6456:6476].reshape(4, 5).T
    rows_got = swap(jnp.where(is_first, result, grad_0))
    section_rows = jnp.where(
        is_first, jnp.stack([grad_0, rows_got]), jnp.stack([rows_got, result])
    )
    return (
        section_rows[None],
        grad_norm[None],
        grad_inner[None],
        grad_step[None],
        grad_state[None],
        grad_conv_inner[None],
        grad_conv_state[None],
        grad_gate[None],
        grad_heads[None],
        grad_output[None],
    )


def solution(mesh):
    split = Mesh(
        mesh.devices.reshape(mesh.shape["section"], 4, 4, mesh.shape["tensor"]),
        ("section", "dp_0", "dp_1", "tensor"),
    )
    return jax.shard_map(
        shards,
        mesh=split,
        in_specs=(
            P("section", None, DP_TENSOR, None),
            P("section", DP_TENSOR),
            P("section", DP, None, "tensor"),
            P("section", DP, "tensor"),
            P("section", DP_TENSOR, None),
            P("section", None, DP_TENSOR),
            P("section", None, DP_TENSOR),
            P("section", DP_TENSOR),
            P("section", None, "tensor"),
            P("section", "tensor", DP),
        ),
        out_specs=(
            P("section", None, DP_TENSOR, None),
            P("section", DP_TENSOR),
            P("section", DP, None, "tensor"),
            P("section", DP, "tensor"),
            P("section", DP_TENSOR, None),
            P("section", None, DP_TENSOR),
            P("section", None, DP_TENSOR),
            P("section", DP_TENSOR),
            P("section", None, "tensor"),
            P("section", "tensor", DP),
        ),
        check_vma=False,
    )
```

```python
import jax
import jax.numpy as jnp
from jax import lax
from jax.experimental import pallas as pl
from jax.experimental.pallas import tpu as pltpu
from jax.sharding import Mesh
from jax.sharding import PartitionSpec as P

D = 1536
SEQ = 512
BLOCK = 128
BLOCKS = SEQ // BLOCK
STATES = 128
CHANNELS = 768
HEADS = 12
HEAD_DIM = 64
PAIRS = HEADS // 2
DI = 3072
PAD = 8
EPS = 1e-05
NEG = -1e30
DP = ("dp_0", "dp_1")
DP_TENSOR = ("dp_0", "dp_1", "tensor")
SENT = D + 128
BF = jnp.bfloat16
F32 = jnp.float32
HIGH = lax.Precision.HIGHEST
VMEM = pl.BlockSpec(memory_space=pltpu.VMEM)
SMEM = pl.BlockSpec(memory_space=pltpu.SMEM)
HBM = pl.BlockSpec(memory_space=pltpu.HBM)
ANY = pl.BlockSpec(memory_space=pl.ANY)
SIDE = D // 2
WIDE = 2 * CHANNELS + CHANNELS + 384
IN = slice(0, 2 * CHANNELS)
OUT = slice(2 * CHANNELS, 3 * CHANNELS)
SS = slice(3 * CHANNELS, WIDE)
STATE = slice(3 * CHANNELS, 3 * CHANNELS + 256)
MISC = slice(3 * CHANNELS + 256, WIDE)
SPLIT = 1408
PART = 256
LEFT, RIGHT = slice(0, SPLIT), slice(SPLIT, WIDE)
VMEM_LIMIT = 54


def shape(*dims, dtype=F32):
    return jax.ShapeDtypeStruct(dims, dtype)


def limit(megabytes):
    return pltpu.CompilerParams(vmem_limit_bytes=megabytes * 1024 * 1024)


def cost(flops, read):
    return pl.CostEstimate(flops=flops, bytes_accessed=read, transcendentals=0)


def dot_nn(left, right):
    return lax.dot_general(left, right, (((1,), (0,)), ((), ())), preferred_element_type=F32)


def dot_nt(left, right):
    return lax.dot_general(left, right, (((1,), (1,)), ((), ())), preferred_element_type=F32)


def dot_tn(left, right):
    return lax.dot_general(left, right, (((0,), (0,)), ((), ())), preferred_element_type=F32)


def dot_high(left, right):
    return lax.dot_general(
        left, right, (((1,), (0,)), ((), ())), precision=HIGH, preferred_element_type=F32
    )


def sigmoid(v):
    return 1.0 / (1.0 + jnp.exp(-v))


def softplus(v):
    return jnp.maximum(v, 0.0) + jnp.log1p(jnp.exp(-jnp.abs(v)))


def rows_at(index):
    return pl.ds(pl.multiple_of(index * BLOCK, BLOCK), BLOCK)


def lanes_at(index):
    return pl.ds(pl.multiple_of(index * 128, 128), 128)


def iota(shape, dim):
    return lax.broadcasted_iota(jnp.int32, shape, dim)


def two_parts(v):
    upper = v.astype(BF)
    lower = (v - upper.astype(F32)).astype(BF)
    return upper, lower


def lane_tiles(width):
    return [slice(at, at + 128) for at in range(0, width, 128)]


def conv_rows(padded, taps, out):
    for cols in lane_tiles(out.shape[1]):
        for start in range(0, SEQ, BLOCK):
            total = taps[4:5, cols] + taps[0:1, cols] * padded[start + 5 : start + 5 + BLOCK, cols]
            for k in range(1, 4):
                at = start + 5 + k
                total = total + taps[k : k + 1, cols] * padded[at : at + BLOCK, cols]
            out[start : start + BLOCK, cols] = total


def conv_back(padded_grad, padded, taps, grad_taps, store):
    for cols in lane_tiles(padded.shape[1]):
        sums = [jnp.zeros((1, 128), F32)] * 5
        for start in range(0, SEQ, BLOCK):
            own = padded_grad[start : start + BLOCK, cols]
            total = taps[3:4, cols] * own
            sums[4] = sums[4] + jnp.sum(own, axis=0, keepdims=True)
            for k in range(4):
                at = start + 5 + k
                sums[k] = sums[k] + jnp.sum(own * padded[at : at + BLOCK, cols], axis=0, keepdims=True)
                if k < 3:
                    at = start + 3 - k
                    total = total + taps[k : k + 1, cols] * padded_grad[at : at + BLOCK, cols]
            store(start, cols, total.astype(BF))
        for k in range(5):
            grad_taps[k : k + 1, cols] = sums[k]


def step_terms(raw, heads):
    valid = iota((BLOCK, 128), 1) < HEADS
    raised = jnp.where(valid, raw + heads[0:1, :], -30.0)
    step = softplus(raised)
    log_decay = -step * jnp.exp(heads[1:2, :])
    lower = (iota((BLOCK, BLOCK), 0) >= iota((BLOCK, BLOCK), 1)).astype(F32)
    summed = dot_high(lower, log_decay)
    return raised, step, log_decay, summed, jnp.transpose(summed)


def spread(values, head):
    first = iota((BLOCK, 128), 1) < HEAD_DIM
    return jnp.where(first, values[:, head : head + 1], values[:, head + 1 : head + 2])


def side_by_side(v):
    first = iota(v.shape, 1) < HEAD_DIM
    zero = jnp.zeros_like(v)
    return jnp.concatenate([jnp.where(first, v, zero), jnp.where(first, zero, v)], axis=0)


def over_48(v):
    return lax.shift_right_logical(v * 1366, 16)


def select_lines(half):
    row, channel = iota((384, CHANNELS), 0), iota((384, CHANNELS), 1)
    side = (row >= 192).astype(jnp.int32)
    group = over_48(row - 192 * side)
    inside = row - 192 * side - 48 * group
    return (channel == group * 192 + 96 * half + 48 * side + inside).astype(BF)


def select_state():
    row, channel = iota((SIDE, 256), 0), iota((SIDE, 256), 1)
    group = over_48(row)
    inside = row - 48 * group
    return ((inside < 16) & (channel == 16 * group + inside)).astype(BF)


def lines_at(place, side):
    return pl.ds(pl.multiple_of(side * SIDE + place * 192, 64), 192)


def small_params(place, misc, heads_ref, taps, taps_state, gain):
    lines = jnp.concatenate([misc[lines_at(place, side), :] for side in range(2)], axis=0)
    first = dot_tn(lines, select_lines(0))
    second = dot_tn(lines, select_lines(1))
    picks = (iota((128, CHANNELS), 0) == iota((128, CHANNELS), 1) // HEAD_DIM).astype(BF)
    skip = dot_nn(heads_ref[...].astype(BF), picks)
    taps[0:6, :] = first[12:18, :] + second[18:24, :]
    taps[6:7, :] = skip[2:3, :]
    taps[7:8, :] = jnp.zeros((1, CHANNELS), F32)
    taps_state[...] = jnp.zeros((8, 256), F32)
    taps_state[0:5, :] = dot_tn(misc[0:SIDE, :], select_state())[25:30, :]
    gain[...] = jnp.transpose(misc[...].astype(F32))[24:25, :]


SMALL = (shape(8, CHANNELS), shape(8, 256), shape(1, D))


class Copies:
    def __init__(self, sems):
        self.sems = sems
        self.count = 0
        self.pending = []

    def start(self, source, target):
        copy = pltpu.make_async_copy(source, target, self.sems.at[self.count])
        self.count += 1
        copy.start()
        return copy

    def store(self, source, target):
        self.pending.append(self.start(source, target))

    def finish(self):
        for copy in self.pending:
            copy.wait()


def side_rows(core):
    return pl.ds(pl.multiple_of(core * SIDE, SIDE), SIDE)


def place_blocks(copies, where_ref, core, pieces, full):
    row, col = where_ref[2], where_ref[3]
    own, ahead, far_left, far_right, behind = pieces
    started = []
    for o in range(4):
        part = slice(o * 48, (o + 1) * 48)
        for q in range(4):
            along = lax.rem(row + o, 4) * 4 + lax.rem(col + q, 4)
            across = lax.rem(row + q, 4) * 4 + lax.rem(col + o, 4)
            at = along + core * (across - along)
            spot = pl.ds(pl.multiple_of(core * SIDE + at * 48, 16), 48)
            if q == 2:
                started.append(copies.start(far_left.at[part, :], full.at[spot, LEFT]))
                started.append(copies.start(far_right.at[part, :], full.at[spot, RIGHT]))
            else:
                source = {0: own, 1: ahead, 3: behind}[q]
                started.append(copies.start(source.at[part, :], full.at[spot, :]))
    return started


def forward_kernel(last, *refs):
    refs = list(refs)

    def take(n):
        taken, refs[:n] = refs[:n], []
        return taken

    where_ref, ends = take(2)
    if last:
        chunks, (own_in, other_in) = take(4), take(2)
        taps_ref, taps_state_ref, heads_ref, gain_ref = take(4)
    else:
        own_pieces, other_pieces, (heads_ref,) = take(5), take(5), take(1)
    normed_out, zx_out, ss_out, y_out, starts_out, gg_out, whole_out = take(7)
    if last:
        dscaled_out, stats, mixed_out = take(3)
    else:
        outs = take(4)
        taps_ref, taps_state_ref, gain_ref = take(3)
    normed, zx, ss, y_all, starts, gated_gain, whole = take(7)
    x_pad, state_pad, x_conv, state_conv, hidden, sems, held_rows = take(7)
    if last:
        dscaled, mixed = take(2)
    copies = Copies(sems)
    place, core = where_ref[0], where_ref[1]
    sides = (side_rows(core), side_rows(1 - core))
    if last:
        load_in, load_rest = [
            [
                copies.start(part.at[:, cols], whole.at[rows, cols])
                for part, rows in zip((own_in, other_in), sides)
            ]
            for cols in (IN, slice(OUT.start, WIDE))
        ]
    else:
        load_rows = [
            copies.start(ends.at[k, 0], held_rows.at[rows_at(k), :]) for k in range(BLOCKS)
        ]
        load_in = place_blocks(copies, where_ref, core, own_pieces, whole)
        load_in += place_blocks(copies, where_ref, 1 - core, other_pieces, whole)
        for load in load_rows + load_in:
            load.wait()
        copies.store(whole, whole_out)
        small_params(place, whole.at[:, MISC], heads_ref, taps_ref, taps_state_ref, gain_ref)
    for k, offset in enumerate((0, 3, 1, 2)):
        rows = rows_at(lax.rem(place + offset, 4))
        v = (chunks[k][...] if last else held_rows[rows, :]).astype(F32)
        q = lax.rsqrt(jnp.mean(v * v, axis=1, keepdims=True) + EPS)
        normed[rows, :] = (v * q * gain_ref[...]).astype(BF)
    copies.store(normed, normed_out)
    if last:
        load_rows = [
            copies.start(ends.at[k, 1], held_rows.at[rows_at(k), :]) for k in range(BLOCKS)
        ]
        for load in load_in:
            load.wait()
    zx[...] = dot_nn(normed[...], whole[:, IN])
    copies.store(zx, zx_out)
    if last:
        for load in load_rest + load_rows:
            load.wait()
        copies.store(whole, whole_out)
    ss[...] = dot_nn(normed[...], whole[:, SS])
    copies.store(ss, ss_out)
    if last:
        dscaled[...] = dot_nn(held_rows[...], whole[:, OUT])
        copies.store(dscaled, dscaled_out)
    x_pad[:PAD, :] = jnp.zeros((PAD, CHANNELS), F32)
    x_pad[PAD:, :] = zx[:, CHANNELS:]
    state_pad[:PAD, :] = jnp.zeros((PAD, 2 * STATES), F32)
    state_pad[PAD:, :] = ss[:, : 2 * STATES]
    hidden[...] = jnp.zeros_like(hidden)
    conv_rows(x_pad, taps_ref, x_conv)
    conv_rows(state_pad, taps_state_ref, state_conv)

    def block(b, carry):
        rows = rows_at(b)
        state_u = state_conv[rows, :]
        state = state_u * sigmoid(state_u)
        keys, reads = state[:, :STATES].astype(BF), state[:, STATES:].astype(BF)
        keys_t = jnp.transpose(state[:, :STATES]).astype(BF)
        _, step, _, summed, summed_t = step_terms(ss[rows, 2 * STATES :], heads_ref)
        meets = dot_nt(reads, keys)
        causal = iota((BLOCK, BLOCK), 0) >= iota((BLOCK, BLOCK), 1)
        squares = jnp.zeros((BLOCK, 128), F32)
        crosses = jnp.zeros((BLOCK, 128), F32)
        for p in range(PAIRS):
            cols = slice(p * 128, (p + 1) * 128)
            u = x_conv[rows, cols]
            x = u * sigmoid(u)
            weighted = x * spread(step, 2 * p)
            summed_wide = spread(summed, 2 * p)
            grown = jnp.exp(summed_wide)
            to_end = jnp.exp(summed_wide[BLOCK - 1 : BLOCK, :] - summed_wide)
            mixes = []
            for h in (2 * p, 2 * p + 1):
                gaps = summed[:, h : h + 1] - summed_t[h : h + 1, :]
                mixes.append((jnp.exp(jnp.where(causal, gaps, NEG)) * meets).astype(BF))
            within = dot_nn(
                jnp.concatenate(mixes, axis=1), side_by_side(weighted).astype(BF)
            )
            held = hidden[:, cols]
            held_low = held.astype(BF)
            starts[b, :, cols] = held_low
            y = within + grown * dot_nn(reads, held_low) + x * taps_ref[6:7, cols]
            hidden[:, cols] = grown[BLOCK - 1 : BLOCK, :] * held + dot_nn(
                keys_t, (to_end * weighted).astype(BF)
            )
            y_all[rows, cols] = y
            z = zx[rows, cols]
            gated = y * z * sigmoid(z)
            squares = squares + gated * gated
            gained = gated * taps_ref[5:6, cols]
            gated_gain[rows, cols] = gained.astype(BF)
            if last:
                crosses = crosses + gained * dscaled[rows, cols]
        square = jnp.sum(squares, axis=1, keepdims=True)
        upper, lower = two_parts(square)
        lane = iota((BLOCK, 128), 1)
        zero = jnp.zeros((BLOCK, 128), F32)
        tail = jnp.where(
            lane == 0, upper.astype(F32), jnp.where(lane == 1, lower.astype(F32), zero)
        ).astype(BF)
        for o, out in enumerate(() if last else outs):

            @pl.when(b == lax.rem(place + o, 4))
            def _(out=out):
                out[:, D:] = tail

        if last:
            cross = jnp.sum(crosses, axis=1, keepdims=True)
            both = jnp.where(lane == 0, square, jnp.where(lane == 1, cross, zero))
            stats[:, rows] = jnp.transpose(both)[:8, :]
        return carry

    lax.fori_loop(0, BLOCKS, block, 0)
    copies.store(y_all, y_out)
    copies.store(starts, starts_out)
    copies.store(gated_gain, gg_out)
    for at in range(0, D, PART):
        cols = slice(at, at + PART)
        part = dot_nt(gated_gain[...], whole[cols, OUT]).astype(BF)
        target = mixed if last else held_rows
        target[:, cols] = part
    if last:
        copies.store(mixed, mixed_out)
    else:
        for o in range(4):
            outs[o][:, :D] = held_rows[rows_at(lax.rem(place + o, 4)), :]
    copies.finish()


def in_hbm(shapes):
    return [pltpu.HBM(k.shape, k.dtype) for k in shapes]


def forward_call(where, ends, chunks, weights):
    last = len(chunks) > 0
    kept = [
        shape(SEQ, D, dtype=BF),
        shape(SEQ, 2 * CHANNELS),
        shape(SEQ, 384),
        shape(SEQ, CHANNELS),
        shape(BLOCKS, STATES, CHANNELS, dtype=BF),
        shape(SEQ, CHANNELS, dtype=BF),
        shape(D, WIDE, dtype=BF),
    ]
    out_shape, out_specs = in_hbm(kept), [HBM] * 7
    scratch = [pltpu.VMEM(k.shape, k.dtype) for k in kept]
    scratch += [
        pltpu.VMEM((PAD + SEQ, CHANNELS), F32),
        pltpu.VMEM((PAD + SEQ, 2 * STATES), F32),
        pltpu.VMEM((SEQ, CHANNELS), F32),
        pltpu.VMEM((SEQ, 2 * STATES), F32),
        pltpu.VMEM((STATES, CHANNELS), F32),
        pltpu.SemaphoreType.DMA((24 if last else 64,)),
        pltpu.VMEM((SEQ, D), BF),
    ]
    if last:
        args = (where, ends, *chunks, *weights)
        in_specs = [SMEM, ANY] + [VMEM] * 4 + [ANY] * 2 + [VMEM] * 4
        more = [shape(SEQ, CHANNELS), shape(SEQ, D, dtype=BF)]
        out_shape += in_hbm(more[:1]) + [shape(8, SEQ)] + in_hbm(more[1:])
        out_specs += [HBM, VMEM, HBM]
        scratch += [pltpu.VMEM(k.shape, k.dtype) for k in more]
    else:
        args = (where, ends, *weights)
        in_specs = [SMEM, ANY] + [ANY] * 10 + [VMEM]
        out_shape += [shape(BLOCK, SENT, dtype=BF)] * 4 + list(SMALL)
        out_specs += [VMEM] * 7

    def kernel(*refs):
        forward_kernel(last, *refs)

    return pl.pallas_call(
        kernel,
        out_shape=out_shape,
        in_specs=in_specs,
        out_specs=out_specs,
        scratch_shapes=scratch,
        compiler_params=limit(VMEM_LIMIT),
        cost_estimate=cost(20 * 10**9, 24 * 10**6),
        name="layer_forward",
    )(*args)


def scaled_rows(rows_grad, factor):
    return (rows_grad.astype(F32) * factor).astype(BF)


def misc_extra(place, side, grad_small, extra):
    taps_low = grad_small[0:8, 0:CHANNELS].astype(BF)
    lane, rank = iota((128, 8), 0), iota((128, 8), 1)
    lines = jnp.zeros((384, 128), F32)
    for half in range(2):
        put = ((lane == 12 + 6 * half + rank) & (rank < 6)).astype(BF)
        lines = lines + dot_nt(select_lines(half), dot_nn(put, taps_low).astype(BF))
    put = ((lane == 25 + rank) & (rank < 5)).astype(BF)
    state_low = grad_small[0:8, CHANNELS : CHANNELS + 256].astype(BF)
    state_lines = dot_nn(put, state_low).astype(BF)
    put = ((lane == 30 + rank) & (rank < 3)).astype(BF)
    heads_low = grad_small[0:8, CHANNELS + 256 : CHANNELS + 384].astype(BF)
    head_lines = dot_nn(put, heads_low).astype(BF)
    row, head = iota((SIDE, 128), 0), iota((SIDE, 128), 1)
    head_rows = ((row - 48 * over_48(row) == head) & (head < HEADS)).astype(BF)
    first_only = dot_nt(select_state(), state_lines) + dot_nt(head_rows, head_lines)
    gains = grad_small[8:9, pl.ds(pl.multiple_of(side * SIDE, SIDE), SIDE)]
    gain = jnp.transpose(jnp.where(iota((128, SIDE), 0) == 24, gains, 0.0))
    extra[...] = gain + jnp.where(side == 0, first_only, 0.0)
    extra[lines_at(place, 0), :] += jnp.where(side == 0, lines[:192], lines[192:])


def weight_products(side, normed, rows_held, d_inner, gated_gain, dss, extra, out):
    for at in range(0, SIDE, PART):
        rows = slice(at, at + PART)
        lanes = pl.ds(pl.multiple_of(side * SIDE + at, PART), PART)
        out[rows, IN] = dot_tn(normed[:, lanes], d_inner[...]).astype(BF)
        out[rows, OUT] = dot_tn(rows_held[:, lanes], gated_gain[...]).astype(BF)
        shared = dot_tn(normed[:, lanes], dss[...])
        out[rows, STATE] = shared[:, :256].astype(BF)
        out[rows, MISC] = (shared[:, 256:] + extra[rows, :]).astype(BF)


def backward_kernel(last, *refs):
    refs = list(refs)

    def take(n):
        taken, refs[:n] = refs[:n], []
        return taken

    (where_ref,) = take(1)
    normed_in, zx_in, ss_in, y_in, starts_in, gated_gain_in, whole_in = take(7)
    taps_ref, taps_state_ref, heads_ref, gain_ref = take(4)
    if last:
        dscaled_in, cot = take(2)
        stat_parts = take(4)
    else:
        chunks = take(4)
    d_inner_out, dss_out = take(2)
    outs = take(4)
    (grad_small,) = take(1)
    theirs_out, rows_out = take(2)
    normed, zx, ss, y_all, starts, gated_gain, whole, dscaled = take(8)
    x_pad, state_pad, x_conv, state_conv, du_pad, dstate_pad = take(6)
    d_hidden, d_inner, factors, sems = take(4)
    dss, theirs, rows_grad, sent, extra = take(5)
    grad_taps, grad_taps_state = grad_small.at[0:8, 0:CHANNELS], grad_small.at[0:8, 768:1024]
    grad_heads, grad_gain = grad_small.at[0:8, 1024:1152], grad_small.at[8:9, :]
    copies = Copies(sems)
    place, core = where_ref[0], where_ref[1]
    if not last:
        load_out = copies.start(whole_in.at[:, OUT], whole.at[:, OUT])
    load_x = copies.start(zx_in.at[:, CHANNELS:], zx.at[:, CHANNELS:])
    load_ss = copies.start(ss_in, ss)
    if last:
        load_cot = [copies.start(cot.at[k, 1], sent.at[rows_at(k), :]) for k in range(BLOCKS)]
    du_pad[SEQ:, :] = jnp.zeros((PAD, CHANNELS), F32)
    dstate_pad[SEQ:, :] = jnp.zeros((PAD, 2 * STATES), F32)
    for ref in (d_hidden, grad_small):
        ref[...] = jnp.zeros_like(ref)
    if last:
        total = stat_parts[0][...] + stat_parts[1][...] + stat_parts[2][...] + stat_parts[3][...]
        factor = lax.rsqrt(total[0:1, :] / DI + EPS)
        cubed = factor * factor * factor / DI * total[1:2, :]
        row = iota((128, SEQ), 0)
        both = jnp.where(row == 0, factor, jnp.where(row == 1, cubed, 0.0))
        for b in range(BLOCKS):
            part = slice(b * BLOCK, (b + 1) * BLOCK)
            factors[part, :] = jnp.transpose(both[:, part])
        for k in range(BLOCKS):
            rows = slice(k * BLOCK, (k + 1) * BLOCK)
            load_cot[k].wait()
            rows_grad[rows, :] = scaled_rows(sent[rows, :], factors[rows, 0:1])
    else:
        for offset, chunk in zip((0, 3, 1, 2), chunks):
            rows = rows_at(lax.rem(place + offset, 4))
            rows_grad[rows, :] = chunk[:, :D]
            tail = chunk[:, D:].astype(F32)
            factor = tail[:, 0:1] + tail[:, 1:2]
            cross = tail[:, 2:3] + tail[:, 3:4]
            lane = iota((BLOCK, 128), 1)
            cubed = factor * factor * factor / DI * cross
            factors[rows, :] = jnp.where(lane == 0, factor, jnp.where(lane == 1, cubed, 0.0))
        load_out.wait()
        dscaled[...] = dot_nn(rows_grad[...], whole[:, OUT])
        rows_grad[...] = scaled_rows(rows_grad[...], factors[:, 0:1])
    copies.store(rows_grad, rows_out)
    load_x.wait()
    load_rows = [
        copies.start(zx_in.at[:, :CHANNELS], zx.at[:, :CHANNELS]),
        copies.start(y_in, y_all),
        copies.start(starts_in, starts),
    ]
    if last:
        load_rows.append(copies.start(dscaled_in, dscaled))
    x_pad[:PAD, :] = jnp.zeros((PAD, CHANNELS), F32)
    x_pad[PAD:, :] = zx[:, CHANNELS:]
    load_ss.wait()
    state_pad[:PAD, :] = jnp.zeros((PAD, 2 * STATES), F32)
    state_pad[PAD:, :] = ss[:, : 2 * STATES]
    conv_rows(x_pad, taps_ref, x_conv)
    conv_rows(state_pad, taps_state_ref, state_conv)
    for load in load_rows:
        load.wait()
    load_late = [
        copies.start(whole_in.at[:, IN], whole.at[:, IN]),
        copies.start(whole_in.at[:, SS], whole.at[:, SS]),
        copies.start(normed_in, normed),
        copies.start(gated_gain_in, gated_gain),
    ]

    def block(turn, carry):
        b = BLOCKS - 1 - turn
        rows = rows_at(b)
        state_u = state_conv[rows, :]
        state_s = sigmoid(state_u)
        state = state_u * state_s
        keys, reads = state[:, :STATES].astype(BF), state[:, STATES:].astype(BF)
        reads_t = jnp.transpose(state[:, STATES:]).astype(BF)
        raised, step, log_decay, summed, summed_t = step_terms(ss[rows, 2 * STATES :], heads_ref)
        meets_t = dot_nt(keys, reads)
        causal_t = iota((BLOCK, BLOCK), 1) >= iota((BLOCK, BLOCK), 0)
        fac = factors[rows, :][:, 0:1]
        cub = factors[rows, :][:, 1:2]
        d_meets_t = jnp.zeros((BLOCK, BLOCK), F32)
        d_keys = jnp.zeros((BLOCK, STATES), F32)
        d_reads = jnp.zeros((BLOCK, STATES), F32)
        head_sums = jnp.zeros((2 * BLOCK, 128), F32)
        last_row = iota((BLOCK, 128), 0) == BLOCK - 1
        for p in range(PAIRS):
            cols = slice(p * 128, (p + 1) * 128)
            u = x_conv[rows, cols]
            us = sigmoid(u)
            x = u * us
            step_wide = spread(step, 2 * p)
            summed_wide = spread(summed, 2 * p)
            grown = jnp.exp(summed_wide)
            end = grown[BLOCK - 1 : BLOCK, :]
            to_end = jnp.exp(summed_wide[BLOCK - 1 : BLOCK, :] - summed_wide)
            skip = taps_ref[6:7, cols]
            gain = taps_ref[5:6, cols]
            z = zx[rows, cols]
            zs = sigmoid(z)
            z_act = z * zs
            y = y_all[rows, cols]
            gated = y * z_act
            incoming = dscaled[rows, cols]
            lifted = gated * fac
            grad_taps[5:6, cols] += jnp.sum(incoming * lifted, axis=0, keepdims=True)
            d_gated = fac * (gain * incoming) - gated * cub
            dy = d_gated * z_act
            d_inner[rows, cols] = (d_gated * y * (zs + z_act * (1.0 - zs))).astype(BF)
            dy_low = dy.astype(BF)
            weighted = x * step_wide
            weighted_low = weighted.astype(BF)
            dy_grown = (dy * grown).astype(BF)
            held_low = starts[b, :, cols]
            dh = d_hidden[:, cols]
            dh_low = dh.astype(BF)
            d_reads = d_reads + dot_nt(dy_grown, held_low)
            kept = dot_nn(keys, dh_low) * to_end
            d_keys = d_keys + dot_nt((to_end * weighted).astype(BF), dh_low)
            decays = []
            for h in (2 * p, 2 * p + 1):
                gaps = summed_t[h : h + 1, :] - summed[:, h : h + 1]
                decays.append(jnp.exp(jnp.where(causal_t, gaps, NEG)))
            mixes = jnp.concatenate([(d * meets_t).astype(BF) for d in decays], axis=1)
            d_weighted = dot_nn(mixes, side_by_side(dy).astype(BF)) + kept
            d_mixes = dot_nt(side_by_side(weighted).astype(BF), dy_low)
            d_meets_t = d_meets_t + d_mixes[:BLOCK] * decays[0] + d_mixes[BLOCK:] * decays[1]
            dx = skip * dy + d_weighted * step_wide
            weighted_f = weighted_low.astype(F32)
            moved = dy_low.astype(F32) * (y - skip * x) - weighted_f * d_weighted
            extra = jnp.sum(weighted_f * kept, axis=0, keepdims=True) + end * jnp.sum(
                dh * held_low.astype(F32), axis=0, keepdims=True
            )
            moved = jnp.where(last_row, moved + extra, moved)
            upper, lower = two_parts(jnp.concatenate([moved, x * d_weighted], axis=0))
            picks = (
                iota((256, 128), 1) == 2 * p + (iota((256, 128), 0) % 128) // HEAD_DIM
            ).astype(BF)
            head_sums = head_sums + dot_nn(jnp.concatenate([upper, lower], axis=1), picks)
            grad_taps[6:7, cols] += jnp.sum(dy * x, axis=0, keepdims=True)
            du_pad[rows, cols] = dx * (us + x * (1.0 - us))
            d_hidden[:, cols] = end * dh + dot_nn(reads_t, dy_grown)
        d_reads = d_reads + dot_nn(jnp.transpose(d_meets_t).astype(BF), keys)
        d_keys = d_keys + dot_nn(d_meets_t.astype(BF), reads)
        d_state = jnp.concatenate([d_keys, d_reads], axis=1)
        d_state = d_state * (state_s + state * (1.0 - state_s))
        dstate_pad[rows, :] = d_state
        upper_tri = (iota((BLOCK, BLOCK), 1) >= iota((BLOCK, BLOCK), 0)).astype(F32)
        d_decay = dot_high(upper_tri, head_sums[:BLOCK])
        d_step = head_sums[BLOCK:] - d_decay * jnp.exp(heads_ref[1:2, :])
        d_raw = d_step * sigmoid(raised)
        dss[rows, 2 * STATES :] = d_raw.astype(BF)
        grad_heads[0:1, :] += jnp.sum(d_raw, axis=0, keepdims=True)
        grad_heads[1:2, :] += jnp.sum(d_decay * log_decay, axis=0, keepdims=True)
        return carry

    lax.fori_loop(0, BLOCKS, block, 0)

    def store_inner(start, cols, value):
        cols = slice(CHANNELS + cols.start, CHANNELS + cols.stop)
        d_inner[start : start + BLOCK, cols] = value

    def store_state(start, cols, value):
        dss[start : start + BLOCK, cols] = value

    conv_back(du_pad, x_pad, taps_ref, grad_taps, store_inner)
    conv_back(dstate_pad, state_pad, taps_state_ref, grad_taps_state, store_state)
    copies.store(d_inner, d_inner_out)
    copies.store(dss, dss_out)
    picks = (iota((CHANNELS, 128), 1) == iota((CHANNELS, 128), 0) // HEAD_DIM).astype(F32)
    grad_heads[2:3, :] = dot_high(grad_taps[...], picks)[6:7, :]
    for load in load_late:
        load.wait()
    for at in range(0, D, PART):
        cols = slice(at, at + PART)
        part = dot_nt(d_inner[...], whole[cols, IN]) + dot_nt(dss[...], whole[cols, SS])
        total = jnp.sum(part * normed[:, cols].astype(F32), axis=0, keepdims=True)
        grad_gain[:, cols] = total / gain_ref[:, cols]
        sent[:, cols] = part.astype(BF)
    for o, out in enumerate(outs):
        copies.store(sent.at[rows_at(lax.rem(place + o, 4)), :], out)
    misc_extra(place, 1 - core, grad_small, extra)
    weight_products(1 - core, normed, rows_grad, d_inner, gated_gain, dss, extra, theirs)
    copies.store(theirs, theirs_out)
    copies.finish()


def backward_call(where, kept, taps, taps_state, heads, gain, last, extra):
    args = [where, *kept, taps, taps_state, heads, gain, *extra]
    in_specs = [SMEM] + [HBM] * 7 + [VMEM] * 4
    in_specs += [HBM, ANY] + [VMEM] * 4 if last else [VMEM] * 4
    out_shape = [
        pltpu.HBM((SEQ, 2 * CHANNELS), BF),
        pltpu.HBM((SEQ, 384), BF),
        *[pltpu.HBM((BLOCK, D), BF)] * 4,
        shape(16, D),
        pltpu.HBM((SIDE, WIDE), BF),
        pltpu.HBM((SEQ, D), BF),
    ]
    out_specs = [HBM] * 6 + [VMEM] + [HBM] * 2
    scratch = [pltpu.VMEM(k.shape, k.dtype) for k in kept]
    scratch += [
        pltpu.VMEM((SEQ, CHANNELS), F32),
        pltpu.VMEM((PAD + SEQ, CHANNELS), F32),
        pltpu.VMEM((PAD + SEQ, 2 * STATES), F32),
        pltpu.VMEM((SEQ, CHANNELS), F32),
        pltpu.VMEM((SEQ, 2 * STATES), F32),
        pltpu.VMEM((PAD + SEQ, CHANNELS), F32),
        pltpu.VMEM((PAD + SEQ, 2 * STATES), F32),
        pltpu.VMEM((STATES, CHANNELS), F32),
        pltpu.VMEM((SEQ, 2 * CHANNELS), BF),
        pltpu.VMEM((SEQ, 128), F32),
        pltpu.SemaphoreType.DMA((40,)),
        pltpu.VMEM((SEQ, 384), BF),
        pltpu.VMEM((SIDE, WIDE), BF),
        pltpu.VMEM((SEQ, D), BF),
        pltpu.VMEM((SEQ, D), BF),
        pltpu.VMEM((SIDE, 128), F32),
    ]

    def kernel(*refs):
        backward_kernel(last, *refs)

    return pl.pallas_call(
        kernel,
        out_shape=out_shape,
        in_specs=in_specs,
        out_specs=out_specs,
        scratch_shapes=scratch,
        compiler_params=limit(VMEM_LIMIT),
        cost_estimate=cost(32 * 10**9, 30 * 10**6),
        name="layer_backward",
    )(*args)


def arrived(parts):
    return sum((part[...].astype(F32) for part in parts[1:]), parts[0][...].astype(F32))


def after_first_kernel(rows_ref, a, b, c, d, hidden, mixed, factor_out):
    total = arrived((a, b, c, d))
    mixed[...] = total[:, :D]
    square = total[:, D : D + 1] + total[:, D + 1 : D + 2]
    factor = lax.rsqrt(square / DI + EPS)
    factor_out[...] = jnp.broadcast_to(factor, (BLOCK, 128))
    hidden[...] = (rows_ref[...].astype(F32) + factor * total[:, :D]).astype(BF)


def after_first_call(rows, parts):
    return pl.pallas_call(
        after_first_kernel,
        out_shape=[shape(BLOCK, D, dtype=BF), shape(BLOCK, D), shape(BLOCK, 128)],
        in_specs=[VMEM] * 5,
        out_specs=[VMEM] * 3,
        name="between_layers",
    )(rows, *parts)


def after_last_kernel(where_ref, rows_ref, mixed, a, b, c, d, result):
    total = a[...] + b[...] + c[...] + d[...]
    factor = lax.rsqrt(total[0:1, :] / DI + EPS)
    row = iota((128, SEQ), 0)
    column = jnp.zeros((BLOCK, 128), F32)
    for k in range(4):
        part = slice(k * BLOCK, (k + 1) * BLOCK)
        turned = jnp.transpose(jnp.where(row[:, part] == 0, factor[:, part], 0.0))
        column = jnp.where(where_ref[0] == k, turned, column)
    result[...] = rows_ref[...].astype(F32) + column[:, 0:1] * mixed[...].astype(F32)


def after_last_call(where, rows, mixed, stat_parts):
    return pl.pallas_call(
        after_last_kernel,
        out_shape=shape(BLOCK, D),
        in_specs=[SMEM] + [VMEM] * 6,
        out_specs=VMEM,
        name="last_rows",
    )(where, rows, mixed, *stat_parts)


def rows_back(rows_ref, parts, gain_ref, grad_ref):
    incoming = arrived(parts)
    v = rows_ref[...].astype(F32)
    q = lax.rsqrt(jnp.mean(v * v, axis=1, keepdims=True) + EPS)
    weighted = incoming * gain_ref[...]
    inner = jnp.sum(weighted * v, axis=1, keepdims=True)
    return grad_ref[...].astype(F32) + q * weighted - v * (q * q * q / D * inner)


def back_last_kernel(rows_ref, a, b, c, d, gain_ref, grad_ref, mixed_ref, factor_ref, out):
    low = rows_back(rows_ref, (a, b, c, d), gain_ref, grad_ref).astype(BF)
    out[:, :D] = low
    cross = jnp.sum(low.astype(F32) * mixed_ref[...], axis=1, keepdims=True)
    factor = factor_ref[:, 0:1]
    pieces = [*two_parts(factor), *two_parts(cross)]
    lane = iota((BLOCK, 128), 1)
    tail = jnp.zeros((BLOCK, 128), F32)
    for k, piece in enumerate(pieces):
        tail = jnp.where(lane == k, piece.astype(F32), tail)
    out[:, D:] = tail.astype(BF)


def back_last_call(rows, parts, gain, grad, mixed, factor):
    return pl.pallas_call(
        back_last_kernel,
        out_shape=shape(BLOCK, SENT, dtype=BF),
        in_specs=[VMEM] * 9,
        out_specs=VMEM,
        name="between_layers_back",
    )(rows, *parts, gain, grad, mixed, factor)


def back_first_kernel(rows_ref, a, b, c, d, gain_ref, grad_ref, out):
    out[...] = rows_back(rows_ref, (a, b, c, d), gain_ref, grad_ref[:, :D])


def back_first_call(rows, parts, gain, grad):
    return pl.pallas_call(
        back_first_kernel,
        out_shape=shape(BLOCK, D),
        in_specs=[VMEM] * 7,
        out_specs=VMEM,
        name="first_rows_back",
    )(rows, *parts, gain, grad)


def params_kernel(where_ref, misc, heads_ref, taps, taps_state, gain):
    small_params(where_ref[0], misc, heads_ref, taps, taps_state, gain)


def params_call(where, misc, heads):
    return pl.pallas_call(
        params_kernel,
        out_shape=SMALL,
        in_specs=[SMEM, VMEM, VMEM],
        out_specs=[VMEM] * 3,
        compiler_params=limit(16),
        name="small_parameters",
    )(where, misc, heads)


def mine_kernel(where_ref, normed, rows_held, d_inner, gated_gain, dss, grad_small, out, extra):
    side = where_ref[1]
    misc_extra(where_ref[0], side, grad_small, extra)
    weight_products(side, normed, rows_held, d_inner, gated_gain, dss, extra, out)


def mine_call(where, normed, gated_gain, back):
    return pl.pallas_call(
        mine_kernel,
        out_shape=shape(SIDE, WIDE, dtype=BF),
        in_specs=[SMEM] + [VMEM] * 6,
        out_specs=VMEM,
        scratch_shapes=[pltpu.VMEM((SIDE, 128), F32)],
        compiler_params=limit(24),
        cost_estimate=cost(10**6, 10**4),
        name="weight_grads_kept",
    )(where, normed, back[8], back[0], gated_gain, back[1], back[6])


def both_kernel(where_ref, mine, given, *outs):
    if len(outs) == 1:
        outs[0][...] = (mine[...].astype(F32) + given[...].astype(F32)).astype(BF)
        return
    core, row, col = where_ref[1], where_ref[2], where_ref[3]
    own, ahead, far_left, far_right, behind, parts = outs
    for i in range(4):
        for j in range(4):
            rows = slice((4 * i + j) * 48, (4 * i + j + 1) * 48)
            total = (mine[rows, :].astype(F32) + given[rows, :].astype(F32)).astype(BF)
            along, across = lax.rem(i - row + 4, 4), lax.rem(j - col + 4, 4)
            o = along + core * (across - along)
            q = across + core * (along - across)
            parts[o, pl.ds(pl.multiple_of(q * 48, 16), 48), :] = total
    own[...] = parts[0]
    ahead[...] = parts[1]
    far_left[...] = parts[2, :, LEFT]
    far_right[...] = parts[2, :, RIGHT]
    behind[...] = parts[3]


def ring_shapes(rows):
    whole = shape(rows, WIDE, dtype=BF)
    left, right = shape(rows, SPLIT, dtype=BF), shape(rows, WIDE - SPLIT, dtype=BF)
    return [whole, whole, left, right, whole]


def both_call(where, mine, given, relative):
    out_shape = ring_shapes(192) if relative else [shape(SIDE, WIDE, dtype=BF)]
    return pl.pallas_call(
        both_kernel,
        out_shape=out_shape,
        in_specs=[SMEM] + [VMEM] * 2,
        out_specs=[VMEM] * len(out_shape),
        scratch_shapes=[pltpu.VMEM((4, 192, WIDE), BF)] if relative else [],
        compiler_params=limit(28),
        cost_estimate=cost(10**6, 10**4),
        name="both_cores_grads",
    )(where, mine, given)


def passed_kernel(ahead, behind, left, right, out_ahead, out_behind):
    out_ahead[:, LEFT] = (ahead[:, LEFT].astype(F32) + left[...].astype(F32)).astype(BF)
    out_ahead[:, RIGHT] = ahead[:, RIGHT]
    out_behind[:, LEFT] = behind[:, LEFT]
    out_behind[:, RIGHT] = (behind[:, RIGHT].astype(F32) + right[...].astype(F32)).astype(BF)


def passed_call(ahead, behind, left, right):
    return pl.pallas_call(
        passed_kernel,
        out_shape=[shape(*ahead.shape, dtype=BF)] * 2,
        in_specs=[VMEM] * 4,
        out_specs=[VMEM] * 2,
        compiler_params=limit(16),
        cost_estimate=cost(10**6, 10**4),
        name="grads_passed_on",
    )(ahead, behind, left, right)


def halfway_kernel(a, b, c, own, ahead, far_left, far_right, behind):
    total = arrived((a, b, c)).astype(BF)
    own[...] = total[:48]
    ahead[...] = total[48:96]
    far_left[...] = total[96:144, LEFT]
    far_right[...] = total[96:144, RIGHT]
    behind[...] = total[144:]


def halfway_call(parts):
    return pl.pallas_call(
        halfway_kernel,
        out_shape=ring_shapes(48),
        in_specs=[VMEM] * 3,
        out_specs=[VMEM] * 5,
        compiler_params=limit(20),
        name="grads_halfway",
    )(*parts)


def shard_kernel(where_ref, a, b, c, share_1, own, given):
    share_0 = arrived((a, b, c))
    is_first = where_ref[1] == 0
    other = share_1[...].astype(F32)
    own[...] = jnp.where(is_first, share_0, other)
    given[...] = jnp.where(is_first, other, share_0).astype(BF)


def shard_call(where, parts, share_1):
    return pl.pallas_call(
        shard_kernel,
        out_shape=[shape(48, WIDE), shape(48, WIDE, dtype=BF)],
        in_specs=[SMEM] + [VMEM] * 4,
        out_specs=[VMEM] * 2,
        name="grads_shard",
    )(where, *parts, share_1)


def swap(v):
    return lax.ppermute(v, "section", [(0, 1), (1, 0)])


def turn(v, by, axis="tensor"):
    return lax.ppermute(v, axis, [(i, (i + by) % 4) for i in range(4)])


def spread_rows(v):
    return (v, turn(v, 1), turn(v, -1), turn(v, 2))


def meet(parts, axis="tensor"):
    own, ahead, across, behind = parts
    return (own, turn(ahead, 1, axis), turn(behind, -1, axis), turn(across, 2, axis))


def from_ring(v, axis):
    return (v, turn(v, -1, axis), turn(v, 2, axis), turn(v, 1, axis))


def ring(v, by, phase):
    pairs = []
    for s in range(2):
        for a in range(4):
            for b in range(4):
                to = ((a + by) % 4, b) if s == phase else (a, (b + by) % 4)
                pairs.append((16 * s + 4 * a + b, 16 * s + 4 * to[0] + to[1]))
    return lax.ppermute(v, ("section", *DP), pairs)


def around(v, phase):
    ahead, behind = lax.optimization_barrier((ring(v, -1, phase), ring(v, 1, phase)))
    return (
        v,
        ahead,
        ring(ahead[:, LEFT], -1, phase),
        ring(behind[:, RIGHT], 1, phase),
        behind,
    )


def toward(parts, phase):
    own, ahead, far_left, far_right, behind = parts
    left, right = ring(far_left, 1, phase), ring(far_right, -1, phase)
    ahead, behind = passed_call(ahead, behind, left, right)
    return own, ring(ahead, 1, phase), ring(behind, -1, phase)


def gather_by_turns(shard):
    own, ahead, far_left, far_right, behind = around(shard, 0)
    far = jnp.concatenate([far_left, far_right], axis=1)
    return around(jnp.concatenate([own, ahead, far, behind], axis=0), 1)


def inner_order(v):
    return v.reshape(-1, 16, 2, 48).transpose(0, 2, 1, 3).reshape(v.shape)


def outer_order(v):
    return v.reshape(-1, 2, 16, 48).transpose(0, 2, 1, 3).reshape(v.shape)


def pick(v, index, axis):
    return lax.dynamic_index_in_dim(v, index, axis, keepdims=False)


def after(values, earlier):
    return lax.optimization_barrier((values, earlier))[0]


def shards(
    section_ends,
    norm_gain,
    proj_inner,
    proj_step,
    proj_state,
    conv_inner,
    conv_state,
    gate_gain,
    head_params,
    proj_output,
):
    core = lax.axis_index("section")
    place = lax.axis_index("tensor")
    is_first = core == 0
    where = jnp.stack(
        [place, core, lax.axis_index("dp_0"), lax.axis_index("dp_1")]
    ).astype(jnp.int32)

    packed = jnp.concatenate(
        [
            proj_state[0].reshape(-1),
            norm_gain[0],
            conv_inner[0].reshape(-1),
            gate_gain[0],
            conv_state[0].reshape(-1),
            jnp.zeros((32 * 256 - 6144 - 332,), BF),
        ]
    ).reshape(32, 256)
    turned = jnp.stack(from_ring(packed, "tensor") * 2)
    filled = lax.dynamic_slice_in_dim(turned, lax.rem(4 - place, 4), 4, 0).reshape(4, 32 * 256)
    state_rows = filled[:, :6144].reshape(96, 256)
    norm_col = filled[:, 6144:6168].reshape(96, 1)
    inner_cols = filled[:, 6168:6408].reshape(4, 5, 48).transpose(0, 2, 1).reshape(192, 5)
    gate_col = filled[:, 6408:6456].reshape(192, 1)
    both = jnp.concatenate([inner_cols, gate_col], axis=1)
    both = both.reshape(2, 96, 6).transpose(1, 0, 2).reshape(96, 12)
    state_cols = filled[:, 6456:6476].reshape(4, 5, 4).transpose(0, 2, 1).reshape(16, 5)
    state_cols = jnp.pad(state_cols, ((0, 80), (0, 0)))
    misc = jnp.concatenate(
        [proj_step[0], both, norm_col, state_cols, jnp.zeros((96, 128 - 30), BF)], axis=1
    )

    shard = jnp.concatenate(
        [proj_inner[0].reshape(96, 2 * CHANNELS), proj_output[0].T, state_rows, misc], axis=1
    ).reshape(2, 48, WIDE)
    keep, got = pick(shard, core, 0), swap(pick(shard, 1 - core, 0))
    shard_0, shard_1 = jnp.where(is_first, keep, got), jnp.where(is_first, got, keep)

    ends = section_ends[0]
    got_rows = swap(pick(ends, 1 - core, 0))
    rows_in = jnp.where(is_first, ends[0], got_rows)
    cot = jnp.where(is_first, got_rows, ends[1])
    heads_own = head_params[0].astype(F32)
    heads_got = swap(head_params[0]).astype(F32)
    heads = [
        jnp.pad(jnp.where(core == layer, heads_own, heads_got), ((0, 5), (0, 128 - HEADS)))
        for layer in range(2)
    ]
    both_ends = inner_order(jnp.stack([rows_in, cot]))
    rows_in, cot = both_ends[0], both_ends[1]
    ends_all = lax.all_gather(both_ends, "tensor", axis=0)
    own_pieces = gather_by_turns(shard_0)
    full_1 = lax.all_gather(
        after(shard_1, tuple(own_pieces[2:4])), DP, axis=0, tiled=True
    )
    other_pieces = [swap(v) for v in own_pieces]
    first = forward_call(where, ends_all, (), (*own_pieces, *other_pieces, heads[0]))
    kept_0, sent_0, small_0 = first[:7], first[7:11], first[11:]
    weights_0 = (small_0[0], small_0[1], heads[0], small_0[2])
    met_0 = meet(sent_0)
    own_1 = after(full_1, met_0)
    other_1 = swap(own_1)
    misc_1 = jnp.where(
        is_first,
        jnp.concatenate([own_1[:, MISC], other_1[:, MISC]], axis=0),
        jnp.concatenate([other_1[:, MISC], own_1[:, MISC]], axis=0),
    )
    small_1 = params_call(where, misc_1, heads[1])
    weights_1 = (small_1[0], small_1[1], heads[1], small_1[2])
    hidden, mixed_0, factor_0 = after_first_call(rows_in, met_0)
    kept_1 = forward_call(
        where, ends_all, spread_rows(hidden), (own_1, other_1, *weights_1)
    )
    dscaled_1, stats, mixed_1 = kept_1[7:]
    stat_parts = spread_rows(stats)
    back_1 = backward_call(
        where, kept_1[:7], *weights_1, True, (dscaled_1, ends_all, *stat_parts)
    )
    met_1 = lax.psum_scatter(mixed_1, "tensor", scatter_dimension=0, tiled=True)
    back_1 = after(tuple(back_1), met_1)
    mine_1 = mine_call(where, kept_1[0], kept_1[5], back_1)
    payload_1 = both_call(where, mine_1, swap(back_1[7]), False)[0]
    d_met_1 = after(meet(back_1[2:6]), payload_1)
    grad_1 = back_last_call(hidden, d_met_1, weights_1[3], cot, mixed_0, factor_0)
    chunks_0 = spread_rows(grad_1)
    share_1 = lax.psum_scatter(after(payload_1, grad_1), DP, scatter_dimension=0, tiled=True)
    result = outer_order(after_last_call(where, hidden, after(met_1, grad_1), stat_parts))
    chunks_0 = after(chunks_0, result)
    back_0 = backward_call(where, kept_0, *weights_0, False, chunks_0)
    mine_0 = mine_call(where, kept_0[0], kept_0[5], back_0)
    parts_0 = both_call(where, mine_0, swap(back_0[7]), True)
    pieces = halfway_call(toward(parts_0, 0))
    half_met = toward(pieces, 1)
    share_own, share_given = shard_call(where, half_met, share_1)
    d_met_0 = after(meet(back_0[2:6]), pieces[0])
    grad_0 = back_first_call(rows_in, d_met_0, weights_0[3], grad_1)

    share_got = swap(share_given).astype(F32)
    whole = jnp.where(
        is_first,
        jnp.concatenate([share_own, share_got], axis=0),
        jnp.concatenate([share_got, share_own], axis=0),
    )
    grad_inner = whole[:, IN].reshape(96, 2, CHANNELS)
    grad_output = whole[:, OUT].T
    misc = whole[:, MISC]
    grad_step = misc[:, :HEADS]
    grad_heads = misc[:HEADS, 30:33].T
    to_send = jnp.concatenate(
        [
            whole[:, STATE].reshape(4, 6144),
            misc[:, 24].reshape(4, 24),
            misc[:, 12:24].reshape(96, 2, 6).transpose(1, 0, 2).reshape(4, 48 * 6),
            misc[:16, 25:30].reshape(4, 20),
            jnp.zeros((4, 32 * 256 - 6144 - 332), F32),
        ],
        axis=1,
    ).reshape(4, 32, 256)
    pieces = [pick(to_send, lax.rem(place + o, 4), 0) for o in range(4)]
    met = meet(pieces)
    total = (met[0] + met[1] + met[2] + met[3]).reshape(-1)
    grad_state = total[:6144].reshape(24, 256)
    grad_norm = total[6144:6168]
    inner_lines = total[6168:6456].reshape(48, 6).T
    grad_conv_inner = inner_lines[:5]
    grad_gate = inner_lines[5]
    grad_conv_state = total[6456:6476].reshape(4, 5).T
    grad_0 = outer_order(grad_0)
    rows_got = swap(jnp.where(is_first, result, grad_0))
    section_rows = jnp.where(
        is_first, jnp.stack([grad_0, rows_got]), jnp.stack([rows_got, result])
    )
    return (
        section_rows[None],
        grad_norm[None],
        grad_inner[None],
        grad_step[None],
        grad_state[None],
        grad_conv_inner[None],
        grad_conv_state[None],
        grad_gate[None],
        grad_heads[None],
        grad_output[None],
    )


def solution(mesh):
    split = Mesh(
        mesh.devices.reshape(mesh.shape["section"], 4, 4, mesh.shape["tensor"]),
        ("section", "dp_0", "dp_1", "tensor"),
    )
    return jax.shard_map(
        shards,
        mesh=split,
        in_specs=(
            P("section", None, DP_TENSOR, None),
            P("section", DP_TENSOR),
            P("section", DP, None, "tensor"),
            P("section", DP, "tensor"),
            P("section", DP_TENSOR, None),
            P("section", None, DP_TENSOR),
            P("section", None, DP_TENSOR),
            P("section", DP_TENSOR),
            P("section", None, "tensor"),
            P("section", "tensor", DP),
        ),
        out_specs=(
            P("section", None, DP_TENSOR, None),
            P("section", DP_TENSOR),
            P("section", DP, None, "tensor"),
            P("section", DP, "tensor"),
            P("section", DP_TENSOR, None),
            P("section", None, DP_TENSOR),
            P("section", None, DP_TENSOR),
            P("section", DP_TENSOR),
            P("section", None, "tensor"),
            P("section", "tensor", DP),
        ),
        check_vma=False,
    )
```

```python
import jax
import jax.numpy as jnp
from jax import lax
from jax.experimental import pallas as pl
from jax.experimental.pallas import tpu as pltpu
from jax.sharding import Mesh
from jax.sharding import PartitionSpec as P

D = 1536
SEQ = 512
BLOCK = 128
BLOCKS = SEQ // BLOCK
STATES = 128
CHANNELS = 768
HEADS = 12
HEAD_DIM = 64
PAIRS = HEADS // 2
DI = 3072
PAD = 8
EPS = 1e-05
NEG = -1e30
DP = ("dp_0", "dp_1")
DP_TENSOR = ("dp_0", "dp_1", "tensor")
SENT = D + 128
BF = jnp.bfloat16
F32 = jnp.float32
HIGH = lax.Precision.HIGHEST
VMEM = pl.BlockSpec(memory_space=pltpu.VMEM)
SMEM = pl.BlockSpec(memory_space=pltpu.SMEM)
HBM = pl.BlockSpec(memory_space=pltpu.HBM)
ANY = pl.BlockSpec(memory_space=pl.ANY)
SIDE = D // 2
WIDE = 2 * CHANNELS + CHANNELS + 384
IN = slice(0, 2 * CHANNELS)
OUT = slice(2 * CHANNELS, 3 * CHANNELS)
SS = slice(3 * CHANNELS, WIDE)
STATE = slice(3 * CHANNELS, 3 * CHANNELS + 256)
MISC = slice(3 * CHANNELS + 256, WIDE)
MAIN = 3 * CHANNELS
SPLIT = 2 * CHANNELS
PART = 256
LEFT, RIGHT = slice(0, SPLIT), slice(SPLIT, WIDE)
VMEM_LIMIT = 54


def shape(*dims, dtype=F32):
    return jax.ShapeDtypeStruct(dims, dtype)


def limit(megabytes):
    return pltpu.CompilerParams(vmem_limit_bytes=megabytes * 1024 * 1024)


def cost(flops, read):
    return pl.CostEstimate(flops=flops, bytes_accessed=read, transcendentals=0)


def dot_nn(left, right):
    return lax.dot_general(left, right, (((1,), (0,)), ((), ())), preferred_element_type=F32)


def dot_nt(left, right):
    return lax.dot_general(left, right, (((1,), (1,)), ((), ())), preferred_element_type=F32)


def dot_tn(left, right):
    return lax.dot_general(left, right, (((0,), (0,)), ((), ())), preferred_element_type=F32)


def dot_high(left, right):
    return lax.dot_general(
        left, right, (((1,), (0,)), ((), ())), precision=HIGH, preferred_element_type=F32
    )


def sigmoid(v):
    return 1.0 / (1.0 + jnp.exp(-v))


def softplus(v):
    return jnp.maximum(v, 0.0) + jnp.log1p(jnp.exp(-jnp.abs(v)))


def rows_at(index):
    return pl.ds(pl.multiple_of(index * BLOCK, BLOCK), BLOCK)


def lanes_at(index):
    return pl.ds(pl.multiple_of(index * 128, 128), 128)


def iota(shape, dim):
    return lax.broadcasted_iota(jnp.int32, shape, dim)


def two_parts(v):
    upper = v.astype(BF)
    lower = (v - upper.astype(F32)).astype(BF)
    return upper, lower


def lane_tiles(width):
    return [slice(at, at + 128) for at in range(0, width, 128)]


def conv_rows(padded, taps, out):
    for cols in lane_tiles(out.shape[1]):
        for start in range(0, SEQ, BLOCK):
            total = taps[4:5, cols] + taps[0:1, cols] * padded[start + 5 : start + 5 + BLOCK, cols]
            for k in range(1, 4):
                at = start + 5 + k
                total = total + taps[k : k + 1, cols] * padded[at : at + BLOCK, cols]
            out[start : start + BLOCK, cols] = total


def conv_back(padded_grad, padded, taps, grad_taps, store):
    for cols in lane_tiles(padded.shape[1]):
        sums = [jnp.zeros((1, 128), F32)] * 5
        for start in range(0, SEQ, BLOCK):
            own = padded_grad[start : start + BLOCK, cols]
            total = taps[3:4, cols] * own
            sums[4] = sums[4] + jnp.sum(own, axis=0, keepdims=True)
            for k in range(4):
                at = start + 5 + k
                sums[k] = sums[k] + jnp.sum(own * padded[at : at + BLOCK, cols], axis=0, keepdims=True)
                if k < 3:
                    at = start + 3 - k
                    total = total + taps[k : k + 1, cols] * padded_grad[at : at + BLOCK, cols]
            store(start, cols, total.astype(BF))
        for k in range(5):
            grad_taps[k : k + 1, cols] = sums[k]


def step_terms(raw, heads):
    valid = iota((BLOCK, 128), 1) < HEADS
    raised = jnp.where(valid, raw + heads[0:1, :], -30.0)
    step = softplus(raised)
    log_decay = -step * jnp.exp(heads[1:2, :])
    lower = (iota((BLOCK, BLOCK), 0) >= iota((BLOCK, BLOCK), 1)).astype(F32)
    summed = dot_high(lower, log_decay)
    return raised, step, log_decay, summed, jnp.transpose(summed)


def spread(values, head):
    first = iota((BLOCK, 128), 1) < HEAD_DIM
    return jnp.where(first, values[:, head : head + 1], values[:, head + 1 : head + 2])


def side_by_side(v):
    first = iota(v.shape, 1) < HEAD_DIM
    zero = jnp.zeros_like(v)
    return jnp.concatenate([jnp.where(first, v, zero), jnp.where(first, zero, v)], axis=0)


def over_96(v):
    return lax.shift_right_logical(v * 683, 16)


def select_lines(half):
    row, channel = iota((384, CHANNELS), 0), iota((384, CHANNELS), 1)
    return (channel == over_96(row) * 96 + row + 96 * half).astype(BF)


def select_state(rows, first):
    row, channel = iota((rows, 256), 0) + first, iota((rows, 256), 1)
    group = over_96(row)
    inside = row - 96 * group
    return ((inside < 16) & (channel == 16 * group + inside)).astype(BF)


def small_params(place, misc, heads_ref, taps, taps_state, gain):
    lines = misc[pl.ds(pl.multiple_of(place * 384, 128), 384), :]
    first = dot_tn(lines, select_lines(0))
    second = dot_tn(lines, select_lines(1))
    picks = (iota((128, CHANNELS), 0) == iota((128, CHANNELS), 1) // HEAD_DIM).astype(BF)
    skip = dot_nn(heads_ref[...].astype(BF), picks)
    taps[0:6, :] = first[12:18, :] + second[18:24, :]
    taps[6:7, :] = skip[2:3, :]
    taps[7:8, :] = jnp.zeros((1, CHANNELS), F32)
    taps_state[...] = jnp.zeros((8, 256), F32)
    taps_state[0:5, :] = dot_tn(misc[...], select_state(D, 0))[25:30, :]
    gain[...] = jnp.transpose(misc[...].astype(F32))[24:25, :]


SMALL = (shape(8, CHANNELS), shape(8, 256), shape(1, D))


class Copies:
    def __init__(self, sems):
        self.sems = sems
        self.count = 0
        self.pending = []

    def start(self, source, target):
        copy = pltpu.make_async_copy(source, target, self.sems.at[self.count])
        self.count += 1
        copy.start()
        return copy

    def store(self, source, target):
        self.pending.append(self.start(source, target))

    def finish(self):
        for copy in self.pending:
            copy.wait()


def place_blocks(copies, where_ref, parts, whole, cols):
    row, col = where_ref[2], where_ref[3]
    started = []
    for k, pieces in enumerate(parts):
        core = where_ref[1] if k == 0 else 1 - where_ref[1]
        if len(pieces) == 1:
            for at in range(16):
                spot = pl.ds(pl.multiple_of(at * 96 + 48 * core, 16), 48)
                source = pieces[0].at[at * 48 : (at + 1) * 48, cols]
                started.append(copies.start(source, whole.at[spot, cols]))
            continue
        own, ahead, far_left, far_right, behind = pieces
        far, shifted = far_left, cols
        if cols.start >= SPLIT:
            far, shifted = far_right, slice(cols.start - SPLIT, cols.stop - SPLIT)
        for o in range(4):
            part = slice(o * 48, (o + 1) * 48)
            for q in range(4):
                along = lax.rem(row + o, 4) * 4 + lax.rem(col + q, 4)
                across = lax.rem(row + q, 4) * 4 + lax.rem(col + o, 4)
                at = along + core * (across - along)
                spot = pl.ds(pl.multiple_of(at * 96 + 48 * core, 16), 48)
                if q == 2:
                    source = far.at[part, shifted]
                else:
                    source = {0: own, 1: ahead, 3: behind}[q].at[part, cols]
                started.append(copies.start(source, whole.at[spot, cols]))
    return started


def forward_kernel(last, *refs):
    refs = list(refs)

    def take(n):
        taken, refs[:n] = refs[:n], []
        return taken

    where_ref, ends = take(2)
    if last:
        chunks, own_in, other_in = take(4), take(1), take(1)
        taps_ref, taps_state_ref, heads_ref, gain_ref = take(4)
    else:
        own_in, other_in, (heads_ref,) = take(5), take(5), take(1)
    normed_out, zx_out, ss_out, y_out, starts_out, gg_out = take(6)
    if last:
        dscaled_out, stats, mixed_out = take(3)
    else:
        outs = take(4)
        taps_ref, taps_state_ref, gain_ref = take(3)
    normed, zx, ss, y_all, starts, gated_gain, whole = take(7)
    x_pad, state_pad, x_conv, state_conv, hidden, sems, held_rows = take(7)
    if last:
        dscaled, mixed = take(2)
    copies = Copies(sems)
    place, core = where_ref[0], where_ref[1]
    weights = (own_in, other_in)
    if not last:
        load_rows = [
            copies.start(ends.at[k, 0], held_rows.at[rows_at(k), :]) for k in range(BLOCKS)
        ]
        load_rest = place_blocks(copies, where_ref, weights, whole, RIGHT)
    load_in = place_blocks(copies, where_ref, weights, whole, LEFT)
    if last:
        load_rest = place_blocks(copies, where_ref, weights, whole, RIGHT)
    else:
        for load in load_rest + load_rows:
            load.wait()
        small_params(place, whole.at[:, MISC], heads_ref, taps_ref, taps_state_ref, gain_ref)
    for k, offset in enumerate((0, 3, 1, 2)):
        rows = rows_at(lax.rem(place + offset, 4))
        v = (chunks[k][...] if last else held_rows[rows, :]).astype(F32)
        q = lax.rsqrt(jnp.mean(v * v, axis=1, keepdims=True) + EPS)
        normed[rows, :] = (v * q * gain_ref[...]).astype(BF)
    copies.store(normed, normed_out)
    if last:
        load_rows = [
            copies.start(ends.at[k, 1], held_rows.at[rows_at(k), :]) for k in range(BLOCKS)
        ]
    for load in load_in:
        load.wait()
    zx[...] = dot_nn(normed[...], whole[:, IN])
    copies.store(zx, zx_out)
    if last:
        for load in load_rest + load_rows:
            load.wait()
    ss[...] = dot_nn(normed[...], whole[:, SS])
    copies.store(ss, ss_out)
    if last:
        dscaled[...] = dot_nn(held_rows[...], whole[:, OUT])
        copies.store(dscaled, dscaled_out)
    x_pad[:PAD, :] = jnp.zeros((PAD, CHANNELS), F32)
    x_pad[PAD:, :] = zx[:, CHANNELS:]
    state_pad[:PAD, :] = jnp.zeros((PAD, 2 * STATES), F32)
    state_pad[PAD:, :] = ss[:, : 2 * STATES]
    hidden[...] = jnp.zeros_like(hidden)
    conv_rows(x_pad, taps_ref, x_conv)
    conv_rows(state_pad, taps_state_ref, state_conv)

    def block(b, carry):
        rows = rows_at(b)
        state_u = state_conv[rows, :]
        state = state_u * sigmoid(state_u)
        keys, reads = state[:, :STATES].astype(BF), state[:, STATES:].astype(BF)
        keys_t = jnp.transpose(state[:, :STATES]).astype(BF)
        _, step, _, summed, summed_t = step_terms(ss[rows, 2 * STATES :], heads_ref)
        meets = dot_nt(reads, keys)
        causal = iota((BLOCK, BLOCK), 0) >= iota((BLOCK, BLOCK), 1)
        squares = jnp.zeros((BLOCK, 128), F32)
        crosses = jnp.zeros((BLOCK, 128), F32)
        for p in range(PAIRS):
            cols = slice(p * 128, (p + 1) * 128)
            u = x_conv[rows, cols]
            x = u * sigmoid(u)
            weighted = x * spread(step, 2 * p)
            summed_wide = spread(summed, 2 * p)
            grown = jnp.exp(summed_wide)
            to_end = jnp.exp(summed_wide[BLOCK - 1 : BLOCK, :] - summed_wide)
            mixes = []
            for h in (2 * p, 2 * p + 1):
                gaps = summed[:, h : h + 1] - summed_t[h : h + 1, :]
                mixes.append((jnp.exp(jnp.where(causal, gaps, NEG)) * meets).astype(BF))
            within = dot_nn(
                jnp.concatenate(mixes, axis=1), side_by_side(weighted).astype(BF)
            )
            held = hidden[:, cols]
            held_low = held.astype(BF)
            starts[b, :, cols] = held_low
            y = within + grown * dot_nn(reads, held_low) + x * taps_ref[6:7, cols]
            hidden[:, cols] = grown[BLOCK - 1 : BLOCK, :] * held + dot_nn(
                keys_t, (to_end * weighted).astype(BF)
            )
            y_all[rows, cols] = y
            z = zx[rows, cols]
            gated = y * z * sigmoid(z)
            squares = squares + gated * gated
            gained = gated * taps_ref[5:6, cols]
            gated_gain[rows, cols] = gained.astype(BF)
            if last:
                crosses = crosses + gained * dscaled[rows, cols]
        square = jnp.sum(squares, axis=1, keepdims=True)
        upper, lower = two_parts(square)
        lane = iota((BLOCK, 128), 1)
        zero = jnp.zeros((BLOCK, 128), F32)
        tail = jnp.where(
            lane == 0, upper.astype(F32), jnp.where(lane == 1, lower.astype(F32), zero)
        ).astype(BF)
        for o, out in enumerate(() if last else outs):

            @pl.when(b == lax.rem(place + o, 4))
            def _(out=out):
                out[:, D:] = tail

        if last:
            cross = jnp.sum(crosses, axis=1, keepdims=True)
            both = jnp.where(lane == 0, square, jnp.where(lane == 1, cross, zero))
            stats[:, rows] = jnp.transpose(both)[:8, :]
        return carry

    lax.fori_loop(0, BLOCKS, block, 0)
    copies.store(y_all, y_out)
    copies.store(starts, starts_out)
    copies.store(gated_gain, gg_out)
    for at in range(0, D, PART):
        cols = slice(at, at + PART)
        part = dot_nt(gated_gain[...], whole[cols, OUT]).astype(BF)
        target = mixed if last else held_rows
        target[:, cols] = part
    if last:
        copies.store(mixed, mixed_out)
    else:
        for o in range(4):
            outs[o][:, :D] = held_rows[rows_at(lax.rem(place + o, 4)), :]
    copies.finish()


def in_hbm(shapes):
    return [pltpu.HBM(k.shape, k.dtype) for k in shapes]


def forward_call(where, ends, chunks, weights):
    last = len(chunks) > 0
    kept = [
        shape(SEQ, D, dtype=BF),
        shape(SEQ, 2 * CHANNELS),
        shape(SEQ, 384),
        shape(SEQ, CHANNELS),
        shape(BLOCKS, STATES, CHANNELS, dtype=BF),
        shape(SEQ, CHANNELS, dtype=BF),
    ]
    out_shape, out_specs = in_hbm(kept), [HBM] * 6
    scratch = [pltpu.VMEM(k.shape, k.dtype) for k in kept] + [pltpu.VMEM((D, WIDE), BF)]
    scratch += [
        pltpu.VMEM((PAD + SEQ, CHANNELS), F32),
        pltpu.VMEM((PAD + SEQ, 2 * STATES), F32),
        pltpu.VMEM((SEQ, CHANNELS), F32),
        pltpu.VMEM((SEQ, 2 * STATES), F32),
        pltpu.VMEM((STATES, CHANNELS), F32),
        pltpu.SemaphoreType.DMA((96,)),
        pltpu.VMEM((SEQ, D), BF),
    ]
    if last:
        args = (where, ends, *chunks, *weights)
        in_specs = [SMEM, ANY] + [VMEM] * 4 + [ANY] * 2 + [VMEM] * 4
        more = [shape(SEQ, CHANNELS), shape(SEQ, D, dtype=BF)]
        out_shape += in_hbm(more[:1]) + [shape(8, SEQ)] + in_hbm(more[1:])
        out_specs += [HBM, VMEM, HBM]
        scratch += [pltpu.VMEM(k.shape, k.dtype) for k in more]
    else:
        args = (where, ends, *weights)
        in_specs = [SMEM, ANY] + [ANY] * 10 + [VMEM]
        out_shape += [shape(BLOCK, SENT, dtype=BF)] * 4 + list(SMALL)
        out_specs += [VMEM] * 7

    def kernel(*refs):
        forward_kernel(last, *refs)

    return pl.pallas_call(
        kernel,
        out_shape=out_shape,
        in_specs=in_specs,
        out_specs=out_specs,
        scratch_shapes=scratch,
        compiler_params=limit(VMEM_LIMIT),
        cost_estimate=cost(20 * 10**9, 24 * 10**6),
        name="layer_forward",
    )(*args)


def scaled_rows(rows_grad, factor):
    return (rows_grad.astype(F32) * factor).astype(BF)


def misc_parts(grad_small):
    taps_low = grad_small[0:8, 0:CHANNELS].astype(BF)
    lane, rank = iota((128, 8), 0), iota((128, 8), 1)
    lines = jnp.zeros((384, 128), F32)
    for half in range(2):
        put = ((lane == 12 + 6 * half + rank) & (rank < 6)).astype(BF)
        lines = lines + dot_nt(select_lines(half), dot_nn(put, taps_low).astype(BF))
    put = ((lane == 25 + rank) & (rank < 5)).astype(BF)
    state_low = grad_small[0:8, CHANNELS : CHANNELS + 256].astype(BF)
    state_lines = dot_nn(put, state_low).astype(BF)
    put = ((lane == 30 + rank) & (rank < 3)).astype(BF)
    heads_low = grad_small[0:8, CHANNELS + 256 : CHANNELS + 384].astype(BF)
    head_lines = dot_nn(put, heads_low).astype(BF)
    row, head = iota((384, 128), 0), iota((384, 128), 1)
    head_rows = ((row - 96 * over_96(row) == head) & (head < HEADS)).astype(BF)
    return lines, state_lines, dot_nt(head_rows, head_lines)


def misc_tile(i, place, parts, grad_small):
    lines, state_lines, head_part = parts
    misc = head_part + dot_nt(select_state(384, i * 384), state_lines)
    misc = misc + jnp.where(place == i, lines, 0.0)
    gains = grad_small[8:9, i * 384 : (i + 1) * 384]
    return misc + jnp.transpose(jnp.where(iota((128, 384), 0) == 24, gains, 0.0))


def backward_kernel(last, *refs):
    refs = list(refs)

    def take(n):
        taken, refs[:n] = refs[:n], []
        return taken

    (where_ref,) = take(1)
    normed_in, zx_in, ss_in, y_in, starts_in, gated_gain_in = take(6)
    weights = (take(1), take(1)) if last else (take(5), take(5))
    taps_ref, taps_state_ref, heads_ref, gain_ref = take(4)
    if last:
        dscaled_in, cot = take(2)
        stat_parts = take(4)
    else:
        chunks = take(4)
    outs = take(4 if last else 1)
    (grad_small,) = take(1)
    mine_out, theirs_out = take(2)
    normed, zx, ss, y_all, starts, gated_gain, whole, dscaled = take(8)
    x_pad, state_pad, x_conv, state_conv, du_pad, dstate_pad = take(6)
    d_hidden, d_inner, factors, sems = take(4)
    dss, products, rows_grad, sent = take(4)
    grad_taps, grad_taps_state = grad_small.at[0:8, 0:CHANNELS], grad_small.at[0:8, 768:1024]
    grad_heads, grad_gain = grad_small.at[0:8, 1024:1152], grad_small.at[8:9, :]
    copies = Copies(sems)
    place, core = where_ref[0], where_ref[1]
    if not last:
        load_out = place_blocks(copies, where_ref, weights, whole, OUT)
    load_x = copies.start(zx_in.at[:, CHANNELS:], zx.at[:, CHANNELS:])
    load_ss = copies.start(ss_in, ss)
    if last:
        load_cot = [copies.start(cot.at[k, 1], sent.at[rows_at(k), :]) for k in range(BLOCKS)]
    du_pad[SEQ:, :] = jnp.zeros((PAD, CHANNELS), F32)
    dstate_pad[SEQ:, :] = jnp.zeros((PAD, 2 * STATES), F32)
    for ref in (d_hidden, grad_small):
        ref[...] = jnp.zeros_like(ref)
    if last:
        total = stat_parts[0][...] + stat_parts[1][...] + stat_parts[2][...] + stat_parts[3][...]
        factor = lax.rsqrt(total[0:1, :] / DI + EPS)
        cubed = factor * factor * factor / DI * total[1:2, :]
        row = iota((128, SEQ), 0)
        both = jnp.where(row == 0, factor, jnp.where(row == 1, cubed, 0.0))
        for b in range(BLOCKS):
            part = slice(b * BLOCK, (b + 1) * BLOCK)
            factors[part, :] = jnp.transpose(both[:, part])
        for k in range(BLOCKS):
            rows = slice(k * BLOCK, (k + 1) * BLOCK)
            load_cot[k].wait()
            rows_grad[rows, :] = scaled_rows(sent[rows, :], factors[rows, 0:1])
    else:
        for offset, chunk in zip((0, 3, 1, 2), chunks):
            rows = rows_at(lax.rem(place + offset, 4))
            rows_grad[rows, :] = chunk[:, :D]
            tail = chunk[:, D:].astype(F32)
            factor = tail[:, 0:1] + tail[:, 1:2]
            cross = tail[:, 2:3] + tail[:, 3:4]
            lane = iota((BLOCK, 128), 1)
            cubed = factor * factor * factor / DI * cross
            factors[rows, :] = jnp.where(lane == 0, factor, jnp.where(lane == 1, cubed, 0.0))
        for load in load_out:
            load.wait()
        dscaled[...] = dot_nn(rows_grad[...], whole[:, OUT])
        rows_grad[...] = scaled_rows(rows_grad[...], factors[:, 0:1])
    load_x.wait()
    load_rows = [
        copies.start(zx_in.at[:, :CHANNELS], zx.at[:, :CHANNELS]),
        copies.start(y_in, y_all),
        copies.start(starts_in, starts),
    ]
    if last:
        load_rows.append(copies.start(dscaled_in, dscaled))
    x_pad[:PAD, :] = jnp.zeros((PAD, CHANNELS), F32)
    x_pad[PAD:, :] = zx[:, CHANNELS:]
    load_ss.wait()
    state_pad[:PAD, :] = jnp.zeros((PAD, 2 * STATES), F32)
    state_pad[PAD:, :] = ss[:, : 2 * STATES]
    conv_rows(x_pad, taps_ref, x_conv)
    conv_rows(state_pad, taps_state_ref, state_conv)
    for load in load_rows:
        load.wait()
    load_late = [
        copies.start(normed_in, normed),
        copies.start(gated_gain_in, gated_gain),
        *place_blocks(copies, where_ref, weights, whole, IN),
        *place_blocks(copies, where_ref, weights, whole, SS),
    ]

    def block(turn, carry):
        b = BLOCKS - 1 - turn
        rows = rows_at(b)
        state_u = state_conv[rows, :]
        state_s = sigmoid(state_u)
        state = state_u * state_s
        keys, reads = state[:, :STATES].astype(BF), state[:, STATES:].astype(BF)
        reads_t = jnp.transpose(state[:, STATES:]).astype(BF)
        raised, step, log_decay, summed, summed_t = step_terms(ss[rows, 2 * STATES :], heads_ref)
        meets_t = dot_nt(keys, reads)
        causal_t = iota((BLOCK, BLOCK), 1) >= iota((BLOCK, BLOCK), 0)
        fac = factors[rows, :][:, 0:1]
        cub = factors[rows, :][:, 1:2]
        d_meets_t = jnp.zeros((BLOCK, BLOCK), F32)
        d_keys = jnp.zeros((BLOCK, STATES), F32)
        d_reads = jnp.zeros((BLOCK, STATES), F32)
        head_sums = jnp.zeros((2 * BLOCK, 128), F32)
        last_row = iota((BLOCK, 128), 0) == BLOCK - 1
        for p in range(PAIRS):
            cols = slice(p * 128, (p + 1) * 128)
            u = x_conv[rows, cols]
            us = sigmoid(u)
            x = u * us
            step_wide = spread(step, 2 * p)
            summed_wide = spread(summed, 2 * p)
            grown = jnp.exp(summed_wide)
            end = grown[BLOCK - 1 : BLOCK, :]
            to_end = jnp.exp(summed_wide[BLOCK - 1 : BLOCK, :] - summed_wide)
            skip = taps_ref[6:7, cols]
            gain = taps_ref[5:6, cols]
            z = zx[rows, cols]
            zs = sigmoid(z)
            z_act = z * zs
            y = y_all[rows, cols]
            gated = y * z_act
            incoming = dscaled[rows, cols]
            lifted = gated * fac
            grad_taps[5:6, cols] += jnp.sum(incoming * lifted, axis=0, keepdims=True)
            d_gated = fac * (gain * incoming) - gated * cub
            dy = d_gated * z_act
            d_inner[rows, cols] = (d_gated * y * (zs + z_act * (1.0 - zs))).astype(BF)
            dy_low = dy.astype(BF)
            weighted = x * step_wide
            weighted_low = weighted.astype(BF)
            dy_grown = (dy * grown).astype(BF)
            held_low = starts[b, :, cols]
            dh = d_hidden[:, cols]
            dh_low = dh.astype(BF)
            d_reads = d_reads + dot_nt(dy_grown, held_low)
            kept = dot_nn(keys, dh_low) * to_end
            d_keys = d_keys + dot_nt((to_end * weighted).astype(BF), dh_low)
            decays = []
            for h in (2 * p, 2 * p + 1):
                gaps = summed_t[h : h + 1, :] - summed[:, h : h + 1]
                decays.append(jnp.exp(jnp.where(causal_t, gaps, NEG)))
            mixes = jnp.concatenate([(d * meets_t).astype(BF) for d in decays], axis=1)
            d_weighted = dot_nn(mixes, side_by_side(dy).astype(BF)) + kept
            d_mixes = dot_nt(side_by_side(weighted).astype(BF), dy_low)
            d_meets_t = d_meets_t + d_mixes[:BLOCK] * decays[0] + d_mixes[BLOCK:] * decays[1]
            dx = skip * dy + d_weighted * step_wide
            weighted_f = weighted_low.astype(F32)
            moved = dy_low.astype(F32) * (y - skip * x) - weighted_f * d_weighted
            extra = jnp.sum(weighted_f * kept, axis=0, keepdims=True) + end * jnp.sum(
                dh * held_low.astype(F32), axis=0, keepdims=True
            )
            moved = jnp.where(last_row, moved + extra, moved)
            upper, lower = two_parts(jnp.concatenate([moved, x * d_weighted], axis=0))
            picks = (
                iota((256, 128), 1) == 2 * p + (iota((256, 128), 0) % 128) // HEAD_DIM
            ).astype(BF)
            head_sums = head_sums + dot_nn(jnp.concatenate([upper, lower], axis=1), picks)
            grad_taps[6:7, cols] += jnp.sum(dy * x, axis=0, keepdims=True)
            du_pad[rows, cols] = dx * (us + x * (1.0 - us))
            d_hidden[:, cols] = end * dh + dot_nn(reads_t, dy_grown)
        d_reads = d_reads + dot_nn(jnp.transpose(d_meets_t).astype(BF), keys)
        d_keys = d_keys + dot_nn(d_meets_t.astype(BF), reads)
        d_state = jnp.concatenate([d_keys, d_reads], axis=1)
        d_state = d_state * (state_s + state * (1.0 - state_s))
        dstate_pad[rows, :] = d_state
        upper_tri = (iota((BLOCK, BLOCK), 1) >= iota((BLOCK, BLOCK), 0)).astype(F32)
        d_decay = dot_high(upper_tri, head_sums[:BLOCK])
        d_step = head_sums[BLOCK:] - d_decay * jnp.exp(heads_ref[1:2, :])
        d_raw = d_step * sigmoid(raised)
        dss[rows, 2 * STATES :] = d_raw.astype(BF)
        grad_heads[0:1, :] += jnp.sum(d_raw, axis=0, keepdims=True)
        grad_heads[1:2, :] += jnp.sum(d_decay * log_decay, axis=0, keepdims=True)
        return carry

    lax.fori_loop(0, BLOCKS, block, 0)

    def store_inner(start, cols, value):
        cols = slice(CHANNELS + cols.start, CHANNELS + cols.stop)
        d_inner[start : start + BLOCK, cols] = value

    def store_state(start, cols, value):
        dss[start : start + BLOCK, cols] = value

    conv_back(du_pad, x_pad, taps_ref, grad_taps, store_inner)
    conv_back(dstate_pad, state_pad, taps_state_ref, grad_taps_state, store_state)
    picks = (iota((CHANNELS, 128), 1) == iota((CHANNELS, 128), 0) // HEAD_DIM).astype(F32)
    grad_heads[2:3, :] = dot_high(grad_taps[...], picks)[6:7, :]
    for load in load_late:
        load.wait()
    for at in range(0, D, PART):
        cols = slice(at, at + PART)
        part = dot_nt(d_inner[...], whole[cols, IN]) + dot_nt(dss[...], whole[cols, SS])
        total = jnp.sum(part * normed[:, cols].astype(F32), axis=0, keepdims=True)
        grad_gain[:, cols] = total / gain_ref[:, cols]
        sent[:, cols] = part.astype(BF)
    if last:
        for o, out in enumerate(outs):
            copies.store(sent.at[rows_at(lax.rem(place + o, 4)), :], out)
    else:
        copies.store(sent, outs[0])
    parts = misc_parts(grad_small)
    for i in range(4):
        lanes = slice(i * 384, (i + 1) * 384)
        shared = dot_tn(normed[:, lanes], dss[...])
        for cols, value in (
            (IN, dot_tn(normed[:, lanes], d_inner[...])),
            (OUT, dot_tn(rows_grad[:, lanes], gated_gain[...])),
            (STATE, shared[:, :256]),
            (MISC, shared[:, 256:] + misc_tile(i, place, parts, grad_small)),
        ):
            low = value.astype(BF)
            for k in range(8):
                at = (4 * i + k // 2) * 48
                products[k % 2, at : at + 48, cols] = low[k * 48 : (k + 1) * 48]
        rows = slice(i * 192, (i + 1) * 192)
        copies.store(products.at[1 - core, rows, :], theirs_out.at[rows, :])
        copies.store(products.at[core, rows, :], mine_out.at[rows, :])
    copies.finish()


def backward_call(where, kept, weights, taps, taps_state, heads, gain, last, extra):
    args = [where, *kept, *weights, taps, taps_state, heads, gain, *extra]
    in_specs = [SMEM] + [HBM] * 6 + [ANY] * len(weights) + [VMEM] * 4
    in_specs += [HBM, ANY] + [VMEM] * 4 if last else [VMEM] * 4
    out_shape = [
        *([pltpu.HBM((BLOCK, D), BF)] * 4 if last else [pltpu.HBM((SEQ, D), BF)]),
        shape(16, D),
        *[pltpu.HBM((SIDE, WIDE), BF)] * 2,
    ]
    out_specs = [HBM] * (len(out_shape) - 3) + [VMEM] + [HBM] * 2
    scratch = [pltpu.VMEM(k.shape, k.dtype) for k in kept] + [pltpu.VMEM((D, WIDE), BF)]
    scratch += [
        pltpu.VMEM((SEQ, CHANNELS), F32),
        pltpu.VMEM((PAD + SEQ, CHANNELS), F32),
        pltpu.VMEM((PAD + SEQ, 2 * STATES), F32),
        pltpu.VMEM((SEQ, CHANNELS), F32),
        pltpu.VMEM((SEQ, 2 * STATES), F32),
        pltpu.VMEM((PAD + SEQ, CHANNELS), F32),
        pltpu.VMEM((PAD + SEQ, 2 * STATES), F32),
        pltpu.VMEM((STATES, CHANNELS), F32),
        pltpu.VMEM((SEQ, 2 * CHANNELS), BF),
        pltpu.VMEM((SEQ, 128), F32),
        pltpu.SemaphoreType.DMA((128,)),
        pltpu.VMEM((SEQ, 384), BF),
        pltpu.VMEM((2, SIDE, WIDE), BF),
        pltpu.VMEM((SEQ, D), BF),
        pltpu.VMEM((SEQ, D), BF),
    ]

    def kernel(*refs):
        backward_kernel(last, *refs)

    return pl.pallas_call(
        kernel,
        out_shape=out_shape,
        in_specs=in_specs,
        out_specs=out_specs,
        scratch_shapes=scratch,
        compiler_params=limit(VMEM_LIMIT),
        cost_estimate=cost(32 * 10**9, 30 * 10**6),
        name="layer_backward",
    )(*args)


def arrived(parts):
    return sum((part[...].astype(F32) for part in parts[1:]), parts[0][...].astype(F32))


def after_first_kernel(rows_ref, a, b, c, d, hidden, mixed, factor_out):
    total = arrived((a, b, c, d))
    mixed[...] = total[:, :D]
    square = total[:, D : D + 1] + total[:, D + 1 : D + 2]
    factor = lax.rsqrt(square / DI + EPS)
    factor_out[...] = jnp.broadcast_to(factor, (BLOCK, 128))
    hidden[...] = (rows_ref[...].astype(F32) + factor * total[:, :D]).astype(BF)


def after_first_call(rows, parts):
    return pl.pallas_call(
        after_first_kernel,
        out_shape=[shape(BLOCK, D, dtype=BF), shape(BLOCK, D), shape(BLOCK, 128)],
        in_specs=[VMEM] * 5,
        out_specs=[VMEM] * 3,
        name="between_layers",
    )(rows, *parts)


def after_last_kernel(where_ref, rows_ref, mixed, a, b, c, d, result):
    total = a[...] + b[...] + c[...] + d[...]
    factor = lax.rsqrt(total[0:1, :] / DI + EPS)
    row = iota((128, SEQ), 0)
    column = jnp.zeros((BLOCK, 128), F32)
    for k in range(4):
        part = slice(k * BLOCK, (k + 1) * BLOCK)
        turned = jnp.transpose(jnp.where(row[:, part] == 0, factor[:, part], 0.0))
        column = jnp.where(where_ref[0] == k, turned, column)
    result[...] = rows_ref[...].astype(F32) + column[:, 0:1] * mixed[...].astype(F32)


def after_last_call(where, rows, mixed, stat_parts):
    return pl.pallas_call(
        after_last_kernel,
        out_shape=shape(BLOCK, D),
        in_specs=[SMEM] + [VMEM] * 6,
        out_specs=VMEM,
        name="last_rows",
    )(where, rows, mixed, *stat_parts)


def rows_back(rows_ref, parts, gain_ref, grad_ref):
    incoming = arrived(parts)
    v = rows_ref[...].astype(F32)
    q = lax.rsqrt(jnp.mean(v * v, axis=1, keepdims=True) + EPS)
    weighted = incoming * gain_ref[...]
    inner = jnp.sum(weighted * v, axis=1, keepdims=True)
    return grad_ref[...].astype(F32) + q * weighted - v * (q * q * q / D * inner)


def back_last_kernel(rows_ref, a, b, c, d, gain_ref, grad_ref, mixed_ref, factor_ref, out):
    low = rows_back(rows_ref, (a, b, c, d), gain_ref, grad_ref).astype(BF)
    out[:, :D] = low
    cross = jnp.sum(low.astype(F32) * mixed_ref[...], axis=1, keepdims=True)
    factor = factor_ref[:, 0:1]
    pieces = [*two_parts(factor), *two_parts(cross)]
    lane = iota((BLOCK, 128), 1)
    tail = jnp.zeros((BLOCK, 128), F32)
    for k, piece in enumerate(pieces):
        tail = jnp.where(lane == k, piece.astype(F32), tail)
    out[:, D:] = tail.astype(BF)


def back_last_call(rows, parts, gain, grad, mixed, factor):
    return pl.pallas_call(
        back_last_kernel,
        out_shape=shape(BLOCK, SENT, dtype=BF),
        in_specs=[VMEM] * 9,
        out_specs=VMEM,
        name="between_layers_back",
    )(rows, *parts, gain, grad, mixed, factor)


def back_first_kernel(rows_ref, incoming, gain_ref, grad_ref, out):
    out[...] = rows_back(rows_ref, (incoming,), gain_ref, grad_ref[:, :D])


def back_first_call(rows, incoming, gain, grad):
    return pl.pallas_call(
        back_first_kernel,
        out_shape=shape(BLOCK, D),
        in_specs=[VMEM] * 4,
        out_specs=VMEM,
        name="first_rows_back",
    )(rows, incoming, gain, grad)


def params_kernel(where_ref, misc, heads_ref, taps, taps_state, gain):
    small_params(where_ref[0], misc, heads_ref, taps, taps_state, gain)


def params_call(where, misc, heads):
    return pl.pallas_call(
        params_kernel,
        out_shape=SMALL,
        in_specs=[SMEM, VMEM, VMEM],
        out_specs=[VMEM] * 3,
        compiler_params=limit(16),
        name="small_parameters",
    )(where, misc, heads)


def both_kernel(where_ref, mine, given, *outs):
    if len(outs) == 1:
        outs[0][...] = (mine[...].astype(F32) + given[...].astype(F32)).astype(BF)
        return
    core, row, col = where_ref[1], where_ref[2], where_ref[3]
    own, ahead, far_left, far_right, behind, parts = outs
    for i in range(4):
        for j in range(4):
            rows = slice((4 * i + j) * 48, (4 * i + j + 1) * 48)
            total = (mine[rows, :].astype(F32) + given[rows, :].astype(F32)).astype(BF)
            along, across = lax.rem(i - row + 4, 4), lax.rem(j - col + 4, 4)
            o = along + core * (across - along)
            q = across + core * (along - across)
            parts[o, pl.ds(pl.multiple_of(q * 48, 16), 48), :] = total
    own[...] = parts[0]
    ahead[...] = parts[1]
    far_left[...] = parts[2, :, LEFT]
    far_right[...] = parts[2, :, RIGHT]
    behind[...] = parts[3]


def ring_shapes(rows):
    whole = shape(rows, WIDE, dtype=BF)
    left, right = shape(rows, SPLIT, dtype=BF), shape(rows, WIDE - SPLIT, dtype=BF)
    return [whole, whole, left, right, whole]


def both_call(where, mine, given, relative):
    out_shape = ring_shapes(192) if relative else [shape(SIDE, WIDE, dtype=BF)]
    return pl.pallas_call(
        both_kernel,
        out_shape=out_shape,
        in_specs=[SMEM] + [VMEM] * 2,
        out_specs=[VMEM] * len(out_shape),
        scratch_shapes=[pltpu.VMEM((4, 192, WIDE), BF)] if relative else [],
        compiler_params=limit(28),
        cost_estimate=cost(10**6, 10**4),
        name="both_cores_grads",
    )(where, mine, given)


def passed_kernel(ahead, behind, left, right, out_ahead, out_behind):
    out_ahead[:, LEFT] = (ahead[:, LEFT].astype(F32) + left[...].astype(F32)).astype(BF)
    out_ahead[:, RIGHT] = ahead[:, RIGHT]
    out_behind[:, LEFT] = behind[:, LEFT]
    out_behind[:, RIGHT] = (behind[:, RIGHT].astype(F32) + right[...].astype(F32)).astype(BF)


def passed_call(ahead, behind, left, right):
    return pl.pallas_call(
        passed_kernel,
        out_shape=[shape(*ahead.shape, dtype=BF)] * 2,
        in_specs=[VMEM] * 4,
        out_specs=[VMEM] * 2,
        compiler_params=limit(16),
        cost_estimate=cost(10**6, 10**4),
        name="grads_passed_on",
    )(ahead, behind, left, right)


def halfway_kernel(a, b, c, own, ahead, far_left, far_right, behind):
    total = arrived((a, b, c)).astype(BF)
    own[...] = total[:48]
    ahead[...] = total[48:96]
    far_left[...] = total[96:144, LEFT]
    far_right[...] = total[96:144, RIGHT]
    behind[...] = total[144:]


def halfway_call(parts):
    return pl.pallas_call(
        halfway_kernel,
        out_shape=ring_shapes(48),
        in_specs=[VMEM] * 3,
        out_specs=[VMEM] * 5,
        compiler_params=limit(20),
        name="grads_halfway",
    )(*parts)


def shard_kernel(where_ref, a, b, c, share_1, own, given):
    share_0 = arrived((a, b, c))
    is_first = where_ref[1] == 0
    other = share_1[...].astype(F32)
    own[...] = jnp.where(is_first, share_0, other)
    given[...] = jnp.where(is_first, other, share_0).astype(BF)


def shard_call(where, parts, share_1):
    return pl.pallas_call(
        shard_kernel,
        out_shape=[shape(48, WIDE), shape(48, WIDE, dtype=BF)],
        in_specs=[SMEM] + [VMEM] * 4,
        out_specs=[VMEM] * 2,
        name="grads_shard",
    )(where, *parts, share_1)


def swap(v):
    return lax.ppermute(v, "section", [(0, 1), (1, 0)])


def turn(v, by, axis="tensor"):
    return lax.ppermute(v, axis, [(i, (i + by) % 4) for i in range(4)])


def spread_rows(v):
    return (v, turn(v, 1), turn(v, -1), turn(v, 2))


def meet(parts, axis="tensor"):
    own, ahead, across, behind = parts
    return (own, turn(ahead, 1, axis), turn(behind, -1, axis), turn(across, 2, axis))


def from_ring(v, axis):
    return (v, turn(v, -1, axis), turn(v, 2, axis), turn(v, 1, axis))


def ring(v, by, phase):
    pairs = []
    for s in range(2):
        for a in range(4):
            for b in range(4):
                to = ((a + by) % 4, b) if s == phase else (a, (b + by) % 4)
                pairs.append((16 * s + 4 * a + b, 16 * s + 4 * to[0] + to[1]))
    return lax.ppermute(v, ("section", *DP), pairs)


def around(v, phase):
    ahead, behind = lax.optimization_barrier((ring(v, -1, phase), ring(v, 1, phase)))
    return (
        v,
        ahead,
        ring(ahead[:, :SPLIT], -1, phase),
        ring(behind[:, SPLIT:], 1, phase),
        behind,
    )


def gather_by_turns(main, rest):
    own, ahead, far_left, far_right, behind = around(main, 0)
    far = jnp.concatenate([far_left, far_right], axis=1)
    rest = (rest, ring(rest, -1, 0), ring(rest, 2, 0), ring(rest, 1, 0))
    rows = [
        jnp.concatenate(pair, axis=1) for pair in zip((own, ahead, far, behind), rest)
    ]
    return around(jnp.concatenate(rows, axis=0), 1)


def pick(v, index, axis):
    return lax.dynamic_index_in_dim(v, index, axis, keepdims=False)


def tie(*values):
    return lax.optimization_barrier(values)


def shards(
    section_ends,
    norm_gain,
    proj_inner,
    proj_step,
    proj_state,
    conv_inner,
    conv_state,
    gate_gain,
    head_params,
    proj_output,
):
    core = lax.axis_index("section")
    place = lax.axis_index("tensor")
    is_first = core == 0
    where = jnp.stack(
        [place, core, lax.axis_index("dp_0"), lax.axis_index("dp_1")]
    ).astype(jnp.int32)

    packed = jnp.concatenate(
        [
            proj_state[0].reshape(-1),
            norm_gain[0],
            conv_inner[0].reshape(-1),
            gate_gain[0],
            conv_state[0].reshape(-1),
            jnp.zeros((32 * 256 - 6144 - 332,), BF),
        ]
    ).reshape(32, 256)
    turned = jnp.stack(from_ring(packed, "tensor") * 2)
    filled = lax.dynamic_slice_in_dim(turned, lax.rem(4 - place, 4), 4, 0).reshape(4, 32 * 256)
    state_rows = filled[:, :6144].reshape(96, 256)
    norm_col = filled[:, 6144:6168].reshape(96, 1)
    inner_cols = filled[:, 6168:6408].reshape(4, 5, 48).transpose(0, 2, 1).reshape(192, 5)
    gate_col = filled[:, 6408:6456].reshape(192, 1)
    both = jnp.concatenate([inner_cols, gate_col], axis=1)
    both = both.reshape(2, 96, 6).transpose(1, 0, 2).reshape(96, 12)
    state_cols = filled[:, 6456:6476].reshape(4, 5, 4).transpose(0, 2, 1).reshape(16, 5)
    state_cols = jnp.pad(state_cols, ((0, 80), (0, 0)))
    misc = jnp.concatenate(
        [proj_step[0], both, norm_col, state_cols, jnp.zeros((96, 128 - 30), BF)], axis=1
    )

    def by_layer_of(keep, got):
        return jnp.where(is_first, keep, got), jnp.where(is_first, got, keep)

    def by_layer(halves):
        return by_layer_of(pick(halves, core, 0), swap(pick(halves, 1 - core, 0)))

    main = jnp.concatenate([proj_inner[0].reshape(96, 2 * CHANNELS), proj_output[0].T], axis=1)
    main_0, main_1 = by_layer(main.reshape(2, 48, MAIN))
    main_0, heads_got = tie(main_0, swap(head_params[0]))
    rest_0, rest_1 = by_layer(jnp.concatenate([state_rows, misc], axis=1).reshape(2, 48, 384))

    ends = section_ends[0]
    got_rows = swap(pick(ends, 1 - core, 0))
    rows_in = jnp.where(is_first, ends[0], got_rows)
    cot = jnp.where(is_first, got_rows, ends[1])
    heads = [
        jnp.pad(v.astype(F32), ((0, 5), (0, 128 - HEADS)))
        for v in by_layer_of(head_params[0], heads_got)
    ]
    ends_all = lax.all_gather(jnp.stack([rows_in, cot]), "tensor", axis=0)
    own_pieces = gather_by_turns(main_0, rest_0)
    shard_1 = jnp.concatenate([main_1, rest_1], axis=1)
    shard_1, *rest = tie(shard_1, *heads, *own_pieces)
    heads, own_pieces = rest[:2], rest[2:]
    full_1 = lax.all_gather(shard_1, DP, axis=0, tiled=True)
    pieces_0 = (*own_pieces, *[swap(v) for v in own_pieces])
    first = forward_call(where, ends_all, (), (*pieces_0, heads[0]))
    kept_0, sent_0, small_0 = first[:6], first[6:10], first[10:]
    weights_0 = (pieces_0, small_0[0], small_0[1], heads[0], small_0[2])
    own_1, *met_0 = tie(full_1, *meet(sent_0))
    other_1 = swap(own_1)
    order = (own_1[:, MISC].reshape(16, 48, 128), other_1[:, MISC].reshape(16, 48, 128))
    misc_1 = jnp.where(is_first, jnp.stack(order, axis=1), jnp.stack(order[::-1], axis=1))
    small_1 = params_call(where, misc_1.reshape(D, 128), heads[1])
    weights_1 = ((own_1, other_1), small_1[0], small_1[1], heads[1], small_1[2])
    hidden, mixed_0, factor_0 = after_first_call(rows_in, met_0)
    kept_1 = forward_call(
        where, ends_all, spread_rows(hidden), (own_1, other_1, *weights_1[1:])
    )
    dscaled_1, stats, mixed_1 = kept_1[6:]
    stat_parts = spread_rows(stats)
    met_1 = lax.psum_scatter(mixed_1, "tensor", scatter_dimension=0, tiled=True)
    back_1 = backward_call(
        where, kept_1[:6], *weights_1, True, (dscaled_1, ends_all, *stat_parts)
    )
    met_1, *back_1 = tie(met_1, *back_1)
    payload_1 = both_call(where, back_1[5], swap(back_1[6]), False)[0]
    payload_1, *d_met_1 = tie(payload_1, *meet(back_1[:4]))
    grad_1 = back_last_call(hidden, d_met_1, weights_1[4], cot, mixed_0, factor_0)
    payload_1, met_1, grad_1 = tie(payload_1, met_1, grad_1)
    share_1 = lax.psum_scatter(payload_1, DP, scatter_dimension=0, tiled=True)
    result = after_last_call(where, hidden, met_1, stat_parts)
    result, *chunks_0 = tie(result, *spread_rows(grad_1))
    back_0 = backward_call(where, kept_0, *weights_0, False, chunks_0)
    parts_0 = both_call(where, back_0[2], swap(back_0[3]), True)
    own, ahead, far_left, far_right, behind = parts_0
    ahead, behind = passed_call(
        ahead, behind, ring(far_left, 1, 0), ring(far_right, -1, 0)
    )
    share_1, rows_0, ahead, behind = tie(share_1, back_0[0], ahead, behind)
    ahead, behind = tie(ring(ahead, 1, 0), ring(behind, -1, 0))
    pieces = halfway_call((own, ahead, behind))
    met_0 = lax.psum_scatter(rows_0, "tensor", scatter_dimension=0, tiled=True)
    own, ahead, far_left, far_right, behind = pieces
    ahead, behind = passed_call(
        ahead, behind, ring(far_left, 1, 1), ring(far_right, -1, 1)
    )
    met_0, ahead, behind = tie(met_0, ahead, behind)
    half_met = (own, ring(ahead, 1, 1), ring(behind, -1, 1))
    grad_0 = back_first_call(rows_in, met_0, weights_0[4], grad_1)
    rows_got = swap(jnp.where(is_first, result, grad_0))
    section_rows = jnp.where(
        is_first, jnp.stack([grad_0, rows_got]), jnp.stack([rows_got, result])
    )
    share_own, share_given = shard_call(where, half_met, share_1)
    share_got = swap(share_given).astype(F32)
    whole = jnp.where(
        is_first,
        jnp.concatenate([share_own, share_got], axis=0),
        jnp.concatenate([share_got, share_own], axis=0),
    )
    grad_inner = whole[:, IN].reshape(96, 2, CHANNELS)
    grad_output = whole[:, OUT].T
    misc = whole[:, MISC]
    grad_step = misc[:, :HEADS]
    grad_heads = misc[:HEADS, 30:33].T
    to_send = jnp.concatenate(
        [
            whole[:, STATE].reshape(4, 6144),
            misc[:, 24].reshape(4, 24),
            misc[:, 12:24].reshape(96, 2, 6).transpose(1, 0, 2).reshape(4, 48 * 6),
            misc[:16, 25:30].reshape(4, 20),
            jnp.zeros((4, 32 * 256 - 6144 - 332), F32),
        ],
        axis=1,
    ).reshape(4, 32, 256)
    pieces = [pick(to_send, lax.rem(place + o, 4), 0) for o in range(4)]
    section_rows, *met = tie(section_rows, *meet(pieces))
    total = (met[0] + met[1] + met[2] + met[3]).reshape(-1)
    grad_state = total[:6144].reshape(24, 256)
    grad_norm = total[6144:6168]
    inner_lines = total[6168:6456].reshape(48, 6).T
    grad_conv_inner = inner_lines[:5]
    grad_gate = inner_lines[5]
    grad_conv_state = total[6456:6476].reshape(4, 5).T
    return (
        section_rows[None],
        grad_norm[None],
        grad_inner[None],
        grad_step[None],
        grad_state[None],
        grad_conv_inner[None],
        grad_conv_state[None],
        grad_gate[None],
        grad_heads[None],
        grad_output[None],
    )


def solution(mesh):
    split = Mesh(
        mesh.devices.reshape(mesh.shape["section"], 4, 4, mesh.shape["tensor"]),
        ("section", "dp_0", "dp_1", "tensor"),
    )
    return jax.shard_map(
        shards,
        mesh=split,
        in_specs=(
            P("section", None, DP_TENSOR, None),
            P("section", DP_TENSOR),
            P("section", DP, None, "tensor"),
            P("section", DP, "tensor"),
            P("section", DP_TENSOR, None),
            P("section", None, DP_TENSOR),
            P("section", None, DP_TENSOR),
            P("section", DP_TENSOR),
            P("section", None, "tensor"),
            P("section", "tensor", DP),
        ),
        out_specs=(
            P("section", None, DP_TENSOR, None),
            P("section", DP_TENSOR),
            P("section", DP, None, "tensor"),
            P("section", DP, "tensor"),
            P("section", DP_TENSOR, None),
            P("section", None, DP_TENSOR),
            P("section", None, DP_TENSOR),
            P("section", DP_TENSOR),
            P("section", None, "tensor"),
            P("section", "tensor", DP),
        ),
        check_vma=False,
    )
```

```python
import jax
import jax.numpy as jnp
from jax import lax
from jax.experimental import pallas as pl
from jax.experimental.pallas import tpu as pltpu
from jax.sharding import Mesh
from jax.sharding import PartitionSpec as P

D = 1536
SEQ = 512
BLOCK = 128
BLOCKS = SEQ // BLOCK
STATES = 128
CHANNELS = 768
HEADS = 12
HEAD_DIM = 64
PAIRS = HEADS // 2
DI = 3072
PAD = 8
EPS = 1e-05
NEG = -1e30
DP = ("dp_0", "dp_1")
DP_TENSOR = ("dp_0", "dp_1", "tensor")
SENT = D + 128
BF = jnp.bfloat16
F32 = jnp.float32
HIGH = lax.Precision.HIGHEST
VMEM = pl.BlockSpec(memory_space=pltpu.VMEM)
SMEM = pl.BlockSpec(memory_space=pltpu.SMEM)
HBM = pl.BlockSpec(memory_space=pltpu.HBM)
ANY = pl.BlockSpec(memory_space=pl.ANY)
SIDE = D // 2
WIDE = 2 * CHANNELS + CHANNELS + 384
SS = slice(0, 384)
STATE = slice(0, 256)
MISC = slice(256, 384)
Z = slice(384, 384 + CHANNELS)
X = slice(384 + CHANNELS, 384 + 2 * CHANNELS)
IN = slice(384, 384 + 2 * CHANNELS)
READ = 384 + 2 * CHANNELS
BOTH = slice(0, READ)
OUT = slice(READ, WIDE)
MAIN = 3 * CHANNELS
SPLIT = 2 * CHANNELS
PART = 256
LEFT, RIGHT = slice(0, SPLIT), slice(SPLIT, WIDE)
BETWEEN = slice(SPLIT, READ)
VMEM_LIMIT = 54


def shape(*dims, dtype=F32):
    return jax.ShapeDtypeStruct(dims, dtype)


def limit(megabytes):
    return pltpu.CompilerParams(vmem_limit_bytes=megabytes * 1024 * 1024)


def cost(flops, read):
    return pl.CostEstimate(flops=flops, bytes_accessed=read, transcendentals=0)


def dot_nn(left, right):
    return lax.dot_general(left, right, (((1,), (0,)), ((), ())), preferred_element_type=F32)


def dot_nt(left, right):
    return lax.dot_general(left, right, (((1,), (1,)), ((), ())), preferred_element_type=F32)


def dot_tn(left, right):
    return lax.dot_general(left, right, (((0,), (0,)), ((), ())), preferred_element_type=F32)


def dot_high(left, right):
    return lax.dot_general(
        left, right, (((1,), (0,)), ((), ())), precision=HIGH, preferred_element_type=F32
    )


def sigmoid(v):
    return 1.0 / (1.0 + jnp.exp(-v))


def softplus(v):
    return jnp.maximum(v, 0.0) + jnp.log1p(jnp.exp(-jnp.abs(v)))


def rows_at(index):
    return pl.ds(pl.multiple_of(index * BLOCK, BLOCK), BLOCK)


def lanes_at(index):
    return pl.ds(pl.multiple_of(index * 128, 128), 128)


def iota(shape, dim):
    return lax.broadcasted_iota(jnp.int32, shape, dim)


def two_parts(v):
    upper = v.astype(BF)
    lower = (v - upper.astype(F32)).astype(BF)
    return upper, lower


def lane_tiles(width):
    return [slice(at, at + 128) for at in range(0, width, 128)]


def conv_rows(padded, taps, out):
    for cols in lane_tiles(out.shape[1]):
        for start in range(0, SEQ, BLOCK):
            total = taps[4:5, cols] + taps[0:1, cols] * padded[start + 5 : start + 5 + BLOCK, cols]
            for k in range(1, 4):
                at = start + 5 + k
                total = total + taps[k : k + 1, cols] * padded[at : at + BLOCK, cols]
            out[start : start + BLOCK, cols] = total


def conv_back(padded_grad, padded, taps, grad_taps, store):
    for cols in lane_tiles(padded.shape[1]):
        sums = [jnp.zeros((1, 128), F32)] * 5
        for start in range(0, SEQ, BLOCK):
            own = padded_grad[start : start + BLOCK, cols]
            total = taps[3:4, cols] * own
            sums[4] = sums[4] + jnp.sum(own, axis=0, keepdims=True)
            for k in range(4):
                at = start + 5 + k
                sums[k] = sums[k] + jnp.sum(own * padded[at : at + BLOCK, cols], axis=0, keepdims=True)
                if k < 3:
                    at = start + 3 - k
                    total = total + taps[k : k + 1, cols] * padded_grad[at : at + BLOCK, cols]
            store(start, cols, total.astype(BF))
        for k in range(5):
            grad_taps[k : k + 1, cols] = sums[k]


def step_terms(raw, heads):
    valid = iota((BLOCK, 128), 1) < HEADS
    raised = jnp.where(valid, raw + heads[0:1, :], -30.0)
    step = softplus(raised)
    log_decay = -step * jnp.exp(heads[1:2, :])
    lower = (iota((BLOCK, BLOCK), 0) >= iota((BLOCK, BLOCK), 1)).astype(F32)
    summed = dot_high(lower, log_decay)
    return raised, step, log_decay, summed, jnp.transpose(summed)


def spread(values, head):
    first = iota((BLOCK, 128), 1) < HEAD_DIM
    return jnp.where(first, values[:, head : head + 1], values[:, head + 1 : head + 2])


def side_by_side(v):
    first = iota(v.shape, 1) < HEAD_DIM
    zero = jnp.zeros_like(v)
    return jnp.concatenate([jnp.where(first, v, zero), jnp.where(first, zero, v)], axis=0)


def over_96(v):
    return lax.shift_right_logical(v * 683, 16)


def select_lines(half):
    row, channel = iota((384, CHANNELS), 0), iota((384, CHANNELS), 1)
    return (channel == over_96(row) * 96 + row + 96 * half).astype(BF)


def select_state(rows, first):
    row, channel = iota((rows, 256), 0) + first, iota((rows, 256), 1)
    group = over_96(row)
    inside = row - 96 * group
    return ((inside < 16) & (channel == 16 * group + inside)).astype(BF)


def small_params(place, misc, heads_ref, taps, taps_state, gain):
    lines = misc[pl.ds(pl.multiple_of(place * 384, 128), 384), :]
    first = dot_tn(lines, select_lines(0))
    second = dot_tn(lines, select_lines(1))
    picks = (iota((128, CHANNELS), 0) == iota((128, CHANNELS), 1) // HEAD_DIM).astype(BF)
    skip = dot_nn(heads_ref[...].astype(BF), picks)
    taps[0:6, :] = first[12:18, :] + second[18:24, :]
    taps[6:7, :] = skip[2:3, :]
    taps[7:8, :] = jnp.zeros((1, CHANNELS), F32)
    taps_state[...] = jnp.zeros((8, 256), F32)
    taps_state[0:5, :] = dot_tn(misc[...], select_state(D, 0))[25:30, :]
    gain[...] = jnp.transpose(misc[...].astype(F32))[24:25, :]


SMALL = (shape(8, CHANNELS), shape(8, 256), shape(1, D))


class Copies:
    def __init__(self, sems):
        self.sems = sems
        self.count = 0
        self.pending = []

    def start(self, source, target):
        copy = pltpu.make_async_copy(source, target, self.sems.at[self.count])
        self.count += 1
        copy.start()
        return copy

    def store(self, source, target):
        self.pending.append(self.start(source, target))

    def finish(self):
        for copy in self.pending:
            copy.wait()


def place_blocks(copies, where_ref, parts, whole, cols):
    row, col = where_ref[2], where_ref[3]
    started = []
    for k, pieces in enumerate(parts):
        core = where_ref[1] if k == 0 else 1 - where_ref[1]
        if len(pieces) == 1:
            for at in range(16):
                spot = pl.ds(pl.multiple_of(at * 96 + 48 * core, 16), 48)
                source = pieces[0].at[at * 48 : (at + 1) * 48, cols]
                started.append(copies.start(source, whole.at[spot, cols]))
            continue
        own, ahead, far_left, far_right, behind = pieces
        far, shifted = far_left, cols
        if cols.start >= SPLIT:
            far, shifted = far_right, slice(cols.start - SPLIT, cols.stop - SPLIT)
        for o in range(4):
            part = slice(o * 48, (o + 1) * 48)
            for q in range(4):
                along = lax.rem(row + o, 4) * 4 + lax.rem(col + q, 4)
                across = lax.rem(row + q, 4) * 4 + lax.rem(col + o, 4)
                at = along + core * (across - along)
                spot = pl.ds(pl.multiple_of(at * 96 + 48 * core, 16), 48)
                if q == 2:
                    source = far.at[part, shifted]
                else:
                    source = {0: own, 1: ahead, 3: behind}[q].at[part, cols]
                started.append(copies.start(source, whole.at[spot, cols]))
    return started


def forward_kernel(last, *refs):
    refs = list(refs)

    def take(n):
        taken, refs[:n] = refs[:n], []
        return taken

    where_ref, ends = take(2)
    if last:
        chunks, own_in, other_in = take(4), take(1), take(1)
        taps_ref, taps_state_ref, heads_ref, gain_ref = take(4)
    else:
        own_in, other_in, (heads_ref,) = take(5), take(5), take(1)
    normed_out, read_out, y_out, starts_out, gg_out = take(5)
    if last:
        dscaled_out, stats, mixed_out = take(3)
    else:
        outs = take(4)
        taps_ref, taps_state_ref, gain_ref = take(3)
    normed, read, y_all, starts, gated_gain, whole = take(6)
    x_pad, state_pad, x_conv, state_conv, hidden, sems, held_rows = take(7)
    if last:
        dscaled, mixed = take(2)
    copies = Copies(sems)
    place, core = where_ref[0], where_ref[1]
    weights = (own_in, other_in)
    if last:
        load_in = place_blocks(copies, where_ref, weights, whole, BOTH)
        load_rest = place_blocks(copies, where_ref, weights, whole, OUT)
    else:
        load_rows = [
            copies.start(ends.at[k, 0], held_rows.at[rows_at(k), :]) for k in range(BLOCKS)
        ]
        load_first = place_blocks(copies, where_ref, weights, whole, LEFT)
        load_in = place_blocks(copies, where_ref, weights, whole, RIGHT)
        for load in load_rows + load_first:
            load.wait()
        small_params(place, whole.at[:, MISC], heads_ref, taps_ref, taps_state_ref, gain_ref)
    for k, offset in enumerate((0, 3, 1, 2)):
        rows = rows_at(lax.rem(place + offset, 4))
        v = (chunks[k][...] if last else held_rows[rows, :]).astype(F32)
        q = lax.rsqrt(jnp.mean(v * v, axis=1, keepdims=True) + EPS)
        normed[rows, :] = (v * q * gain_ref[...]).astype(BF)
    copies.store(normed, normed_out)
    if last:
        load_rows = [
            copies.start(ends.at[k, 1], held_rows.at[rows_at(k), :]) for k in range(BLOCKS)
        ]
    for load in load_in:
        load.wait()
    read[...] = dot_nn(normed[...], whole[:, BOTH])
    copies.store(read, read_out)
    if last:
        for load in load_rest + load_rows:
            load.wait()
        dscaled[...] = dot_nn(held_rows[...], whole[:, OUT])
        copies.store(dscaled, dscaled_out)
    x_pad[:PAD, :] = jnp.zeros((PAD, CHANNELS), F32)
    x_pad[PAD:, :] = read[:, X]
    state_pad[:PAD, :] = jnp.zeros((PAD, 2 * STATES), F32)
    state_pad[PAD:, :] = read[:, STATE]
    hidden[...] = jnp.zeros_like(hidden)
    conv_rows(x_pad, taps_ref, x_conv)
    conv_rows(state_pad, taps_state_ref, state_conv)

    def block(b, carry):
        rows = rows_at(b)
        state_u = state_conv[rows, :]
        state = state_u * sigmoid(state_u)
        keys, reads = state[:, :STATES].astype(BF), state[:, STATES:].astype(BF)
        keys_t = jnp.transpose(state[:, :STATES]).astype(BF)
        _, step, _, summed, summed_t = step_terms(read[rows, MISC], heads_ref)
        meets = dot_nt(reads, keys)
        causal = iota((BLOCK, BLOCK), 0) >= iota((BLOCK, BLOCK), 1)
        squares = jnp.zeros((BLOCK, 128), F32)
        crosses = jnp.zeros((BLOCK, 128), F32)
        for p in range(PAIRS):
            cols = slice(p * 128, (p + 1) * 128)
            u = x_conv[rows, cols]
            x = u * sigmoid(u)
            weighted = x * spread(step, 2 * p)
            summed_wide = spread(summed, 2 * p)
            grown = jnp.exp(summed_wide)
            to_end = jnp.exp(summed_wide[BLOCK - 1 : BLOCK, :] - summed_wide)
            mixes = []
            for h in (2 * p, 2 * p + 1):
                gaps = summed[:, h : h + 1] - summed_t[h : h + 1, :]
                mixes.append((jnp.exp(jnp.where(causal, gaps, NEG)) * meets).astype(BF))
            within = dot_nn(
                jnp.concatenate(mixes, axis=1), side_by_side(weighted).astype(BF)
            )
            held = hidden[:, cols]
            held_low = held.astype(BF)
            starts[b, :, cols] = held_low
            y = within + grown * dot_nn(reads, held_low) + x * taps_ref[6:7, cols]
            hidden[:, cols] = grown[BLOCK - 1 : BLOCK, :] * held + dot_nn(
                keys_t, (to_end * weighted).astype(BF)
            )
            y_all[rows, cols] = y
            z = read[rows, Z.start + p * 128 : Z.start + (p + 1) * 128]
            gated = y * z * sigmoid(z)
            squares = squares + gated * gated
            gained = gated * taps_ref[5:6, cols]
            gated_gain[rows, cols] = gained.astype(BF)
            if last:
                crosses = crosses + gained * dscaled[rows, cols]
        square = jnp.sum(squares, axis=1, keepdims=True)
        upper, lower = two_parts(square)
        lane = iota((BLOCK, 128), 1)
        zero = jnp.zeros((BLOCK, 128), F32)
        tail = jnp.where(
            lane == 0, upper.astype(F32), jnp.where(lane == 1, lower.astype(F32), zero)
        ).astype(BF)
        for o, out in enumerate(() if last else outs):

            @pl.when(b == lax.rem(place + o, 4))
            def _(out=out):
                out[:, D:] = tail

        if last:
            cross = jnp.sum(crosses, axis=1, keepdims=True)
            both = jnp.where(lane == 0, square, jnp.where(lane == 1, cross, zero))
            stats[:, rows] = jnp.transpose(both)[:8, :]
        return carry

    lax.fori_loop(0, BLOCKS, block, 0)
    copies.store(y_all, y_out)
    copies.store(starts, starts_out)
    copies.store(gated_gain, gg_out)
    for at in range(0, D, PART):
        cols = slice(at, at + PART)
        part = dot_nt(gated_gain[...], whole[cols, OUT]).astype(BF)
        target = mixed if last else held_rows
        target[:, cols] = part
    if last:
        copies.store(mixed, mixed_out)
    else:
        for o in range(4):
            outs[o][:, :D] = held_rows[rows_at(lax.rem(place + o, 4)), :]
    copies.finish()


def in_hbm(shapes):
    return [pltpu.HBM(k.shape, k.dtype) for k in shapes]


def forward_call(where, ends, chunks, weights):
    last = len(chunks) > 0
    kept = [
        shape(SEQ, D, dtype=BF),
        shape(SEQ, READ),
        shape(SEQ, CHANNELS),
        shape(BLOCKS, STATES, CHANNELS, dtype=BF),
        shape(SEQ, CHANNELS, dtype=BF),
    ]
    out_shape, out_specs = in_hbm(kept), [HBM] * 5
    scratch = [pltpu.VMEM(k.shape, k.dtype) for k in kept] + [pltpu.VMEM((D, WIDE), BF)]
    scratch += [
        pltpu.VMEM((PAD + SEQ, CHANNELS), F32),
        pltpu.VMEM((PAD + SEQ, 2 * STATES), F32),
        pltpu.VMEM((SEQ, CHANNELS), F32),
        pltpu.VMEM((SEQ, 2 * STATES), F32),
        pltpu.VMEM((STATES, CHANNELS), F32),
        pltpu.SemaphoreType.DMA((96,)),
        pltpu.VMEM((SEQ, D), BF),
    ]
    if last:
        args = (where, ends, *chunks, *weights)
        in_specs = [SMEM, ANY] + [VMEM] * 4 + [ANY] * 2 + [VMEM] * 4
        more = [shape(SEQ, CHANNELS), shape(SEQ, D, dtype=BF)]
        out_shape += in_hbm(more[:1]) + [shape(8, SEQ)] + in_hbm(more[1:])
        out_specs += [HBM, VMEM, HBM]
        scratch += [pltpu.VMEM(k.shape, k.dtype) for k in more]
    else:
        args = (where, ends, *weights)
        in_specs = [SMEM, ANY] + [ANY] * 10 + [VMEM]
        out_shape += [shape(BLOCK, SENT, dtype=BF)] * 4 + list(SMALL)
        out_specs += [VMEM] * 7

    def kernel(*refs):
        forward_kernel(last, *refs)

    return pl.pallas_call(
        kernel,
        out_shape=out_shape,
        in_specs=in_specs,
        out_specs=out_specs,
        scratch_shapes=scratch,
        compiler_params=limit(VMEM_LIMIT),
        cost_estimate=cost(20 * 10**9, 24 * 10**6),
        name="layer_forward",
    )(*args)


def scaled_rows(rows_grad, factor):
    return (rows_grad.astype(F32) * factor).astype(BF)


def misc_parts(grad_small):
    taps_low = grad_small[0:8, 0:CHANNELS].astype(BF)
    lane, rank = iota((128, 8), 0), iota((128, 8), 1)
    lines = jnp.zeros((384, 128), F32)
    for half in range(2):
        put = ((lane == 12 + 6 * half + rank) & (rank < 6)).astype(BF)
        lines = lines + dot_nt(select_lines(half), dot_nn(put, taps_low).astype(BF))
    put = ((lane == 25 + rank) & (rank < 5)).astype(BF)
    state_low = grad_small[0:8, CHANNELS : CHANNELS + 256].astype(BF)
    state_lines = dot_nn(put, state_low).astype(BF)
    put = ((lane == 30 + rank) & (rank < 3)).astype(BF)
    heads_low = grad_small[0:8, CHANNELS + 256 : CHANNELS + 384].astype(BF)
    head_lines = dot_nn(put, heads_low).astype(BF)
    row, head = iota((384, 128), 0), iota((384, 128), 1)
    head_rows = ((row - 96 * over_96(row) == head) & (head < HEADS)).astype(BF)
    return lines, state_lines, dot_nt(head_rows, head_lines)


def misc_tile(i, place, parts, grad_small):
    lines, state_lines, head_part = parts
    misc = head_part + dot_nt(select_state(384, i * 384), state_lines)
    misc = misc + jnp.where(place == i, lines, 0.0)
    gains = grad_small[8:9, i * 384 : (i + 1) * 384]
    return misc + jnp.transpose(jnp.where(iota((128, 384), 0) == 24, gains, 0.0))


def backward_kernel(last, *refs):
    refs = list(refs)

    def take(n):
        taken, refs[:n] = refs[:n], []
        return taken

    (where_ref,) = take(1)
    normed_in, read_in, y_in, starts_in, gated_gain_in = take(5)
    weights = (take(1), take(1)) if last else (take(5), take(5))
    taps_ref, taps_state_ref, heads_ref, gain_ref = take(4)
    if last:
        dscaled_in, cot = take(2)
        stat_parts = take(4)
    else:
        chunks = take(4)
    outs = take(4 if last else 1)
    (grad_small,) = take(1)
    mine_out, theirs_out = take(2)
    normed, read, y_all, starts, gated_gain, whole, dscaled = take(7)
    x_pad, state_pad, x_conv, state_conv, du_pad, dstate_pad = take(6)
    d_hidden, d_read, factors, sems = take(4)
    products, rows_grad, sent = take(3)
    grad_taps, grad_taps_state = grad_small.at[0:8, 0:CHANNELS], grad_small.at[0:8, 768:1024]
    grad_heads, grad_gain = grad_small.at[0:8, 1024:1152], grad_small.at[8:9, :]
    copies = Copies(sems)
    place, core = where_ref[0], where_ref[1]
    if not last:
        load_out = place_blocks(copies, where_ref, weights, whole, OUT)
    load_x = copies.start(read_in.at[:, X], read.at[:, X])
    load_ss = copies.start(read_in.at[:, SS], read.at[:, SS])
    if last:
        load_cot = [copies.start(cot.at[k, 1], sent.at[rows_at(k), :]) for k in range(BLOCKS)]
    du_pad[SEQ:, :] = jnp.zeros((PAD, CHANNELS), F32)
    dstate_pad[SEQ:, :] = jnp.zeros((PAD, 2 * STATES), F32)
    for ref in (d_hidden, grad_small):
        ref[...] = jnp.zeros_like(ref)
    if last:
        total = stat_parts[0][...] + stat_parts[1][...] + stat_parts[2][...] + stat_parts[3][...]
        factor = lax.rsqrt(total[0:1, :] / DI + EPS)
        cubed = factor * factor * factor / DI * total[1:2, :]
        row = iota((128, SEQ), 0)
        both = jnp.where(row == 0, factor, jnp.where(row == 1, cubed, 0.0))
        for b in range(BLOCKS):
            part = slice(b * BLOCK, (b + 1) * BLOCK)
            factors[part, :] = jnp.transpose(both[:, part])
        for k in range(BLOCKS):
            rows = slice(k * BLOCK, (k + 1) * BLOCK)
            load_cot[k].wait()
            rows_grad[rows, :] = scaled_rows(sent[rows, :], factors[rows, 0:1])
    else:
        for offset, chunk in zip((0, 3, 1, 2), chunks):
            rows = rows_at(lax.rem(place + offset, 4))
            rows_grad[rows, :] = chunk[:, :D]
            tail = chunk[:, D:].astype(F32)
            factor = tail[:, 0:1] + tail[:, 1:2]
            cross = tail[:, 2:3] + tail[:, 3:4]
            lane = iota((BLOCK, 128), 1)
            cubed = factor * factor * factor / DI * cross
            factors[rows, :] = jnp.where(lane == 0, factor, jnp.where(lane == 1, cubed, 0.0))
        for load in load_out:
            load.wait()
        dscaled[...] = dot_nn(rows_grad[...], whole[:, OUT])
        rows_grad[...] = scaled_rows(rows_grad[...], factors[:, 0:1])
    load_x.wait()
    load_rows = [
        copies.start(read_in.at[:, Z], read.at[:, Z]),
        copies.start(y_in, y_all),
        copies.start(starts_in, starts),
    ]
    if last:
        load_rows.append(copies.start(dscaled_in, dscaled))
    x_pad[:PAD, :] = jnp.zeros((PAD, CHANNELS), F32)
    x_pad[PAD:, :] = read[:, X]
    load_ss.wait()
    state_pad[:PAD, :] = jnp.zeros((PAD, 2 * STATES), F32)
    state_pad[PAD:, :] = read[:, STATE]
    conv_rows(x_pad, taps_ref, x_conv)
    conv_rows(state_pad, taps_state_ref, state_conv)
    for load in load_rows:
        load.wait()
    load_late = [
        copies.start(normed_in, normed),
        copies.start(gated_gain_in, gated_gain),
    ]
    for cols in (BOTH,) if last else (LEFT, BETWEEN):
        load_late += place_blocks(copies, where_ref, weights, whole, cols)

    def block(turn, carry):
        b = BLOCKS - 1 - turn
        rows = rows_at(b)
        state_u = state_conv[rows, :]
        state_s = sigmoid(state_u)
        state = state_u * state_s
        keys, reads = state[:, :STATES].astype(BF), state[:, STATES:].astype(BF)
        reads_t = jnp.transpose(state[:, STATES:]).astype(BF)
        raised, step, log_decay, summed, summed_t = step_terms(read[rows, MISC], heads_ref)
        meets_t = dot_nt(keys, reads)
        causal_t = iota((BLOCK, BLOCK), 1) >= iota((BLOCK, BLOCK), 0)
        fac = factors[rows, :][:, 0:1]
        cub = factors[rows, :][:, 1:2]
        d_meets_t = jnp.zeros((BLOCK, BLOCK), F32)
        d_keys = jnp.zeros((BLOCK, STATES), F32)
        d_reads = jnp.zeros((BLOCK, STATES), F32)
        head_sums = jnp.zeros((2 * BLOCK, 128), F32)
        last_row = iota((BLOCK, 128), 0) == BLOCK - 1
        for p in range(PAIRS):
            cols = slice(p * 128, (p + 1) * 128)
            u = x_conv[rows, cols]
            us = sigmoid(u)
            x = u * us
            step_wide = spread(step, 2 * p)
            summed_wide = spread(summed, 2 * p)
            grown = jnp.exp(summed_wide)
            end = grown[BLOCK - 1 : BLOCK, :]
            to_end = jnp.exp(summed_wide[BLOCK - 1 : BLOCK, :] - summed_wide)
            skip = taps_ref[6:7, cols]
            gain = taps_ref[5:6, cols]
            z = read[rows, Z.start + p * 128 : Z.start + (p + 1) * 128]
            zs = sigmoid(z)
            z_act = z * zs
            y = y_all[rows, cols]
            gated = y * z_act
            incoming = dscaled[rows, cols]
            lifted = gated * fac
            grad_taps[5:6, cols] += jnp.sum(incoming * lifted, axis=0, keepdims=True)
            d_gated = fac * (gain * incoming) - gated * cub
            dy = d_gated * z_act
            d_read[rows, Z.start + p * 128 : Z.start + (p + 1) * 128] = (d_gated * y * (zs + z_act * (1.0 - zs))).astype(BF)
            dy_low = dy.astype(BF)
            weighted = x * step_wide
            weighted_low = weighted.astype(BF)
            dy_grown = (dy * grown).astype(BF)
            held_low = starts[b, :, cols]
            dh = d_hidden[:, cols]
            dh_low = dh.astype(BF)
            d_reads = d_reads + dot_nt(dy_grown, held_low)
            kept = dot_nn(keys, dh_low) * to_end
            d_keys = d_keys + dot_nt((to_end * weighted).astype(BF), dh_low)
            decays = []
            for h in (2 * p, 2 * p + 1):
                gaps = summed_t[h : h + 1, :] - summed[:, h : h + 1]
                decays.append(jnp.exp(jnp.where(causal_t, gaps, NEG)))
            mixes = jnp.concatenate([(d * meets_t).astype(BF) for d in decays], axis=1)
            d_weighted = dot_nn(mixes, side_by_side(dy).astype(BF)) + kept
            d_mixes = dot_nt(side_by_side(weighted).astype(BF), dy_low)
            d_meets_t = d_meets_t + d_mixes[:BLOCK] * decays[0] + d_mixes[BLOCK:] * decays[1]
            dx = skip * dy + d_weighted * step_wide
            weighted_f = weighted_low.astype(F32)
            moved = dy_low.astype(F32) * (y - skip * x) - weighted_f * d_weighted
            extra = jnp.sum(weighted_f * kept, axis=0, keepdims=True) + end * jnp.sum(
                dh * held_low.astype(F32), axis=0, keepdims=True
            )
            moved = jnp.where(last_row, moved + extra, moved)
            upper, lower = two_parts(jnp.concatenate([moved, x * d_weighted], axis=0))
            picks = (
                iota((256, 128), 1) == 2 * p + (iota((256, 128), 0) % 128) // HEAD_DIM
            ).astype(BF)
            head_sums = head_sums + dot_nn(jnp.concatenate([upper, lower], axis=1), picks)
            grad_taps[6:7, cols] += jnp.sum(dy * x, axis=0, keepdims=True)
            du_pad[rows, cols] = dx * (us + x * (1.0 - us))
            d_hidden[:, cols] = end * dh + dot_nn(reads_t, dy_grown)
        d_reads = d_reads + dot_nn(jnp.transpose(d_meets_t).astype(BF), keys)
        d_keys = d_keys + dot_nn(d_meets_t.astype(BF), reads)
        d_state = jnp.concatenate([d_keys, d_reads], axis=1)
        d_state = d_state * (state_s + state * (1.0 - state_s))
        dstate_pad[rows, :] = d_state
        upper_tri = (iota((BLOCK, BLOCK), 1) >= iota((BLOCK, BLOCK), 0)).astype(F32)
        d_decay = dot_high(upper_tri, head_sums[:BLOCK])
        d_step = head_sums[BLOCK:] - d_decay * jnp.exp(heads_ref[1:2, :])
        d_raw = d_step * sigmoid(raised)
        d_read[rows, MISC] = d_raw.astype(BF)
        grad_heads[0:1, :] += jnp.sum(d_raw, axis=0, keepdims=True)
        grad_heads[1:2, :] += jnp.sum(d_decay * log_decay, axis=0, keepdims=True)
        return carry

    lax.fori_loop(0, BLOCKS, block, 0)

    def store_inner(start, cols, value):
        cols = slice(X.start + cols.start, X.start + cols.stop)
        d_read[start : start + BLOCK, cols] = value

    def store_state(start, cols, value):
        d_read[start : start + BLOCK, cols] = value

    conv_back(du_pad, x_pad, taps_ref, grad_taps, store_inner)
    conv_back(dstate_pad, state_pad, taps_state_ref, grad_taps_state, store_state)
    picks = (iota((CHANNELS, 128), 1) == iota((CHANNELS, 128), 0) // HEAD_DIM).astype(F32)
    grad_heads[2:3, :] = dot_high(grad_taps[...], picks)[6:7, :]
    for load in load_late:
        load.wait()
    for at in range(0, D, PART):
        cols = slice(at, at + PART)
        part = dot_nt(d_read[...], whole[cols, BOTH])
        total = jnp.sum(part * normed[:, cols].astype(F32), axis=0, keepdims=True)
        grad_gain[:, cols] = total / gain_ref[:, cols]
        sent[:, cols] = part.astype(BF)
    if last:
        for o, out in enumerate(outs):
            copies.store(sent.at[rows_at(lax.rem(place + o, 4)), :], out)
    else:
        copies.store(sent, outs[0])
    parts = misc_parts(grad_small)
    for i in range(4):
        lanes = slice(i * 384, (i + 1) * 384)
        shared = dot_tn(normed[:, lanes], d_read[...])
        for cols, value in (
            (STATE, shared[:, STATE]),
            (MISC, shared[:, MISC] + misc_tile(i, place, parts, grad_small)),
            (IN, shared[:, IN]),
            (OUT, dot_tn(rows_grad[:, lanes], gated_gain[...])),
        ):
            low = value.astype(BF)
            for k in range(8):
                at = (4 * i + k // 2) * 48
                products[k % 2, at : at + 48, cols] = low[k * 48 : (k + 1) * 48]
        rows = slice(i * 192, (i + 1) * 192)
        copies.store(products.at[1 - core, rows, :], theirs_out.at[rows, :])
        copies.store(products.at[core, rows, :], mine_out.at[rows, :])
    copies.finish()


def backward_call(where, kept, weights, taps, taps_state, heads, gain, last, extra):
    args = [where, *kept, *weights, taps, taps_state, heads, gain, *extra]
    in_specs = [SMEM] + [HBM] * 5 + [ANY] * len(weights) + [VMEM] * 4
    in_specs += [HBM, ANY] + [VMEM] * 4 if last else [VMEM] * 4
    out_shape = [
        *([pltpu.HBM((BLOCK, D), BF)] * 4 if last else [pltpu.HBM((SEQ, D), BF)]),
        shape(16, D),
        *[pltpu.HBM((SIDE, WIDE), BF)] * 2,
    ]
    out_specs = [HBM] * (len(out_shape) - 3) + [VMEM] + [HBM] * 2
    scratch = [pltpu.VMEM(k.shape, k.dtype) for k in kept] + [pltpu.VMEM((D, WIDE), BF)]
    scratch += [
        pltpu.VMEM((SEQ, CHANNELS), F32),
        pltpu.VMEM((PAD + SEQ, CHANNELS), F32),
        pltpu.VMEM((PAD + SEQ, 2 * STATES), F32),
        pltpu.VMEM((SEQ, CHANNELS), F32),
        pltpu.VMEM((SEQ, 2 * STATES), F32),
        pltpu.VMEM((PAD + SEQ, CHANNELS), F32),
        pltpu.VMEM((PAD + SEQ, 2 * STATES), F32),
        pltpu.VMEM((STATES, CHANNELS), F32),
        pltpu.VMEM((SEQ, READ), BF),
        pltpu.VMEM((SEQ, 128), F32),
        pltpu.SemaphoreType.DMA((128,)),
        pltpu.VMEM((2, SIDE, WIDE), BF),
        pltpu.VMEM((SEQ, D), BF),
        pltpu.VMEM((SEQ, D), BF),
    ]

    def kernel(*refs):
        backward_kernel(last, *refs)

    return pl.pallas_call(
        kernel,
        out_shape=out_shape,
        in_specs=in_specs,
        out_specs=out_specs,
        scratch_shapes=scratch,
        compiler_params=limit(VMEM_LIMIT),
        cost_estimate=cost(32 * 10**9, 30 * 10**6),
        name="layer_backward",
    )(*args)


def arrived(parts):
    return sum((part[...].astype(F32) for part in parts[1:]), parts[0][...].astype(F32))


def after_first_kernel(rows_ref, a, b, c, d, hidden, mixed, factor_out):
    total = arrived((a, b, c, d))
    mixed[...] = total[:, :D]
    square = total[:, D : D + 1] + total[:, D + 1 : D + 2]
    factor = lax.rsqrt(square / DI + EPS)
    factor_out[...] = jnp.broadcast_to(factor, (BLOCK, 128))
    hidden[...] = (rows_ref[...].astype(F32) + factor * total[:, :D]).astype(BF)


def after_first_call(rows, parts):
    return pl.pallas_call(
        after_first_kernel,
        out_shape=[shape(BLOCK, D, dtype=BF), shape(BLOCK, D), shape(BLOCK, 128)],
        in_specs=[VMEM] * 5,
        out_specs=[VMEM] * 3,
        name="between_layers",
    )(rows, *parts)


def after_last_kernel(where_ref, rows_ref, mixed, a, b, c, d, result):
    total = a[...] + b[...] + c[...] + d[...]
    factor = lax.rsqrt(total[0:1, :] / DI + EPS)
    row = iota((128, SEQ), 0)
    column = jnp.zeros((BLOCK, 128), F32)
    for k in range(4):
        part = slice(k * BLOCK, (k + 1) * BLOCK)
        turned = jnp.transpose(jnp.where(row[:, part] == 0, factor[:, part], 0.0))
        column = jnp.where(where_ref[0] == k, turned, column)
    result[...] = rows_ref[...].astype(F32) + column[:, 0:1] * mixed[...].astype(F32)


def after_last_call(where, rows, mixed, stat_parts):
    return pl.pallas_call(
        after_last_kernel,
        out_shape=shape(BLOCK, D),
        in_specs=[SMEM] + [VMEM] * 6,
        out_specs=VMEM,
        name="last_rows",
    )(where, rows, mixed, *stat_parts)


def rows_back(rows_ref, parts, gain_ref, grad_ref):
    incoming = arrived(parts)
    v = rows_ref[...].astype(F32)
    q = lax.rsqrt(jnp.mean(v * v, axis=1, keepdims=True) + EPS)
    weighted = incoming * gain_ref[...]
    inner = jnp.sum(weighted * v, axis=1, keepdims=True)
    return grad_ref[...].astype(F32) + q * weighted - v * (q * q * q / D * inner)


def back_last_kernel(rows_ref, a, b, c, d, gain_ref, grad_ref, mixed_ref, factor_ref, out):
    low = rows_back(rows_ref, (a, b, c, d), gain_ref, grad_ref).astype(BF)
    out[:, :D] = low
    cross = jnp.sum(low.astype(F32) * mixed_ref[...], axis=1, keepdims=True)
    factor = factor_ref[:, 0:1]
    pieces = [*two_parts(factor), *two_parts(cross)]
    lane = iota((BLOCK, 128), 1)
    tail = jnp.zeros((BLOCK, 128), F32)
    for k, piece in enumerate(pieces):
        tail = jnp.where(lane == k, piece.astype(F32), tail)
    out[:, D:] = tail.astype(BF)


def back_last_call(rows, parts, gain, grad, mixed, factor):
    return pl.pallas_call(
        back_last_kernel,
        out_shape=shape(BLOCK, SENT, dtype=BF),
        in_specs=[VMEM] * 9,
        out_specs=VMEM,
        name="between_layers_back",
    )(rows, *parts, gain, grad, mixed, factor)


def back_first_kernel(rows_ref, incoming, gain_ref, grad_ref, out):
    out[...] = rows_back(rows_ref, (incoming,), gain_ref, grad_ref[:, :D])


def back_first_call(rows, incoming, gain, grad):
    return pl.pallas_call(
        back_first_kernel,
        out_shape=shape(BLOCK, D),
        in_specs=[VMEM] * 4,
        out_specs=VMEM,
        name="first_rows_back",
    )(rows, incoming, gain, grad)


def params_kernel(where_ref, misc, heads_ref, taps, taps_state, gain):
    small_params(where_ref[0], misc, heads_ref, taps, taps_state, gain)


def params_call(where, misc, heads):
    return pl.pallas_call(
        params_kernel,
        out_shape=SMALL,
        in_specs=[SMEM, VMEM, VMEM],
        out_specs=[VMEM] * 3,
        compiler_params=limit(16),
        name="small_parameters",
    )(where, misc, heads)


def both_kernel(where_ref, mine, given, *outs):
    if len(outs) == 1:
        outs[0][...] = (mine[...].astype(F32) + given[...].astype(F32)).astype(BF)
        return
    core, row, col = where_ref[1], where_ref[2], where_ref[3]
    own, ahead, far_left, far_right, behind, parts = outs
    for i in range(4):
        for j in range(4):
            rows = slice((4 * i + j) * 48, (4 * i + j + 1) * 48)
            total = (mine[rows, :].astype(F32) + given[rows, :].astype(F32)).astype(BF)
            along, across = lax.rem(i - row + 4, 4), lax.rem(j - col + 4, 4)
            o = along + core * (across - along)
            q = across + core * (along - across)
            parts[o, pl.ds(pl.multiple_of(q * 48, 16), 48), :] = total
    own[...] = parts[0]
    ahead[...] = parts[1]
    far_left[...] = parts[2, :, LEFT]
    far_right[...] = parts[2, :, RIGHT]
    behind[...] = parts[3]


def ring_shapes(rows):
    whole = shape(rows, WIDE, dtype=BF)
    left, right = shape(rows, SPLIT, dtype=BF), shape(rows, WIDE - SPLIT, dtype=BF)
    return [whole, whole, left, right, whole]


def both_call(where, mine, given, relative):
    out_shape = ring_shapes(192) if relative else [shape(SIDE, WIDE, dtype=BF)]
    return pl.pallas_call(
        both_kernel,
        out_shape=out_shape,
        in_specs=[SMEM] + [VMEM] * 2,
        out_specs=[VMEM] * len(out_shape),
        scratch_shapes=[pltpu.VMEM((4, 192, WIDE), BF)] if relative else [],
        compiler_params=limit(28),
        cost_estimate=cost(10**6, 10**4),
        name="both_cores_grads",
    )(where, mine, given)


def passed_kernel(ahead, behind, left, right, out_ahead, out_behind):
    out_ahead[:, LEFT] = (ahead[:, LEFT].astype(F32) + left[...].astype(F32)).astype(BF)
    out_ahead[:, RIGHT] = ahead[:, RIGHT]
    out_behind[:, LEFT] = behind[:, LEFT]
    out_behind[:, RIGHT] = (behind[:, RIGHT].astype(F32) + right[...].astype(F32)).astype(BF)


def passed_call(ahead, behind, left, right):
    return pl.pallas_call(
        passed_kernel,
        out_shape=[shape(*ahead.shape, dtype=BF)] * 2,
        in_specs=[VMEM] * 4,
        out_specs=[VMEM] * 2,
        compiler_params=limit(16),
        cost_estimate=cost(10**6, 10**4),
        name="grads_passed_on",
    )(ahead, behind, left, right)


def halfway_kernel(a, b, c, own, ahead, far_left, far_right, behind):
    total = arrived((a, b, c)).astype(BF)
    own[...] = total[:48]
    ahead[...] = total[48:96]
    far_left[...] = total[96:144, LEFT]
    far_right[...] = total[96:144, RIGHT]
    behind[...] = total[144:]


def halfway_call(parts):
    return pl.pallas_call(
        halfway_kernel,
        out_shape=ring_shapes(48),
        in_specs=[VMEM] * 3,
        out_specs=[VMEM] * 5,
        compiler_params=limit(20),
        name="grads_halfway",
    )(*parts)


def shard_kernel(where_ref, a, b, c, share_1, own, given):
    share_0 = arrived((a, b, c))
    is_first = where_ref[1] == 0
    other = share_1[...].astype(F32)
    own[...] = jnp.where(is_first, share_0, other)
    given[...] = jnp.where(is_first, other, share_0).astype(BF)


def shard_call(where, parts, share_1):
    return pl.pallas_call(
        shard_kernel,
        out_shape=[shape(48, WIDE), shape(48, WIDE, dtype=BF)],
        in_specs=[SMEM] + [VMEM] * 4,
        out_specs=[VMEM] * 2,
        name="grads_shard",
    )(where, *parts, share_1)


def swap(v):
    return lax.ppermute(v, "section", [(0, 1), (1, 0)])


def turn(v, by, axis="tensor"):
    return lax.ppermute(v, axis, [(i, (i + by) % 4) for i in range(4)])


def spread_rows(v):
    return (v, turn(v, 1), turn(v, -1), turn(v, 2))


def meet(parts, axis="tensor"):
    own, ahead, across, behind = parts
    return (own, turn(ahead, 1, axis), turn(behind, -1, axis), turn(across, 2, axis))


def from_ring(v, axis):
    return (v, turn(v, -1, axis), turn(v, 2, axis), turn(v, 1, axis))


def ring(v, by, phase):
    pairs = []
    for s in range(2):
        for a in range(4):
            for b in range(4):
                to = ((a + by) % 4, b) if s == phase else (a, (b + by) % 4)
                pairs.append((16 * s + 4 * a + b, 16 * s + 4 * to[0] + to[1]))
    return lax.ppermute(v, ("section", *DP), pairs)


def around(v, phase):
    ahead, behind = lax.optimization_barrier((ring(v, -1, phase), ring(v, 1, phase)))
    return (
        v,
        ahead,
        ring(ahead[:, :SPLIT], -1, phase),
        ring(behind[:, SPLIT:], 1, phase),
        behind,
    )


def gather_by_turns(main, rest):
    own, ahead, far_left, far_right, behind = around(main, 0)
    far = jnp.concatenate([far_left, far_right], axis=1)
    rest = (rest, ring(rest, -1, 0), ring(rest, 2, 0), ring(rest, 1, 0))
    rows = [
        jnp.concatenate(pair, axis=1) for pair in zip(rest, (own, ahead, far, behind))
    ]
    return around(jnp.concatenate(rows, axis=0), 1)


def pick(v, index, axis):
    return lax.dynamic_index_in_dim(v, index, axis, keepdims=False)


def tie(*values):
    return lax.optimization_barrier(values)


def shards(
    section_ends,
    norm_gain,
    proj_inner,
    proj_step,
    proj_state,
    conv_inner,
    conv_state,
    gate_gain,
    head_params,
    proj_output,
):
    core = lax.axis_index("section")
    place = lax.axis_index("tensor")
    is_first = core == 0
    where = jnp.stack(
        [place, core, lax.axis_index("dp_0"), lax.axis_index("dp_1")]
    ).astype(jnp.int32)

    def by_layer_of(keep, got):
        return jnp.where(is_first, keep, got), jnp.where(is_first, got, keep)

    def by_layer(halves):
        return by_layer_of(pick(halves, core, 0), swap(pick(halves, 1 - core, 0)))

    main = jnp.concatenate([proj_inner[0].reshape(96, 2 * CHANNELS), proj_output[0].T], axis=1)
    main_0, main_1 = by_layer(main.reshape(2, 48, MAIN))
    main_0, heads_got, *small = tie(
        main_0,
        swap(head_params[0]),
        proj_state[0],
        norm_gain[0],
        conv_inner[0],
        gate_gain[0],
        conv_state[0],
    )
    packed = jnp.concatenate(
        [
            *[v.reshape(-1) for v in small],
            jnp.zeros((32 * 256 - 6144 - 332,), BF),
        ]
    ).reshape(32, 256)
    turned = jnp.stack(from_ring(packed, "tensor") * 2)
    filled = lax.dynamic_slice_in_dim(turned, lax.rem(4 - place, 4), 4, 0).reshape(4, 32 * 256)
    state_rows = filled[:, :6144].reshape(96, 256)
    norm_col = filled[:, 6144:6168].reshape(96, 1)
    inner_cols = filled[:, 6168:6408].reshape(4, 5, 48).transpose(0, 2, 1).reshape(192, 5)
    gate_col = filled[:, 6408:6456].reshape(192, 1)
    both = jnp.concatenate([inner_cols, gate_col], axis=1)
    both = both.reshape(2, 96, 6).transpose(1, 0, 2).reshape(96, 12)
    state_cols = filled[:, 6456:6476].reshape(4, 5, 4).transpose(0, 2, 1).reshape(16, 5)
    state_cols = jnp.pad(state_cols, ((0, 80), (0, 0)))
    misc = jnp.concatenate(
        [proj_step[0], both, norm_col, state_cols, jnp.zeros((96, 128 - 30), BF)], axis=1
    )

    rest_0, rest_1 = by_layer(jnp.concatenate([state_rows, misc], axis=1).reshape(2, 48, 384))

    ends = section_ends[0]
    got_rows = swap(pick(ends, 1 - core, 0))
    rows_in = jnp.where(is_first, ends[0], got_rows)
    cot = jnp.where(is_first, got_rows, ends[1])
    heads = [
        jnp.pad(v.astype(F32), ((0, 5), (0, 128 - HEADS)))
        for v in by_layer_of(head_params[0], heads_got)
    ]
    ends_all = lax.all_gather(jnp.stack([rows_in, cot]), "tensor", axis=0)
    own_pieces = gather_by_turns(main_0, rest_0)
    shard_1 = jnp.concatenate([rest_1, main_1], axis=1)
    shard_1, *rest = tie(shard_1, *heads, *own_pieces)
    heads, own_pieces = rest[:2], rest[2:]
    full_1 = lax.all_gather(shard_1, DP, axis=0, tiled=True)
    pieces_0 = (*own_pieces, *[swap(v) for v in own_pieces])
    first = forward_call(where, ends_all, (), (*pieces_0, heads[0]))
    kept_0, sent_0, small_0 = first[:5], first[5:9], first[9:]
    weights_0 = (pieces_0, small_0[0], small_0[1], heads[0], small_0[2])
    own_1, *met_0 = tie(full_1, *meet(sent_0))
    other_1 = swap(own_1)
    order = (own_1[:, MISC].reshape(16, 48, 128), other_1[:, MISC].reshape(16, 48, 128))
    misc_1 = jnp.where(is_first, jnp.stack(order, axis=1), jnp.stack(order[::-1], axis=1))
    small_1 = params_call(where, misc_1.reshape(D, 128), heads[1])
    weights_1 = ((own_1, other_1), small_1[0], small_1[1], heads[1], small_1[2])
    hidden, mixed_0, factor_0 = after_first_call(rows_in, met_0)
    kept_1 = forward_call(
        where, ends_all, spread_rows(hidden), (own_1, other_1, *weights_1[1:])
    )
    dscaled_1, stats, mixed_1 = kept_1[5:]
    stat_parts = spread_rows(stats)
    met_1 = lax.psum_scatter(mixed_1, "tensor", scatter_dimension=0, tiled=True)
    back_1 = backward_call(
        where, kept_1[:5], *weights_1, True, (dscaled_1, ends_all, *stat_parts)
    )
    met_1, *back_1 = tie(met_1, *back_1)
    payload_1 = both_call(where, back_1[5], swap(back_1[6]), False)[0]
    payload_1, *d_met_1 = tie(payload_1, *meet(back_1[:4]))
    grad_1 = back_last_call(hidden, d_met_1, weights_1[4], cot, mixed_0, factor_0)
    payload_1, met_1, grad_1 = tie(payload_1, met_1, grad_1)
    share_1 = lax.psum_scatter(payload_1, DP, scatter_dimension=0, tiled=True)
    result = after_last_call(where, hidden, met_1, stat_parts)
    result, *chunks_0 = tie(result, *spread_rows(grad_1))
    back_0 = backward_call(where, kept_0, *weights_0, False, chunks_0)
    parts_0 = both_call(where, back_0[2], swap(back_0[3]), True)
    own, ahead, far_left, far_right, behind = parts_0
    ahead, behind = passed_call(
        ahead, behind, ring(far_left, 1, 0), ring(far_right, -1, 0)
    )
    share_1, rows_0, ahead, behind = tie(share_1, back_0[0], ahead, behind)
    ahead, behind = tie(ring(ahead, 1, 0), ring(behind, -1, 0))
    pieces = halfway_call((own, ahead, behind))
    met_0 = lax.psum_scatter(rows_0, "tensor", scatter_dimension=0, tiled=True)
    own, ahead, far_left, far_right, behind = pieces
    ahead, behind = passed_call(
        ahead, behind, ring(far_left, 1, 1), ring(far_right, -1, 1)
    )
    met_0, ahead, behind = tie(met_0, ahead, behind)
    half_met = (own, ring(ahead, 1, 1), ring(behind, -1, 1))
    grad_0 = back_first_call(rows_in, met_0, weights_0[4], grad_1)
    rows_got = swap(jnp.where(is_first, result, grad_0))
    section_rows = jnp.where(
        is_first, jnp.stack([grad_0, rows_got]), jnp.stack([rows_got, result])
    )
    share_own, share_given = shard_call(where, half_met, share_1)
    share_got = swap(share_given).astype(F32)
    whole = jnp.where(
        is_first,
        jnp.concatenate([share_own, share_got], axis=0),
        jnp.concatenate([share_got, share_own], axis=0),
    )
    grad_inner = whole[:, IN].reshape(96, 2, CHANNELS)
    grad_output = whole[:, OUT].T
    misc = whole[:, MISC]
    grad_step = misc[:, :HEADS]
    grad_heads = misc[:HEADS, 30:33].T
    to_send = jnp.concatenate(
        [
            whole[:, STATE].reshape(4, 6144),
            misc[:, 24].reshape(4, 24),
            misc[:, 12:24].reshape(96, 2, 6).transpose(1, 0, 2).reshape(4, 48 * 6),
            misc[:16, 25:30].reshape(4, 20),
            jnp.zeros((4, 32 * 256 - 6144 - 332), F32),
        ],
        axis=1,
    ).reshape(4, 32, 256)
    pieces = [pick(to_send, lax.rem(place + o, 4), 0) for o in range(4)]
    section_rows, *met = tie(section_rows, *meet(pieces))
    total = (met[0] + met[1] + met[2] + met[3]).reshape(-1)
    grad_state = total[:6144].reshape(24, 256)
    grad_norm = total[6144:6168]
    inner_lines = total[6168:6456].reshape(48, 6).T
    grad_conv_inner = inner_lines[:5]
    grad_gate = inner_lines[5]
    grad_conv_state = total[6456:6476].reshape(4, 5).T
    return (
        section_rows[None],
        grad_norm[None],
        grad_inner[None],
        grad_step[None],
        grad_state[None],
        grad_conv_inner[None],
        grad_conv_state[None],
        grad_gate[None],
        grad_heads[None],
        grad_output[None],
    )


def solution(mesh):
    split = Mesh(
        mesh.devices.reshape(mesh.shape["section"], 4, 4, mesh.shape["tensor"]),
        ("section", "dp_0", "dp_1", "tensor"),
    )
    return jax.shard_map(
        shards,
        mesh=split,
        in_specs=(
            P("section", None, DP_TENSOR, None),
            P("section", DP_TENSOR),
            P("section", DP, None, "tensor"),
            P("section", DP, "tensor"),
            P("section", DP_TENSOR, None),
            P("section", None, DP_TENSOR),
            P("section", None, DP_TENSOR),
            P("section", DP_TENSOR),
            P("section", None, "tensor"),
            P("section", "tensor", DP),
        ),
        out_specs=(
            P("section", None, DP_TENSOR, None),
            P("section", DP_TENSOR),
            P("section", DP, None, "tensor"),
            P("section", DP, "tensor"),
            P("section", DP_TENSOR, None),
            P("section", None, DP_TENSOR),
            P("section", None, DP_TENSOR),
            P("section", DP_TENSOR),
            P("section", None, "tensor"),
            P("section", "tensor", DP),
        ),
        check_vma=False,
    )
```

```python
import jax
import jax.numpy as jnp
from jax import lax
from jax.experimental import pallas as pl
from jax.experimental.pallas import tpu as pltpu
from jax.sharding import Mesh
from jax.sharding import PartitionSpec as P

D = 1536
SEQ = 512
BLOCK = 128
BLOCKS = SEQ // BLOCK
STATES = 128
CHANNELS = 768
HEADS = 12
HEAD_DIM = 64
PAIRS = HEADS // 2
DI = 3072
PAD = 8
EPS = 1e-05
NEG = -1e30
DP = ("dp_0", "dp_1")
DP_TENSOR = ("dp_0", "dp_1", "tensor")
SENT = D + 128
BF = jnp.bfloat16
F32 = jnp.float32
HIGH = lax.Precision.HIGHEST
VMEM = pl.BlockSpec(memory_space=pltpu.VMEM)
SMEM = pl.BlockSpec(memory_space=pltpu.SMEM)
HBM = pl.BlockSpec(memory_space=pltpu.HBM)
ANY = pl.BlockSpec(memory_space=pl.ANY)
SIDE = D // 2
WIDE = 2 * CHANNELS + CHANNELS + 384
SS = slice(0, 384)
STATE = slice(0, 256)
MISC = slice(256, 384)
Z = slice(384, 384 + CHANNELS)
X = slice(384 + CHANNELS, 384 + 2 * CHANNELS)
IN = slice(384, 384 + 2 * CHANNELS)
READ = 384 + 2 * CHANNELS
BOTH = slice(0, READ)
OUT = slice(READ, WIDE)
MAIN = 3 * CHANNELS
SPLIT = 2 * CHANNELS
PART = 256
LEFT, RIGHT = slice(0, SPLIT), slice(SPLIT, WIDE)
BETWEEN = slice(SPLIT, READ)
VMEM_LIMIT = 54


def shape(*dims, dtype=F32):
    return jax.ShapeDtypeStruct(dims, dtype)


def limit(megabytes):
    return pltpu.CompilerParams(vmem_limit_bytes=megabytes * 1024 * 1024)


def cost(flops, read):
    return pl.CostEstimate(flops=flops, bytes_accessed=read, transcendentals=0)


def dot_nn(left, right):
    return lax.dot_general(left, right, (((1,), (0,)), ((), ())), preferred_element_type=F32)


def dot_nt(left, right):
    return lax.dot_general(left, right, (((1,), (1,)), ((), ())), preferred_element_type=F32)


def dot_tn(left, right):
    return lax.dot_general(left, right, (((0,), (0,)), ((), ())), preferred_element_type=F32)


def dot_high(left, right):
    return lax.dot_general(
        left, right, (((1,), (0,)), ((), ())), precision=HIGH, preferred_element_type=F32
    )


def sigmoid(v):
    return 0.5 * jnp.tanh(0.5 * v) + 0.5


def softplus(v):
    return jnp.maximum(v, 0.0) + jnp.log1p(jnp.exp(-jnp.abs(v)))


def rows_at(index):
    return pl.ds(pl.multiple_of(index * BLOCK, BLOCK), BLOCK)


def lanes_at(index):
    return pl.ds(pl.multiple_of(index * 128, 128), 128)


def iota(shape, dim):
    return lax.broadcasted_iota(jnp.int32, shape, dim)


def two_parts(v):
    upper = v.astype(BF)
    lower = (v - upper.astype(F32)).astype(BF)
    return upper, lower


def lane_tiles(width):
    return [slice(at, at + 128) for at in range(0, width, 128)]


def conv_rows(padded, taps, out):
    for cols in lane_tiles(out.shape[1]):
        for start in range(0, SEQ, BLOCK):
            total = taps[4:5, cols] + taps[0:1, cols] * padded[start + 5 : start + 5 + BLOCK, cols]
            for k in range(1, 4):
                at = start + 5 + k
                total = total + taps[k : k + 1, cols] * padded[at : at + BLOCK, cols]
            out[start : start + BLOCK, cols] = total


def conv_back(padded_grad, padded, taps, grad_taps, store):
    for cols in lane_tiles(padded.shape[1]):
        sums = [jnp.zeros((1, 128), F32)] * 5
        for start in range(0, SEQ, BLOCK):
            own = padded_grad[start : start + BLOCK, cols]
            total = taps[3:4, cols] * own
            sums[4] = sums[4] + jnp.sum(own, axis=0, keepdims=True)
            for k in range(4):
                at = start + 5 + k
                sums[k] = sums[k] + jnp.sum(own * padded[at : at + BLOCK, cols], axis=0, keepdims=True)
                if k < 3:
                    at = start + 3 - k
                    total = total + taps[k : k + 1, cols] * padded_grad[at : at + BLOCK, cols]
            store(start, cols, total.astype(BF))
        for k in range(5):
            grad_taps[k : k + 1, cols] = sums[k]


def step_terms(raw, heads):
    valid = iota((BLOCK, 128), 1) < HEADS
    raised = jnp.where(valid, raw + heads[0:1, :], -30.0)
    step = softplus(raised)
    log_decay = -step * jnp.exp(heads[1:2, :])
    lower = (iota((BLOCK, BLOCK), 0) >= iota((BLOCK, BLOCK), 1)).astype(F32)
    summed = dot_high(lower, log_decay)
    return raised, step, log_decay, summed, jnp.transpose(summed)


def spread(values, head):
    first = iota((BLOCK, 128), 1) < HEAD_DIM
    return jnp.where(first, values[:, head : head + 1], values[:, head + 1 : head + 2])


def side_by_side(v):
    first = iota(v.shape, 1) < HEAD_DIM
    zero = jnp.zeros_like(v)
    return jnp.concatenate([jnp.where(first, v, zero), jnp.where(first, zero, v)], axis=0)


def over_96(v):
    return lax.shift_right_logical(v * 683, 16)


def select_lines(half):
    row, channel = iota((384, CHANNELS), 0), iota((384, CHANNELS), 1)
    return (channel == over_96(row) * 96 + row + 96 * half).astype(BF)


def select_state(rows, first):
    row, channel = iota((rows, 256), 0) + first, iota((rows, 256), 1)
    group = over_96(row)
    inside = row - 96 * group
    return ((inside < 16) & (channel == 16 * group + inside)).astype(BF)


def small_params(place, misc, heads_ref, taps, taps_state, gain):
    lines = misc[pl.ds(pl.multiple_of(place * 384, 128), 384), :]
    first = dot_tn(lines, select_lines(0))
    second = dot_tn(lines, select_lines(1))
    picks = (iota((128, CHANNELS), 0) == iota((128, CHANNELS), 1) // HEAD_DIM).astype(BF)
    skip = dot_nn(heads_ref[...].astype(BF), picks)
    taps[0:6, :] = first[12:18, :] + second[18:24, :]
    taps[6:7, :] = skip[2:3, :]
    taps[7:8, :] = jnp.zeros((1, CHANNELS), F32)
    taps_state[...] = jnp.zeros((8, 256), F32)
    taps_state[0:5, :] = dot_tn(misc[...], select_state(D, 0))[25:30, :]
    gain[...] = jnp.transpose(misc[...].astype(F32))[24:25, :]


SMALL = (shape(8, CHANNELS), shape(8, 256), shape(1, D))


class Copies:
    def __init__(self, sems):
        self.sems = sems
        self.count = 0
        self.pending = []

    def start(self, source, target):
        copy = pltpu.make_async_copy(source, target, self.sems.at[self.count])
        self.count += 1
        copy.start()
        return copy

    def store(self, source, target):
        self.pending.append(self.start(source, target))

    def finish(self):
        for copy in self.pending:
            copy.wait()


def place_blocks(copies, where_ref, parts, whole, cols):
    row, col = where_ref[2], where_ref[3]
    started = []
    for k, pieces in enumerate(parts):
        core = where_ref[1] if k == 0 else 1 - where_ref[1]
        if len(pieces) == 1:
            for at in range(16):
                spot = pl.ds(pl.multiple_of(at * 96 + 48 * core, 16), 48)
                source = pieces[0].at[at * 48 : (at + 1) * 48, cols]
                started.append(copies.start(source, whole.at[spot, cols]))
            continue
        own, ahead, far_left, far_right, behind = pieces
        far, shifted = far_left, cols
        if cols.start >= SPLIT:
            far, shifted = far_right, slice(cols.start - SPLIT, cols.stop - SPLIT)
        for o in range(4):
            part = slice(o * 48, (o + 1) * 48)
            for q in range(4):
                along = lax.rem(row + o, 4) * 4 + lax.rem(col + q, 4)
                across = lax.rem(row + q, 4) * 4 + lax.rem(col + o, 4)
                at = along + core * (across - along)
                spot = pl.ds(pl.multiple_of(at * 96 + 48 * core, 16), 48)
                if q == 2:
                    source = far.at[part, shifted]
                else:
                    source = {0: own, 1: ahead, 3: behind}[q].at[part, cols]
                started.append(copies.start(source, whole.at[spot, cols]))
    return started


def forward_kernel(last, *refs):
    refs = list(refs)

    def take(n):
        taken, refs[:n] = refs[:n], []
        return taken

    where_ref, ends = take(2)
    if last:
        chunks, own_in, other_in = take(4), take(1), take(1)
        taps_ref, taps_state_ref, heads_ref, gain_ref = take(4)
    else:
        own_in, other_in, (heads_ref,) = take(5), take(5), take(1)
    normed_out, read_out, y_out, starts_out, gg_out = take(5)
    if last:
        dscaled_out, stats, mixed_out = take(3)
    else:
        outs = take(4)
        taps_ref, taps_state_ref, gain_ref = take(3)
    normed, read, y_all, starts, gated_gain, whole = take(6)
    x_pad, state_pad, x_conv, state_conv, hidden, sems, held_rows = take(7)
    if last:
        dscaled, mixed = take(2)
    copies = Copies(sems)
    place, core = where_ref[0], where_ref[1]
    weights = (own_in, other_in)
    if last:
        load_in = place_blocks(copies, where_ref, weights, whole, BOTH)
        load_rest = place_blocks(copies, where_ref, weights, whole, OUT)
    else:
        load_rows = [
            copies.start(ends.at[k, 0], held_rows.at[rows_at(k), :]) for k in range(BLOCKS)
        ]
        load_first = place_blocks(copies, where_ref, weights, whole, LEFT)
        load_in = place_blocks(copies, where_ref, weights, whole, RIGHT)
        for load in load_rows + load_first:
            load.wait()
        small_params(place, whole.at[:, MISC], heads_ref, taps_ref, taps_state_ref, gain_ref)
    for k, offset in enumerate((0, 3, 1, 2)):
        rows = rows_at(lax.rem(place + offset, 4))
        v = (chunks[k][...] if last else held_rows[rows, :]).astype(F32)
        q = lax.rsqrt(jnp.mean(v * v, axis=1, keepdims=True) + EPS)
        normed[rows, :] = (v * q * gain_ref[...]).astype(BF)
    copies.store(normed, normed_out)
    if last:
        load_rows = [
            copies.start(ends.at[k, 1], held_rows.at[rows_at(k), :]) for k in range(BLOCKS)
        ]
    for load in load_in:
        load.wait()
    read[...] = dot_nn(normed[...], whole[:, BOTH])
    copies.store(read, read_out)
    if last:
        for load in load_rest + load_rows:
            load.wait()
        dscaled[...] = dot_nn(held_rows[...], whole[:, OUT])
        copies.store(dscaled, dscaled_out)
    x_pad[:PAD, :] = jnp.zeros((PAD, CHANNELS), F32)
    x_pad[PAD:, :] = read[:, X]
    state_pad[:PAD, :] = jnp.zeros((PAD, 2 * STATES), F32)
    state_pad[PAD:, :] = read[:, STATE]
    hidden[...] = jnp.zeros_like(hidden)
    conv_rows(x_pad, taps_ref, x_conv)
    conv_rows(state_pad, taps_state_ref, state_conv)

    def block(b, carry):
        rows = rows_at(b)
        state_u = state_conv[rows, :]
        state = state_u * sigmoid(state_u)
        keys, reads = state[:, :STATES].astype(BF), state[:, STATES:].astype(BF)
        keys_t = jnp.transpose(state[:, :STATES]).astype(BF)
        _, step, _, summed, summed_t = step_terms(read[rows, MISC], heads_ref)
        meets = dot_nt(reads, keys)
        causal = iota((BLOCK, BLOCK), 0) >= iota((BLOCK, BLOCK), 1)
        squares = jnp.zeros((BLOCK, 128), F32)
        crosses = jnp.zeros((BLOCK, 128), F32)
        for p in range(PAIRS):
            cols = slice(p * 128, (p + 1) * 128)
            u = x_conv[rows, cols]
            x = u * sigmoid(u)
            weighted = x * spread(step, 2 * p)
            summed_wide = spread(summed, 2 * p)
            grown = jnp.exp(summed_wide)
            to_end = jnp.exp(summed_wide[BLOCK - 1 : BLOCK, :] - summed_wide)
            mixes = []
            for h in (2 * p, 2 * p + 1):
                gaps = summed[:, h : h + 1] - summed_t[h : h + 1, :]
                mixes.append((jnp.exp(jnp.where(causal, gaps, NEG)) * meets).astype(BF))
            within = dot_nn(
                jnp.concatenate(mixes, axis=1), side_by_side(weighted).astype(BF)
            )
            held = hidden[:, cols]
            held_low = held.astype(BF)
            starts[b, :, cols] = held_low
            y = within + grown * dot_nn(reads, held_low) + x * taps_ref[6:7, cols]
            hidden[:, cols] = grown[BLOCK - 1 : BLOCK, :] * held + dot_nn(
                keys_t, (to_end * weighted).astype(BF)
            )
            y_all[rows, cols] = y
            z = read[rows, Z.start + p * 128 : Z.start + (p + 1) * 128]
            gated = y * z * sigmoid(z)
            squares = squares + gated * gated
            gained = gated * taps_ref[5:6, cols]
            gated_gain[rows, cols] = gained.astype(BF)
            if last:
                crosses = crosses + gained * dscaled[rows, cols]
        square = jnp.sum(squares, axis=1, keepdims=True)
        upper, lower = two_parts(square)
        lane = iota((BLOCK, 128), 1)
        zero = jnp.zeros((BLOCK, 128), F32)
        tail = jnp.where(
            lane == 0, upper.astype(F32), jnp.where(lane == 1, lower.astype(F32), zero)
        ).astype(BF)
        for o, out in enumerate(() if last else outs):

            @pl.when(b == lax.rem(place + o, 4))
            def _(out=out):
                out[:, D:] = tail

        if last:
            cross = jnp.sum(crosses, axis=1, keepdims=True)
            both = jnp.where(lane == 0, square, jnp.where(lane == 1, cross, zero))
            stats[:, rows] = jnp.transpose(both)[:8, :]
        return carry

    lax.fori_loop(0, BLOCKS, block, 0)
    copies.store(y_all, y_out)
    copies.store(starts, starts_out)
    copies.store(gated_gain, gg_out)
    for at in range(0, D, PART):
        cols = slice(at, at + PART)
        part = dot_nt(gated_gain[...], whole[cols, OUT]).astype(BF)
        target = mixed if last else held_rows
        target[:, cols] = part
    if last:
        copies.store(mixed, mixed_out)
    else:
        for o in range(4):
            outs[o][:, :D] = held_rows[rows_at(lax.rem(place + o, 4)), :]
    copies.finish()


def in_hbm(shapes):
    return [pltpu.HBM(k.shape, k.dtype) for k in shapes]


def forward_call(where, ends, chunks, weights):
    last = len(chunks) > 0
    kept = [
        shape(SEQ, D, dtype=BF),
        shape(SEQ, READ),
        shape(SEQ, CHANNELS),
        shape(BLOCKS, STATES, CHANNELS, dtype=BF),
        shape(SEQ, CHANNELS, dtype=BF),
    ]
    out_shape, out_specs = in_hbm(kept), [HBM] * 5
    scratch = [pltpu.VMEM(k.shape, k.dtype) for k in kept] + [pltpu.VMEM((D, WIDE), BF)]
    scratch += [
        pltpu.VMEM((PAD + SEQ, CHANNELS), F32),
        pltpu.VMEM((PAD + SEQ, 2 * STATES), F32),
        pltpu.VMEM((SEQ, CHANNELS), F32),
        pltpu.VMEM((SEQ, 2 * STATES), F32),
        pltpu.VMEM((STATES, CHANNELS), F32),
        pltpu.SemaphoreType.DMA((96,)),
        pltpu.VMEM((SEQ, D), BF),
    ]
    if last:
        args = (where, ends, *chunks, *weights)
        in_specs = [SMEM, ANY] + [VMEM] * 4 + [ANY] * 2 + [VMEM] * 4
        more = [shape(SEQ, CHANNELS), shape(SEQ, D, dtype=BF)]
        out_shape += in_hbm(more[:1]) + [shape(8, SEQ)] + in_hbm(more[1:])
        out_specs += [HBM, VMEM, HBM]
        scratch += [pltpu.VMEM(k.shape, k.dtype) for k in more]
    else:
        args = (where, ends, *weights)
        in_specs = [SMEM, ANY] + [ANY] * 10 + [VMEM]
        out_shape += [shape(BLOCK, SENT, dtype=BF)] * 4 + list(SMALL)
        out_specs += [VMEM] * 7

    def kernel(*refs):
        forward_kernel(last, *refs)

    return pl.pallas_call(
        kernel,
        out_shape=out_shape,
        in_specs=in_specs,
        out_specs=out_specs,
        scratch_shapes=scratch,
        compiler_params=limit(VMEM_LIMIT),
        cost_estimate=cost(20 * 10**9, 24 * 10**6),
        name="layer_forward",
    )(*args)


def scaled_rows(rows_grad, factor):
    return (rows_grad.astype(F32) * factor).astype(BF)


def misc_parts(grad_small):
    taps_low = grad_small[0:8, 0:CHANNELS].astype(BF)
    lane, rank = iota((128, 8), 0), iota((128, 8), 1)
    lines = jnp.zeros((384, 128), F32)
    for half in range(2):
        put = ((lane == 12 + 6 * half + rank) & (rank < 6)).astype(BF)
        lines = lines + dot_nt(select_lines(half), dot_nn(put, taps_low).astype(BF))
    put = ((lane == 25 + rank) & (rank < 5)).astype(BF)
    state_low = grad_small[0:8, CHANNELS : CHANNELS + 256].astype(BF)
    state_lines = dot_nn(put, state_low).astype(BF)
    put = ((lane == 30 + rank) & (rank < 3)).astype(BF)
    heads_low = grad_small[0:8, CHANNELS + 256 : CHANNELS + 384].astype(BF)
    head_lines = dot_nn(put, heads_low).astype(BF)
    row, head = iota((384, 128), 0), iota((384, 128), 1)
    head_rows = ((row - 96 * over_96(row) == head) & (head < HEADS)).astype(BF)
    return lines, state_lines, dot_nt(head_rows, head_lines)


def misc_tile(i, place, parts, grad_small):
    lines, state_lines, head_part = parts
    misc = head_part + dot_nt(select_state(384, i * 384), state_lines)
    misc = misc + jnp.where(place == i, lines, 0.0)
    gains = grad_small[8:9, i * 384 : (i + 1) * 384]
    return misc + jnp.transpose(jnp.where(iota((128, 384), 0) == 24, gains, 0.0))


def backward_kernel(last, *refs):
    refs = list(refs)

    def take(n):
        taken, refs[:n] = refs[:n], []
        return taken

    (where_ref,) = take(1)
    normed_in, read_in, y_in, starts_in, gated_gain_in = take(5)
    weights = (take(1), take(1)) if last else (take(5), take(5))
    taps_ref, taps_state_ref, heads_ref, gain_ref = take(4)
    if last:
        dscaled_in, cot = take(2)
        stat_parts = take(4)
    else:
        chunks = take(4)
    outs = take(4 if last else 1)
    (grad_small,) = take(1)
    mine_out, theirs_out = take(2)
    normed, read, y_all, starts, gated_gain, whole, dscaled = take(7)
    x_pad, state_pad, x_conv, state_conv, du_pad, dstate_pad = take(6)
    d_hidden, d_read, factors, sems = take(4)
    products, rows_grad, sent = take(3)
    grad_taps, grad_taps_state = grad_small.at[0:8, 0:CHANNELS], grad_small.at[0:8, 768:1024]
    grad_heads, grad_gain = grad_small.at[0:8, 1024:1152], grad_small.at[8:9, :]
    copies = Copies(sems)
    place, core = where_ref[0], where_ref[1]
    if not last:
        load_out = place_blocks(copies, where_ref, weights, whole, OUT)
    load_x = copies.start(read_in.at[:, X], read.at[:, X])
    load_ss = copies.start(read_in.at[:, SS], read.at[:, SS])
    if last:
        load_cot = [copies.start(cot.at[k, 1], sent.at[rows_at(k), :]) for k in range(BLOCKS)]
    du_pad[SEQ:, :] = jnp.zeros((PAD, CHANNELS), F32)
    dstate_pad[SEQ:, :] = jnp.zeros((PAD, 2 * STATES), F32)
    for ref in (d_hidden, grad_small):
        ref[...] = jnp.zeros_like(ref)
    if last:
        total = stat_parts[0][...] + stat_parts[1][...] + stat_parts[2][...] + stat_parts[3][...]
        factor = lax.rsqrt(total[0:1, :] / DI + EPS)
        cubed = factor * factor * factor / DI * total[1:2, :]
        row = iota((128, SEQ), 0)
        both = jnp.where(row == 0, factor, jnp.where(row == 1, cubed, 0.0))
        for b in range(BLOCKS):
            part = slice(b * BLOCK, (b + 1) * BLOCK)
            factors[part, :] = jnp.transpose(both[:, part])
        for k in range(BLOCKS):
            rows = slice(k * BLOCK, (k + 1) * BLOCK)
            load_cot[k].wait()
            rows_grad[rows, :] = scaled_rows(sent[rows, :], factors[rows, 0:1])
    else:
        for offset, chunk in zip((0, 3, 1, 2), chunks):
            rows = rows_at(lax.rem(place + offset, 4))
            rows_grad[rows, :] = chunk[:, :D]
            tail = chunk[:, D:].astype(F32)
            factor = tail[:, 0:1] + tail[:, 1:2]
            cross = tail[:, 2:3] + tail[:, 3:4]
            lane = iota((BLOCK, 128), 1)
            cubed = factor * factor * factor / DI * cross
            factors[rows, :] = jnp.where(lane == 0, factor, jnp.where(lane == 1, cubed, 0.0))
        for load in load_out:
            load.wait()
        dscaled[...] = dot_nn(rows_grad[...], whole[:, OUT])
        rows_grad[...] = scaled_rows(rows_grad[...], factors[:, 0:1])
    load_x.wait()
    load_rows = [
        copies.start(read_in.at[:, Z], read.at[:, Z]),
        copies.start(y_in, y_all),
        copies.start(starts_in, starts),
    ]
    if last:
        load_rows.append(copies.start(dscaled_in, dscaled))
    x_pad[:PAD, :] = jnp.zeros((PAD, CHANNELS), F32)
    x_pad[PAD:, :] = read[:, X]
    load_ss.wait()
    state_pad[:PAD, :] = jnp.zeros((PAD, 2 * STATES), F32)
    state_pad[PAD:, :] = read[:, STATE]
    conv_rows(x_pad, taps_ref, x_conv)
    conv_rows(state_pad, taps_state_ref, state_conv)
    for load in load_rows:
        load.wait()
    load_late = [
        copies.start(normed_in, normed),
        copies.start(gated_gain_in, gated_gain),
    ]
    for cols in (BOTH,) if last else (LEFT, BETWEEN):
        load_late += place_blocks(copies, where_ref, weights, whole, cols)

    def block(turn, carry):
        b = BLOCKS - 1 - turn
        rows = rows_at(b)
        state_u = state_conv[rows, :]
        state_s = sigmoid(state_u)
        state = state_u * state_s
        keys, reads = state[:, :STATES].astype(BF), state[:, STATES:].astype(BF)
        reads_t = jnp.transpose(state[:, STATES:]).astype(BF)
        raised, step, log_decay, summed, summed_t = step_terms(read[rows, MISC], heads_ref)
        meets_t = dot_nt(keys, reads)
        causal_t = iota((BLOCK, BLOCK), 1) >= iota((BLOCK, BLOCK), 0)
        fac = factors[rows, :][:, 0:1]
        cub = factors[rows, :][:, 1:2]
        d_meets_t = jnp.zeros((BLOCK, BLOCK), F32)
        d_keys = jnp.zeros((BLOCK, STATES), F32)
        d_reads = jnp.zeros((BLOCK, STATES), F32)
        head_sums = jnp.zeros((2 * BLOCK, 128), F32)
        last_row = iota((BLOCK, 128), 0) == BLOCK - 1
        for p in range(PAIRS):
            cols = slice(p * 128, (p + 1) * 128)
            u = x_conv[rows, cols]
            us = sigmoid(u)
            x = u * us
            step_wide = spread(step, 2 * p)
            summed_wide = spread(summed, 2 * p)
            grown = jnp.exp(summed_wide)
            end = grown[BLOCK - 1 : BLOCK, :]
            to_end = jnp.exp(summed_wide[BLOCK - 1 : BLOCK, :] - summed_wide)
            skip = taps_ref[6:7, cols]
            gain = taps_ref[5:6, cols]
            z = read[rows, Z.start + p * 128 : Z.start + (p + 1) * 128]
            zs = sigmoid(z)
            z_act = z * zs
            y = y_all[rows, cols]
            gated = y * z_act
            incoming = dscaled[rows, cols]
            lifted = gated * fac
            grad_taps[5:6, cols] += jnp.sum(incoming * lifted, axis=0, keepdims=True)
            d_gated = fac * (gain * incoming) - gated * cub
            dy = d_gated * z_act
            d_read[rows, Z.start + p * 128 : Z.start + (p + 1) * 128] = (d_gated * y * (zs + z_act * (1.0 - zs))).astype(BF)
            dy_low = dy.astype(BF)
            weighted = x * step_wide
            weighted_low = weighted.astype(BF)
            dy_grown = (dy * grown).astype(BF)
            held_low = starts[b, :, cols]
            dh = d_hidden[:, cols]
            dh_low = dh.astype(BF)
            d_reads = d_reads + dot_nt(dy_grown, held_low)
            kept = dot_nn(keys, dh_low) * to_end
            d_keys = d_keys + dot_nt((to_end * weighted).astype(BF), dh_low)
            decays = []
            for h in (2 * p, 2 * p + 1):
                gaps = summed_t[h : h + 1, :] - summed[:, h : h + 1]
                decays.append(jnp.exp(jnp.where(causal_t, gaps, NEG)))
            mixes = jnp.concatenate([(d * meets_t).astype(BF) for d in decays], axis=1)
            d_weighted = dot_nn(mixes, side_by_side(dy).astype(BF)) + kept
            d_mixes = dot_nt(side_by_side(weighted).astype(BF), dy_low)
            d_meets_t = d_meets_t + d_mixes[:BLOCK] * decays[0] + d_mixes[BLOCK:] * decays[1]
            dx = skip * dy + d_weighted * step_wide
            weighted_f = weighted_low.astype(F32)
            moved = dy_low.astype(F32) * (y - skip * x) - weighted_f * d_weighted
            extra = jnp.sum(weighted_f * kept, axis=0, keepdims=True) + end * jnp.sum(
                dh * held_low.astype(F32), axis=0, keepdims=True
            )
            moved = jnp.where(last_row, moved + extra, moved)
            upper, lower = two_parts(jnp.concatenate([moved, x * d_weighted], axis=0))
            picks = (
                iota((256, 128), 1) == 2 * p + (iota((256, 128), 0) % 128) // HEAD_DIM
            ).astype(BF)
            head_sums = head_sums + dot_nn(jnp.concatenate([upper, lower], axis=1), picks)
            grad_taps[6:7, cols] += jnp.sum(dy * x, axis=0, keepdims=True)
            du_pad[rows, cols] = dx * (us + x * (1.0 - us))
            d_hidden[:, cols] = end * dh + dot_nn(reads_t, dy_grown)
        d_reads = d_reads + dot_nn(jnp.transpose(d_meets_t).astype(BF), keys)
        d_keys = d_keys + dot_nn(d_meets_t.astype(BF), reads)
        d_state = jnp.concatenate([d_keys, d_reads], axis=1)
        d_state = d_state * (state_s + state * (1.0 - state_s))
        dstate_pad[rows, :] = d_state
        upper_tri = (iota((BLOCK, BLOCK), 1) >= iota((BLOCK, BLOCK), 0)).astype(F32)
        d_decay = dot_high(upper_tri, head_sums[:BLOCK])
        d_step = head_sums[BLOCK:] - d_decay * jnp.exp(heads_ref[1:2, :])
        d_raw = d_step * sigmoid(raised)
        d_read[rows, MISC] = d_raw.astype(BF)
        grad_heads[0:1, :] += jnp.sum(d_raw, axis=0, keepdims=True)
        grad_heads[1:2, :] += jnp.sum(d_decay * log_decay, axis=0, keepdims=True)
        return carry

    lax.fori_loop(0, BLOCKS, block, 0)

    def store_inner(start, cols, value):
        cols = slice(X.start + cols.start, X.start + cols.stop)
        d_read[start : start + BLOCK, cols] = value

    def store_state(start, cols, value):
        d_read[start : start + BLOCK, cols] = value

    conv_back(du_pad, x_pad, taps_ref, grad_taps, store_inner)
    conv_back(dstate_pad, state_pad, taps_state_ref, grad_taps_state, store_state)
    picks = (iota((CHANNELS, 128), 1) == iota((CHANNELS, 128), 0) // HEAD_DIM).astype(F32)
    grad_heads[2:3, :] = dot_high(grad_taps[...], picks)[6:7, :]
    for load in load_late:
        load.wait()
    for at in range(0, D, PART):
        cols = slice(at, at + PART)
        part = dot_nt(d_read[...], whole[cols, BOTH])
        total = jnp.sum(part * normed[:, cols].astype(F32), axis=0, keepdims=True)
        grad_gain[:, cols] = total / gain_ref[:, cols]
        sent[:, cols] = part.astype(BF)
    if last:
        for o, out in enumerate(outs):
            copies.store(sent.at[rows_at(lax.rem(place + o, 4)), :], out)
    else:
        copies.store(sent, outs[0])
    parts = misc_parts(grad_small)
    for i in range(4):
        lanes = slice(i * 384, (i + 1) * 384)
        shared = dot_tn(normed[:, lanes], d_read[...])
        for cols, value in (
            (STATE, shared[:, STATE]),
            (MISC, shared[:, MISC] + misc_tile(i, place, parts, grad_small)),
            (IN, shared[:, IN]),
            (OUT, dot_tn(rows_grad[:, lanes], gated_gain[...])),
        ):
            low = value.astype(BF)
            for k in range(8):
                at = (4 * i + k // 2) * 48
                products[k % 2, at : at + 48, cols] = low[k * 48 : (k + 1) * 48]
        rows = slice(i * 192, (i + 1) * 192)
        copies.store(products.at[1 - core, rows, :], theirs_out.at[rows, :])
        copies.store(products.at[core, rows, :], mine_out.at[rows, :])
    copies.finish()


def backward_call(where, kept, weights, taps, taps_state, heads, gain, last, extra):
    args = [where, *kept, *weights, taps, taps_state, heads, gain, *extra]
    in_specs = [SMEM] + [HBM] * 5 + [ANY] * len(weights) + [VMEM] * 4
    in_specs += [HBM, ANY] + [VMEM] * 4 if last else [VMEM] * 4
    out_shape = [
        *([pltpu.HBM((BLOCK, D), BF)] * 4 if last else [pltpu.HBM((SEQ, D), BF)]),
        shape(16, D),
        *[pltpu.HBM((SIDE, WIDE), BF)] * 2,
    ]
    out_specs = [HBM] * (len(out_shape) - 3) + [VMEM] + [HBM] * 2
    scratch = [pltpu.VMEM(k.shape, k.dtype) for k in kept] + [pltpu.VMEM((D, WIDE), BF)]
    scratch += [
        pltpu.VMEM((SEQ, CHANNELS), F32),
        pltpu.VMEM((PAD + SEQ, CHANNELS), F32),
        pltpu.VMEM((PAD + SEQ, 2 * STATES), F32),
        pltpu.VMEM((SEQ, CHANNELS), F32),
        pltpu.VMEM((SEQ, 2 * STATES), F32),
        pltpu.VMEM((PAD + SEQ, CHANNELS), F32),
        pltpu.VMEM((PAD + SEQ, 2 * STATES), F32),
        pltpu.VMEM((STATES, CHANNELS), F32),
        pltpu.VMEM((SEQ, READ), BF),
        pltpu.VMEM((SEQ, 128), F32),
        pltpu.SemaphoreType.DMA((128,)),
        pltpu.VMEM((2, SIDE, WIDE), BF),
        pltpu.VMEM((SEQ, D), BF),
        pltpu.VMEM((SEQ, D), BF),
    ]

    def kernel(*refs):
        backward_kernel(last, *refs)

    return pl.pallas_call(
        kernel,
        out_shape=out_shape,
        in_specs=in_specs,
        out_specs=out_specs,
        scratch_shapes=scratch,
        compiler_params=limit(VMEM_LIMIT),
        cost_estimate=cost(32 * 10**9, 30 * 10**6),
        name="layer_backward",
    )(*args)


def arrived(parts):
    return sum((part[...].astype(F32) for part in parts[1:]), parts[0][...].astype(F32))


def after_first_kernel(rows_ref, a, b, c, d, hidden, mixed, factor_out):
    total = arrived((a, b, c, d))
    mixed[...] = total[:, :D]
    square = total[:, D : D + 1] + total[:, D + 1 : D + 2]
    factor = lax.rsqrt(square / DI + EPS)
    factor_out[...] = jnp.broadcast_to(factor, (BLOCK, 128))
    hidden[...] = (rows_ref[...].astype(F32) + factor * total[:, :D]).astype(BF)


def after_first_call(rows, parts):
    return pl.pallas_call(
        after_first_kernel,
        out_shape=[shape(BLOCK, D, dtype=BF), shape(BLOCK, D), shape(BLOCK, 128)],
        in_specs=[VMEM] * 5,
        out_specs=[VMEM] * 3,
        name="between_layers",
    )(rows, *parts)


def after_last_kernel(where_ref, rows_ref, mixed, a, b, c, d, result):
    total = a[...] + b[...] + c[...] + d[...]
    factor = lax.rsqrt(total[0:1, :] / DI + EPS)
    row = iota((128, SEQ), 0)
    column = jnp.zeros((BLOCK, 128), F32)
    for k in range(4):
        part = slice(k * BLOCK, (k + 1) * BLOCK)
        turned = jnp.transpose(jnp.where(row[:, part] == 0, factor[:, part], 0.0))
        column = jnp.where(where_ref[0] == k, turned, column)
    result[...] = rows_ref[...].astype(F32) + column[:, 0:1] * mixed[...].astype(F32)


def after_last_call(where, rows, mixed, stat_parts):
    return pl.pallas_call(
        after_last_kernel,
        out_shape=shape(BLOCK, D),
        in_specs=[SMEM] + [VMEM] * 6,
        out_specs=VMEM,
        name="last_rows",
    )(where, rows, mixed, *stat_parts)


def rows_back(rows_ref, parts, gain_ref, grad_ref):
    incoming = arrived(parts)
    v = rows_ref[...].astype(F32)
    q = lax.rsqrt(jnp.mean(v * v, axis=1, keepdims=True) + EPS)
    weighted = incoming * gain_ref[...]
    inner = jnp.sum(weighted * v, axis=1, keepdims=True)
    return grad_ref[...].astype(F32) + q * weighted - v * (q * q * q / D * inner)


def back_last_kernel(rows_ref, a, b, c, d, gain_ref, grad_ref, mixed_ref, factor_ref, out):
    low = rows_back(rows_ref, (a, b, c, d), gain_ref, grad_ref).astype(BF)
    out[:, :D] = low
    cross = jnp.sum(low.astype(F32) * mixed_ref[...], axis=1, keepdims=True)
    factor = factor_ref[:, 0:1]
    pieces = [*two_parts(factor), *two_parts(cross)]
    lane = iota((BLOCK, 128), 1)
    tail = jnp.zeros((BLOCK, 128), F32)
    for k, piece in enumerate(pieces):
        tail = jnp.where(lane == k, piece.astype(F32), tail)
    out[:, D:] = tail.astype(BF)


def back_last_call(rows, parts, gain, grad, mixed, factor):
    return pl.pallas_call(
        back_last_kernel,
        out_shape=shape(BLOCK, SENT, dtype=BF),
        in_specs=[VMEM] * 9,
        out_specs=VMEM,
        name="between_layers_back",
    )(rows, *parts, gain, grad, mixed, factor)


def back_first_kernel(rows_ref, incoming, gain_ref, grad_ref, out):
    out[...] = rows_back(rows_ref, (incoming,), gain_ref, grad_ref[:, :D])


def back_first_call(rows, incoming, gain, grad):
    return pl.pallas_call(
        back_first_kernel,
        out_shape=shape(BLOCK, D),
        in_specs=[VMEM] * 4,
        out_specs=VMEM,
        name="first_rows_back",
    )(rows, incoming, gain, grad)


def params_kernel(where_ref, misc, heads_ref, taps, taps_state, gain):
    small_params(where_ref[0], misc, heads_ref, taps, taps_state, gain)


def params_call(where, misc, heads):
    return pl.pallas_call(
        params_kernel,
        out_shape=SMALL,
        in_specs=[SMEM, VMEM, VMEM],
        out_specs=[VMEM] * 3,
        compiler_params=limit(16),
        name="small_parameters",
    )(where, misc, heads)


def both_kernel(where_ref, mine_in, given, *refs):
    outs, mine, sem = refs[:-2], refs[-2], refs[-1]
    load = pltpu.make_async_copy(mine_in, mine, sem)
    load.start()
    load.wait()
    if len(outs) == 1:
        outs[0][...] = (mine[...].astype(F32) + given[...].astype(F32)).astype(BF)
        return
    core, row, col = where_ref[1], where_ref[2], where_ref[3]
    own, ahead, far_left, far_right, behind, parts = outs
    for i in range(4):
        for j in range(4):
            rows = slice((4 * i + j) * 48, (4 * i + j + 1) * 48)
            total = (mine[rows, :].astype(F32) + given[rows, :].astype(F32)).astype(BF)
            along, across = lax.rem(i - row + 4, 4), lax.rem(j - col + 4, 4)
            o = along + core * (across - along)
            q = across + core * (along - across)
            parts[o, pl.ds(pl.multiple_of(q * 48, 16), 48), :] = total
    own[...] = parts[0]
    ahead[...] = parts[1]
    far_left[...] = parts[2, :, LEFT]
    far_right[...] = parts[2, :, RIGHT]
    behind[...] = parts[3]


def ring_shapes(rows):
    whole = shape(rows, WIDE, dtype=BF)
    left, right = shape(rows, SPLIT, dtype=BF), shape(rows, WIDE - SPLIT, dtype=BF)
    return [whole, whole, left, right, whole]


def both_call(where, mine, given, relative):
    out_shape = ring_shapes(192) if relative else [shape(SIDE, WIDE, dtype=BF)]
    return pl.pallas_call(
        both_kernel,
        out_shape=out_shape,
        in_specs=[SMEM, HBM, VMEM],
        out_specs=[VMEM] * len(out_shape),
        scratch_shapes=([pltpu.VMEM((4, 192, WIDE), BF)] if relative else [])
        + [pltpu.VMEM((SIDE, WIDE), BF), pltpu.SemaphoreType.DMA],
        compiler_params=limit(28),
        cost_estimate=cost(10**6, 10**4),
        name="both_cores_grads",
    )(where, mine, given)


def passed_kernel(ahead, behind, left, right, out_ahead, out_behind):
    out_ahead[:, LEFT] = (ahead[:, LEFT].astype(F32) + left[...].astype(F32)).astype(BF)
    out_ahead[:, RIGHT] = ahead[:, RIGHT]
    out_behind[:, LEFT] = behind[:, LEFT]
    out_behind[:, RIGHT] = (behind[:, RIGHT].astype(F32) + right[...].astype(F32)).astype(BF)


def passed_call(ahead, behind, left, right):
    return pl.pallas_call(
        passed_kernel,
        out_shape=[shape(*ahead.shape, dtype=BF)] * 2,
        in_specs=[VMEM] * 4,
        out_specs=[VMEM] * 2,
        compiler_params=limit(16),
        cost_estimate=cost(10**6, 10**4),
        name="grads_passed_on",
    )(ahead, behind, left, right)


def halfway_kernel(a, b, c, own, ahead, far_left, far_right, behind):
    total = arrived((a, b, c)).astype(BF)
    own[...] = total[:48]
    ahead[...] = total[48:96]
    far_left[...] = total[96:144, LEFT]
    far_right[...] = total[96:144, RIGHT]
    behind[...] = total[144:]


def halfway_call(parts):
    return pl.pallas_call(
        halfway_kernel,
        out_shape=ring_shapes(48),
        in_specs=[VMEM] * 3,
        out_specs=[VMEM] * 5,
        compiler_params=limit(20),
        name="grads_halfway",
    )(*parts)


def shard_kernel(where_ref, a, b, c, share_1, own, given):
    share_0 = arrived((a, b, c))
    is_first = where_ref[1] == 0
    other = share_1[...].astype(F32)
    own[...] = jnp.where(is_first, share_0, other)
    given[...] = jnp.where(is_first, other, share_0).astype(BF)


def shard_call(where, parts, share_1):
    return pl.pallas_call(
        shard_kernel,
        out_shape=[shape(48, WIDE), shape(48, WIDE, dtype=BF)],
        in_specs=[SMEM] + [VMEM] * 4,
        out_specs=[VMEM] * 2,
        name="grads_shard",
    )(where, *parts, share_1)


def swap(v):
    return lax.ppermute(v, "section", [(0, 1), (1, 0)])


def turn(v, by, axis="tensor"):
    return lax.ppermute(v, axis, [(i, (i + by) % 4) for i in range(4)])


def spread_rows(v):
    return (v, turn(v, 1), turn(v, -1), turn(v, 2))


def meet(parts, axis="tensor"):
    own, ahead, across, behind = parts
    return (own, turn(ahead, 1, axis), turn(behind, -1, axis), turn(across, 2, axis))


def from_ring(v, axis):
    return (v, turn(v, -1, axis), turn(v, 2, axis), turn(v, 1, axis))


def ring(v, by, phase):
    pairs = []
    for s in range(2):
        for a in range(4):
            for b in range(4):
                to = ((a + by) % 4, b) if s == phase else (a, (b + by) % 4)
                pairs.append((16 * s + 4 * a + b, 16 * s + 4 * to[0] + to[1]))
    return lax.ppermute(v, ("section", *DP), pairs)


def around(v, phase):
    ahead, behind = lax.optimization_barrier((ring(v, -1, phase), ring(v, 1, phase)))
    return (
        v,
        ahead,
        ring(ahead[:, :SPLIT], -1, phase),
        ring(behind[:, SPLIT:], 1, phase),
        behind,
    )


def gather_by_turns(main, rest):
    own, ahead, far_left, far_right, behind = around(main, 0)
    far = jnp.concatenate([far_left, far_right], axis=1)
    rest = (rest, ring(rest, -1, 0), ring(rest, 2, 0), ring(rest, 1, 0))
    rows = [
        jnp.concatenate(pair, axis=1) for pair in zip(rest, (own, ahead, far, behind))
    ]
    return around(jnp.concatenate(rows, axis=0), 1)


def pick(v, index, axis):
    return lax.dynamic_index_in_dim(v, index, axis, keepdims=False)


def tie(*values):
    return lax.optimization_barrier(values)


def shards(
    section_ends,
    norm_gain,
    proj_inner,
    proj_step,
    proj_state,
    conv_inner,
    conv_state,
    gate_gain,
    head_params,
    proj_output,
):
    core = lax.axis_index("section")
    place = lax.axis_index("tensor")
    is_first = core == 0
    where = jnp.stack(
        [place, core, lax.axis_index("dp_0"), lax.axis_index("dp_1")]
    ).astype(jnp.int32)

    def by_layer_of(keep, got):
        return jnp.where(is_first, keep, got), jnp.where(is_first, got, keep)

    def by_layer(halves):
        return by_layer_of(pick(halves, core, 0), swap(pick(halves, 1 - core, 0)))

    main = jnp.concatenate([proj_inner[0].reshape(96, 2 * CHANNELS), proj_output[0].T], axis=1)
    main_0, main_1 = by_layer(main.reshape(2, 48, MAIN))
    main_0, heads_got, *small = tie(
        main_0,
        swap(head_params[0]),
        proj_state[0],
        norm_gain[0],
        conv_inner[0],
        gate_gain[0],
        conv_state[0],
    )
    packed = jnp.concatenate(
        [
            *[v.reshape(-1) for v in small],
            jnp.zeros((32 * 256 - 6144 - 332,), BF),
        ]
    ).reshape(32, 256)
    turned = jnp.stack(from_ring(packed, "tensor") * 2)
    filled = lax.dynamic_slice_in_dim(turned, lax.rem(4 - place, 4), 4, 0).reshape(4, 32 * 256)
    state_rows = filled[:, :6144].reshape(96, 256)
    norm_col = filled[:, 6144:6168].reshape(96, 1)
    inner_cols = filled[:, 6168:6408].reshape(4, 5, 48).transpose(0, 2, 1).reshape(192, 5)
    gate_col = filled[:, 6408:6456].reshape(192, 1)
    both = jnp.concatenate([inner_cols, gate_col], axis=1)
    both = both.reshape(2, 96, 6).transpose(1, 0, 2).reshape(96, 12)
    state_cols = filled[:, 6456:6476].reshape(4, 5, 4).transpose(0, 2, 1).reshape(16, 5)
    state_cols = jnp.pad(state_cols, ((0, 80), (0, 0)))
    misc = jnp.concatenate(
        [proj_step[0], both, norm_col, state_cols, jnp.zeros((96, 128 - 30), BF)], axis=1
    )

    rest_0, rest_1 = by_layer(jnp.concatenate([state_rows, misc], axis=1).reshape(2, 48, 384))

    ends = section_ends[0]
    got_rows = swap(pick(ends, 1 - core, 0))
    rows_in = jnp.where(is_first, ends[0], got_rows)
    cot = jnp.where(is_first, got_rows, ends[1])
    heads = [
        jnp.pad(v.astype(F32), ((0, 5), (0, 128 - HEADS)))
        for v in by_layer_of(head_params[0], heads_got)
    ]
    ends_all = lax.all_gather(jnp.stack([rows_in, cot]), "tensor", axis=0)
    own_pieces = gather_by_turns(main_0, rest_0)
    shard_1 = jnp.concatenate([rest_1, main_1], axis=1)
    shard_1, *rest = tie(shard_1, *heads, *own_pieces)
    heads, own_pieces = rest[:2], rest[2:]
    full_1 = lax.all_gather(shard_1, DP, axis=0, tiled=True)
    pieces_0 = (*own_pieces, *[swap(v) for v in own_pieces])
    first = forward_call(where, ends_all, (), (*pieces_0, heads[0]))
    kept_0, sent_0, small_0 = first[:5], first[5:9], first[9:]
    weights_0 = (pieces_0, small_0[0], small_0[1], heads[0], small_0[2])
    own_1, *met_0 = tie(full_1, *meet(sent_0))
    other_1 = swap(own_1)
    order = (own_1[:, MISC].reshape(16, 48, 128), other_1[:, MISC].reshape(16, 48, 128))
    misc_1 = jnp.where(is_first, jnp.stack(order, axis=1), jnp.stack(order[::-1], axis=1))
    small_1 = params_call(where, misc_1.reshape(D, 128), heads[1])
    weights_1 = ((own_1, other_1), small_1[0], small_1[1], heads[1], small_1[2])
    hidden, mixed_0, factor_0 = after_first_call(rows_in, met_0)
    kept_1 = forward_call(
        where, ends_all, spread_rows(hidden), (own_1, other_1, *weights_1[1:])
    )
    dscaled_1, stats, mixed_1 = kept_1[5:]
    stat_parts = spread_rows(stats)
    met_1 = lax.psum_scatter(mixed_1, "tensor", scatter_dimension=0, tiled=True)
    back_1 = backward_call(
        where, kept_1[:5], *weights_1, True, (dscaled_1, ends_all, *stat_parts)
    )
    met_1, *back_1 = tie(met_1, *back_1)
    payload_1 = both_call(where, back_1[5], swap(back_1[6]), False)[0]
    payload_1, *d_met_1 = tie(payload_1, *meet(back_1[:4]))
    grad_1 = back_last_call(hidden, d_met_1, weights_1[4], cot, mixed_0, factor_0)
    payload_1, met_1, grad_1 = tie(payload_1, met_1, grad_1)
    share_1 = lax.psum_scatter(payload_1, DP, scatter_dimension=0, tiled=True)
    result = after_last_call(where, hidden, met_1, stat_parts)
    result, *chunks_0 = tie(result, *spread_rows(grad_1))
    back_0 = backward_call(where, kept_0, *weights_0, False, chunks_0)
    parts_0 = both_call(where, back_0[2], swap(back_0[3]), True)
    own, ahead, far_left, far_right, behind = parts_0
    ahead, behind = passed_call(
        ahead, behind, ring(far_left, 1, 0), ring(far_right, -1, 0)
    )
    share_1, rows_0, ahead, behind = tie(share_1, back_0[0], ahead, behind)
    ahead, behind = tie(ring(ahead, 1, 0), ring(behind, -1, 0))
    pieces = halfway_call((own, ahead, behind))
    met_0 = lax.psum_scatter(rows_0, "tensor", scatter_dimension=0, tiled=True)
    own, ahead, far_left, far_right, behind = pieces
    ahead, behind = passed_call(
        ahead, behind, ring(far_left, 1, 1), ring(far_right, -1, 1)
    )
    met_0, ahead, behind = tie(met_0, ahead, behind)
    half_met = (own, ring(ahead, 1, 1), ring(behind, -1, 1))
    grad_0 = back_first_call(rows_in, met_0, weights_0[4], grad_1)
    rows_got = swap(jnp.where(is_first, result, grad_0))
    section_rows = jnp.where(
        is_first, jnp.stack([grad_0, rows_got]), jnp.stack([rows_got, result])
    )
    share_own, share_given = shard_call(where, half_met, share_1)
    share_got = swap(share_given).astype(F32)
    whole = jnp.where(
        is_first,
        jnp.concatenate([share_own, share_got], axis=0),
        jnp.concatenate([share_got, share_own], axis=0),
    )
    grad_inner = whole[:, IN].reshape(96, 2, CHANNELS)
    grad_output = whole[:, OUT].T
    misc = whole[:, MISC]
    grad_step = misc[:, :HEADS]
    grad_heads = misc[:HEADS, 30:33].T
    to_send = jnp.concatenate(
        [
            whole[:, STATE].reshape(4, 6144),
            misc[:, 24].reshape(4, 24),
            misc[:, 12:24].reshape(96, 2, 6).transpose(1, 0, 2).reshape(4, 48 * 6),
            misc[:16, 25:30].reshape(4, 20),
            jnp.zeros((4, 32 * 256 - 6144 - 332), F32),
        ],
        axis=1,
    ).reshape(4, 32, 256)
    pieces = [pick(to_send, lax.rem(place + o, 4), 0) for o in range(4)]
    section_rows, *met = tie(section_rows, *meet(pieces))
    total = (met[0] + met[1] + met[2] + met[3]).reshape(-1)
    grad_state = total[:6144].reshape(24, 256)
    grad_norm = total[6144:6168]
    inner_lines = total[6168:6456].reshape(48, 6).T
    grad_conv_inner = inner_lines[:5]
    grad_gate = inner_lines[5]
    grad_conv_state = total[6456:6476].reshape(4, 5).T
    return (
        section_rows[None],
        grad_norm[None],
        grad_inner[None],
        grad_step[None],
        grad_state[None],
        grad_conv_inner[None],
        grad_conv_state[None],
        grad_gate[None],
        grad_heads[None],
        grad_output[None],
    )


def solution(mesh):
    split = Mesh(
        mesh.devices.reshape(mesh.shape["section"], 4, 4, mesh.shape["tensor"]),
        ("section", "dp_0", "dp_1", "tensor"),
    )
    return jax.shard_map(
        shards,
        mesh=split,
        in_specs=(
            P("section", None, DP_TENSOR, None),
            P("section", DP_TENSOR),
            P("section", DP, None, "tensor"),
            P("section", DP, "tensor"),
            P("section", DP_TENSOR, None),
            P("section", None, DP_TENSOR),
            P("section", None, DP_TENSOR),
            P("section", DP_TENSOR),
            P("section", None, "tensor"),
            P("section", "tensor", DP),
        ),
        out_specs=(
            P("section", None, DP_TENSOR, None),
            P("section", DP_TENSOR),
            P("section", DP, None, "tensor"),
            P("section", DP, "tensor"),
            P("section", DP_TENSOR, None),
            P("section", None, DP_TENSOR),
            P("section", None, DP_TENSOR),
            P("section", DP_TENSOR),
            P("section", None, "tensor"),
            P("section", "tensor", DP),
        ),
        check_vma=False,
    )
```
